128 devices in a mesh: dp: 8 (over x, z_lo), tp: 16 (over z_hi, y, core).
Axes of the slice: x: 4, y: 4, z: 4 (z_hi: 2, z_lo: 2; z = z_hi * 2 + z_lo), core: 2. Of those that a mesh axis runs over, the one named last changes fastest.
Arguments:
- cache: bfloat16 [512, 256, 576], P(('dp', 'tp')), may hold values from -3 to 3, as said below
- cache_length: int32 [512], P(('dp', 'tp')), may hold values from 64 to 254, as said below
- move_slot: int32 [8, 16], P('dp'), may hold values from 0 to 3
- move_peer: int32 [8, 16], P('dp'), may hold values from 0 to 15, as said below
- queries: bfloat16 [2, 512, 128, 576], P(None, ('dp', 'tp')), may hold values from -16 to 16
- new_latent: bfloat16 [2, 512, 576], P(None, ('dp', 'tp')), may hold values from -3 to 3
- value_up: bfloat16 [128, 512, 128], P('tp'), may hold values from -0.25 to 0.25
- out_proj: bfloat16 [16384, 7168], P('tp', 'dp'), may hold values from -0.046875 to 0.046875
- residual: bfloat16 [2, 512, 7168], P(None, None, 'dp'), may hold values from -1.5 to 1.5
- norm_gain: bfloat16 [7168], P('dp'), may hold values from 0.5 to 1.5
- gate_weight: bfloat16 [7168, 18432], P('dp', 'tp'), may hold values from -0.0625 to 0.0625
- up_weight: bfloat16 [7168, 18432], P('dp', 'tp'), may hold values from -0.0625 to 0.0625
- down_weight: bfloat16 [18432, 7168], P('tp', 'dp'), may hold values from -0.046875 to 0.046875
Outputs:
- layer_out: bfloat16 [2, 512, 7168], P(None, 'tp', 'dp')
The draws below stay inside these ranges and needn't reach their ends.
Inputs may be any that keep to these rules, and one draw needn't show every extreme that they name: Row g of cache holds the request of slot g before migration; its positions from cache_length onward (in the slot after migration) are never read. `cache_length`: at least two positions of every request stay free for the new tokens; some request is that long in every draw. `move_peer`: each row is a permutation of the tp indices 0 .. 15; a device whose entry is its own index keeps its requests.
All inputs are finite; a program needn't handle non-finite values.
Results may differ from the reference program's by a relative error of at most 0.01.
Values may be sent and summed in bfloat16 or wider, within the bound.
No kernel may reach another device: no remote copies, remote signals or barrier semaphores. Data moves between devices by JAX's collectives and lax.ppermute only.
A program may use at most 128 MiB of HBM per device.

```python
import jax
import jax.numpy as jnp
from jax import lax

D = 7168
FF = 18432
H = 128
LAT = 512
VH = 128
QKD = 192
R_DEV = 4
LMAX = 256
STEPS = 2
KVW = 576
REQUESTS = 512
N_DP = 8
N_TP = 16


def latent_base(key):
    return jnp.clip(jax.random.normal(key, (REQUESTS, LMAX, KVW), jnp.float32), -3.0, 3.0)


def draw_cache(key, part):
    base_latent = latent_base(key)
    return base_latent.astype(jnp.bfloat16)


def draw_queries(key, part):
    key = jax.random.fold_in(key, 5)
    result = jnp.clip(jax.random.normal(key, (STEPS, REQUESTS, H, KVW), jnp.float32), -4.0, 4.0)
    return result.astype(jnp.bfloat16)


def draw_cache_length(key, part):
    key = jax.random.fold_in(key, 7)
    lengths = jax.random.randint(key, (REQUESTS,), LMAX // 4, LMAX - 1)
    return lengths.at[0].set(LMAX - 2).astype(jnp.int32)


def draw_move_peer(key, part):
    key = jax.random.fold_in(key, 9)
    movers = max(2, 2 * N_TP // 5)

    def one_group(subkey):
        shuffled = jax.random.permutation(subkey, N_TP)
        chosen = shuffled[:movers]
        return jnp.arange(N_TP).at[chosen].set(jnp.roll(chosen, -1))
    return jax.vmap(one_group)(jax.random.split(key, N_DP)).astype(jnp.int32)


def touch_ends(array, rng, low, high):
    longest = array.shape.index(max(array.shape))
    spots = []
    for shift in (0, 1):
        where = [jax.random.randint(jax.random.fold_in(rng, axis), (), 0, length) for axis, length in enumerate(array.shape)]
        where[longest] = (where[longest] + shift) % array.shape[longest]
        spots.append(tuple(where))
    return array.at[spots[0]].set(low).at[spots[1]].set(high)


def levels(key, extent, pieces, low, top_value):
    def one(dim, shards_of):
        draws = jax.random.uniform(jax.random.fold_in(jax.random.fold_in(key, 6), dim), (shards_of,), jnp.float32, low / len(pieces), top_value / len(pieces))
        return jnp.repeat(jnp.exp(draws), extent[dim] // shards_of).reshape((-1,) + (1,) * (len(extent) - dim - 1))

    level = one(*pieces[0])
    for cut in pieces[1:]:
        level = level * one(*cut)
    return level


def noise(own_key, shape, scale, limit, cuts=(), kind=jnp.bfloat16):
    level = levels(own_key, shape, cuts, -0.22, 0.18) if cuts else 1.0
    entries = jax.random.normal(own_key, shape, jnp.float32) * scale * level
    return jnp.minimum(jnp.maximum(entries, -limit), limit).astype(kind)


def setup_inputs(seed: int = 0) -> dict:
    keys = jax.random.split(jax.random.key(seed), 14)
    return {
        "cache": draw_cache(jax.random.fold_in(keys[13], 71), 0),
        "cache_length": draw_cache_length(jax.random.fold_in(keys[13], 71), 0),
        "move_slot": touch_ends(jax.random.randint(keys[2], (N_DP, N_TP), 0, R_DEV), jax.random.fold_in(keys[2], 1), 0, R_DEV - 1).astype(jnp.int32),
        "move_peer": draw_move_peer(jax.random.fold_in(keys[13], 71), 0),
        "queries": draw_queries(jax.random.fold_in(keys[13], 71), 0),
        "new_latent": noise(keys[5], (STEPS, REQUESTS, KVW), 1.0, 3.0, ((1, 128),)),
        "value_up": noise(keys[6], (H, LAT, VH), LAT ** -0.5, 0.25, ((0, 16),)),
        "out_proj": noise(keys[7], (H * VH, D), (H * VH) ** -0.5, 0.046875, ((0, 16), (1, 8))),
        "residual": noise(keys[8], (STEPS, REQUESTS, D), 0.25, 1.5, ((2, 8),)),
        "norm_gain": jnp.clip(1.0 + 0.1 * jax.random.normal(keys[9], (D,), jnp.float32), 0.5, 1.5).astype(jnp.bfloat16),
        "gate_weight": noise(keys[10], (D, FF), D ** -0.5, 0.0625, ((0, 8), (1, 16))),
        "up_weight": noise(keys[11], (D, FF), D ** -0.5, 0.0625, ((0, 8), (1, 16))),
        "down_weight": noise(keys[12], (FF, D), FF ** -0.5, 0.046875, ((0, 16), (1, 8))),
    }


def reference(cache, cache_length, move_slot, move_peer, queries, new_latent, value_up, out_proj, residual, norm_gain, gate_weight, up_weight, down_weight):
    dp_grid = jnp.arange(N_DP, dtype=jnp.int32)[:, None]
    tp_grid = jnp.arange(N_TP, dtype=jnp.int32)[None, :]
    source = ((dp_grid * N_TP + tp_grid) * R_DEV + move_slot).reshape(-1).astype(jnp.int32)
    peer_slot = jnp.take_along_axis(move_slot, move_peer, axis=1)
    target = ((dp_grid * N_TP + move_peer) * R_DEV + peer_slot).reshape(-1).astype(jnp.int32)
    gather_order = jnp.arange(REQUESTS, dtype=jnp.int32).at[target].set(source)
    latents = jnp.take(cache, gather_order, axis=0)
    positions = jnp.arange(LMAX, dtype=jnp.int32)[None, :]
    score_scale = QKD ** (-0.5)
    results = []
    for decode_step in range(STEPS):
        current = cache_length[:, None] + decode_step
        latents = jnp.where((positions == current)[:, :, None], new_latent[decode_step][:, None, :], latents)
        latents_f = latents.astype(jnp.float32)
        scores = jnp.einsum('rhc,rlc->rhl', queries[decode_step].astype(jnp.float32), latents_f) * score_scale
        scores = jnp.where((positions <= current)[:, None, :], scores, -jnp.inf)
        largest = lax.optimization_barrier(jnp.max(scores, axis=-1, keepdims=True))
        expo = jnp.exp(scores - largest)
        denominator = lax.optimization_barrier(jnp.sum(expo, axis=-1, keepdims=True))
        attn_probs = (expo / denominator).astype(jnp.bfloat16)
        latent_out = jnp.einsum('rhl,rlc->rhc', attn_probs.astype(jnp.float32), latents_f[:, :, :LAT]).astype(jnp.bfloat16)
        value_heads = jnp.einsum('rhl,hlv->rhv', latent_out.astype(jnp.float32), value_up.astype(jnp.float32)).astype(jnp.bfloat16)
        attended = jnp.dot(value_heads.reshape(REQUESTS, H * VH), out_proj, preferred_element_type=jnp.float32)
        hidden = residual[decode_step].astype(jnp.float32) + attended
        squares = lax.optimization_barrier(jnp.sum(hidden * hidden, axis=1))
        normed = (hidden * norm_gain.astype(jnp.float32)).astype(jnp.bfloat16)
        inverse = lax.rsqrt(squares / D + 1e-06)[:, None]
        gate = jnp.dot(normed, gate_weight, preferred_element_type=jnp.float32) * inverse
        up = jnp.dot(normed, up_weight, preferred_element_type=jnp.float32) * inverse
        activated = (jax.nn.silu(gate) * up).astype(jnp.bfloat16)
        ffn_out = jnp.dot(activated, down_weight, preferred_element_type=jnp.float32)
        results.append((hidden + ffn_out).astype(jnp.bfloat16))
    return jnp.stack(results)
```

```python
import jax
import jax.numpy as jnp
from jax import lax
from jax.sharding import Mesh, PartitionSpec as P

D = 7168
QKD = 192
STEPS = 2
norm_eps = 1e-06

DP = ("x", "zl")
TP = ("zh", "y", "c")
ZY = ("zh", "y")
N_DP = 8
N_TP = 16
N_ZY = 8
SWAP = [(0, 1), (1, 0)]
bf16 = jnp.bfloat16
f32 = jnp.float32


def exchange(blocks, axes):
    return lax.all_to_all(blocks, axes, 0, 0, tiled=True)


def spread(block, axes, copies):
    return exchange(jnp.broadcast_to(block[None], (copies,) + block.shape), axes)


def migrate(cache, slot_row, peer_row, member, own_slot):
    lanes = jnp.arange(N_TP, dtype=jnp.int32)
    outgoing = lax.dynamic_slice_in_dim(cache, own_slot, 1, 0)[0]
    rows, width = outgoing.shape
    pieces = exchange(outgoing.reshape(N_TP, rows // N_TP, width), TP)
    route = (peer_row[None, :] == lanes[:, None]).astype(bf16)
    routed = jnp.einsum(
        "ji,ipc->jpc", route, pieces, preferred_element_type=f32
    ).astype(bf16)
    arrived = exchange(routed, TP).reshape(1, rows, width)
    return lax.dynamic_update_slice_in_dim(cache, arrived, own_slot, 0)


def attend(latents, cache_length, queries, new_latent, latent_width):
    positions = jnp.arange(latents.shape[1], dtype=jnp.int32)[None, :]
    for step in range(STEPS):
        latents = jnp.where(
            (positions == cache_length[:, None] + step)[:, :, None],
            new_latent[step][:, None, :],
            latents,
        )
    scores = jnp.einsum("srhc,rlc->rshl", queries, latents, preferred_element_type=f32)
    scores = scores * QKD ** (-0.5)
    limit = cache_length[:, None] + jnp.arange(STEPS, dtype=jnp.int32)[None, :]
    seen = positions[None] <= limit[:, :, None]
    scores = jnp.where(seen[:, :, None, :], scores, -jnp.inf)
    expo = jnp.exp(scores - jnp.max(scores, axis=-1, keepdims=True))
    probs = (expo / jnp.sum(expo, axis=-1, keepdims=True)).astype(bf16)
    out = jnp.einsum(
        "rshl,rlc->rshc", probs, latents[:, :, :latent_width], preferred_element_type=f32
    ).astype(bf16)
    return out


def local(
    cache,
    cache_length,
    move_slot,
    move_peer,
    queries,
    new_latent,
    value_up,
    out_proj,
    residual,
    norm_gain,
    gate_weight,
    up_weight,
    down_weight,
):
    member = lax.axis_index(TP)
    core = lax.axis_index("c")
    lanes = jnp.arange(N_TP, dtype=jnp.int32)
    own_slot = jnp.sum(jnp.where(lanes == member, move_slot[0], 0))
    latents = migrate(cache, move_slot[0], move_peer[0], member, own_slot)
    rows_dev = cache.shape[0]
    heads, latent_width, value_width = value_up.shape
    out = attend(latents, cache_length, queries, new_latent, latent_width)

    out = out.reshape(rows_dev, STEPS, N_TP, heads, latent_width)
    out = out.transpose(2, 0, 1, 3, 4)
    by_head = exchange(out, TP).reshape(-1, heads, latent_width)
    value_heads = jnp.einsum(
        "thl,hlv->thv", by_head, value_up, preferred_element_type=f32
    ).astype(bf16)
    value_heads = value_heads.reshape(value_heads.shape[0], heads * value_width)

    gathered = spread(value_heads, DP, N_DP)
    chunk = gathered.shape[1] // 2
    gathered = gathered.reshape(N_DP, 2, chunk, gathered.shape[2])
    first = core == 0
    own_rows = jnp.where(first, gathered[:, 0], gathered[:, 1]).reshape(N_DP * chunk, -1)
    other_rows = jnp.where(first, gathered[:, 1], gathered[:, 0]).reshape(N_DP * chunk, -1)

    def sum_tp(own, other, weight):
        away = jnp.dot(other, weight, preferred_element_type=f32).astype(bf16)
        near = lax.ppermute(away, "c", SWAP)
        total = jnp.dot(own, weight, preferred_element_type=f32) + near.astype(f32)
        parts = exchange(total.astype(bf16).reshape(N_ZY, chunk, -1), ZY)
        return jnp.sum(parts.astype(f32), axis=0)

    attended = sum_tp(own_rows, other_rows, out_proj)
    rows_out = residual.shape[1] // N_TP
    residue = lax.dynamic_slice_in_dim(residual, member * rows_out, rows_out, 1)
    residue = residue.transpose(1, 0, 2).reshape(chunk, -1)
    hidden = residue.astype(f32) + attended

    own_hidden = spread(hidden.astype(bf16), ZY, N_ZY).reshape(N_ZY * chunk, -1)
    other_hidden = lax.ppermute(own_hidden, "c", SWAP)

    def feed(part):
        wide = part.astype(f32)
        squares = jnp.sum(wide * wide, axis=1, keepdims=True)
        normed = (wide * norm_gain.astype(f32)).astype(bf16)
        gate = jnp.dot(normed, gate_weight, preferred_element_type=f32).astype(bf16)
        up = jnp.dot(normed, up_weight, preferred_element_type=f32).astype(bf16)
        high = squares.astype(bf16)
        low = (squares - high.astype(f32)).astype(bf16)
        lane = jnp.arange(128)[None, :]
        extra = jnp.where(lane == 0, high, jnp.where(lane == 1, low, jnp.zeros_like(low)))
        sent = jnp.concatenate([gate, up, extra], axis=1)
        units = gate.shape[1]
        parts = exchange(sent.reshape(N_DP, chunk, -1), DP)
        total = jnp.sum(parts.astype(f32), axis=0)
        square_sum = total[:, 2 * units] + total[:, 2 * units + 1]
        inverse = lax.rsqrt(square_sum / D + norm_eps)[:, None]
        active = jax.nn.silu(total[:, :units] * inverse) * (total[:, units : 2 * units] * inverse)
        return spread(active.astype(bf16), DP, N_DP).reshape(N_DP * chunk, units)

    own_active = feed(own_hidden)
    other_active = feed(other_hidden)
    ffn_out = sum_tp(own_active, other_active, down_weight)
    result = (hidden + ffn_out).astype(bf16)
    return result.reshape(rows_out, STEPS, -1).transpose(1, 0, 2)


def solution(mesh):
    split = Mesh(mesh.devices.reshape(4, 2, 2, 4, 2), ("x", "zl", "zh", "y", "c"))
    in_specs = (
        P(DP + TP, None, None),
        P(DP + TP),
        P(DP, None),
        P(DP, None),
        P(None, DP + TP, None, None),
        P(None, DP + TP, None),
        P(TP, None, None),
        P(TP, DP),
        P(None, None, DP),
        P(DP),
        P(DP, TP),
        P(DP, TP),
        P(TP, DP),
    )
    out_specs = P(None, TP, DP)
    return jax.shard_map(local, mesh=split, in_specs=in_specs, out_specs=out_specs, check_vma=False)
```

```python
import jax
import jax.numpy as jnp
from jax import lax
from jax.sharding import Mesh, PartitionSpec as P

D = 7168
QKD = 192
norm_eps = 1e-06

DP = ("x", "zl")
TP = ("zh", "y", "c")
ZY = ("zh", "y")
N_X = 4
N_DP = 8
N_TP = 16
N_ZY = 8
SWAP = [(0, 1), (1, 0)]
HALVES = ((0,), (1,))
bf16 = jnp.bfloat16
f32 = jnp.float32


def exchange(blocks, axes):
    return lax.all_to_all(blocks, axes, 0, 0, tiled=True)


def spread(block, axes, copies):
    return exchange(jnp.broadcast_to(block[None], (copies,) + block.shape), axes)


def shift_x(block, by):
    return lax.ppermute(block, "x", [(i, (i + by) % N_X) for i in range(N_X)])


def gather_dp(block, x, z):
    near = lax.ppermute(block, "zl", SWAP)
    first = z == 0
    both = jnp.stack([jnp.where(first, block, near), jnp.where(first, near, block)])
    whole = jnp.zeros((N_X,) + both.shape, both.dtype)
    whole = lax.dynamic_update_slice_in_dim(whole, both[None], x, 0)
    for by in (2, 1, 3):
        whole = lax.dynamic_update_slice_in_dim(
            whole, shift_x(both, by)[None], lax.rem(x + N_X - by, N_X), 0
        )
    return whole


def migrate(cache, slot_row, peer_row, member, own_slot):
    lanes = jnp.arange(N_TP, dtype=jnp.int32)
    outgoing = lax.dynamic_slice_in_dim(cache, own_slot, 1, 0)[0]
    rows, width = outgoing.shape
    pieces = exchange(outgoing.reshape(N_TP, rows // N_TP, width), TP)
    route = (peer_row[None, :] == lanes[:, None]).astype(bf16)
    routed = jnp.einsum(
        "ji,ipc->jpc", route, pieces, preferred_element_type=f32
    ).astype(bf16)
    arrived = exchange(routed, TP).reshape(1, rows, width)
    return lax.dynamic_update_slice_in_dim(cache, arrived, own_slot, 0)


def attend(latents, limit, queries, latent_width):
    positions = jnp.arange(latents.shape[1], dtype=jnp.int32)[None, None, :]
    scores = jnp.einsum("srhc,rlc->rshl", queries, latents, preferred_element_type=f32)
    scores = scores * QKD ** (-0.5)
    seen = positions <= limit[:, :, None]
    scores = jnp.where(seen[:, :, None, :], scores, -jnp.inf)
    expo = jnp.exp(scores - jnp.max(scores, axis=-1, keepdims=True))
    probs = (expo / jnp.sum(expo, axis=-1, keepdims=True)).astype(bf16)
    return jnp.einsum(
        "rshl,rlc->rshc", probs, latents[:, :, :latent_width], preferred_element_type=f32
    ).astype(bf16)


def local(
    cache,
    cache_length,
    move_slot,
    move_peer,
    queries,
    new_latent,
    value_up,
    out_proj,
    residual,
    norm_gain,
    gate_weight,
    up_weight,
    down_weight,
):
    member = lax.axis_index(TP)
    x = lax.axis_index("x")
    z = lax.axis_index("zl")
    core = lax.axis_index("c")
    own_first = core == 0
    lanes = jnp.arange(N_TP, dtype=jnp.int32)
    own_slot = jnp.sum(jnp.where(lanes == member, move_slot[0], 0))
    rows_dev = cache.shape[0]
    heads, latent_width, value_width = value_up.shape
    rows_out = residual.shape[1] // N_TP
    features, units = gate_weight.shape
    part = units // 2

    def columns(index):
        return jnp.concatenate(
            [
                lax.dynamic_slice_in_dim(gate_weight, index * part, part, 1),
                lax.dynamic_slice_in_dim(up_weight, index * part, part, 1),
            ],
            axis=1,
        )

    kept = columns(z)
    came = lax.ppermute(columns(1 - z), "zl", SWAP)
    in_weight = jnp.concatenate(
        [jnp.where(z == 0, kept, came), jnp.where(z == 0, came, kept)], axis=0
    )

    latents = migrate(cache, move_slot[0], move_peer[0], member, own_slot)
    positions = jnp.arange(latents.shape[1], dtype=jnp.int32)[None, :]
    for step in range(new_latent.shape[0]):
        latents = jnp.where(
            (positions == cache_length[:, None] + step)[:, :, None],
            new_latent[step][:, None, :],
            latents,
        )

    def sum_tp(own, other, weight):
        chunk = own.shape[0] // N_ZY
        away = jnp.dot(other, weight, preferred_element_type=f32).astype(bf16)
        near = lax.ppermute(away, "c", SWAP)
        total = jnp.dot(own, weight, preferred_element_type=f32) + near.astype(f32)
        parts = exchange(total.astype(bf16).reshape(N_ZY, chunk, -1), ZY)
        return jnp.sum(parts.astype(f32), axis=0)

    def attention(steps):
        count = len(steps)
        limit = cache_length[:, None] + jnp.array(steps, jnp.int32)[None, :]
        out = attend(latents, limit, queries[steps[0] : steps[-1] + 1], latent_width)
        out = out.reshape(rows_dev, count, N_TP, heads, latent_width)
        out = out.transpose(2, 0, 1, 3, 4).reshape(N_TP, rows_dev, count * heads, latent_width)
        by_head = exchange(out, TP).reshape(-1, heads, latent_width)
        value_heads = jnp.einsum(
            "thl,hlv->thv", by_head, value_up, preferred_element_type=f32
        ).astype(bf16)
        return value_heads.reshape(2, rows_out * count, heads * value_width)

    def project(value_heads, steps):
        gathered = gather_dp(value_heads, x, z)
        width = gathered.shape[-1]
        low, high = gathered[:, :, 0], gathered[:, :, 1]
        own = jnp.where(own_first, low, high).reshape(-1, width)
        other = jnp.where(own_first, high, low).reshape(-1, width)
        attended = sum_tp(own, other, out_proj)
        residue = lax.dynamic_slice_in_dim(
            residual[steps[0] : steps[-1] + 1], member * rows_out, rows_out, 1
        )
        residue = residue.transpose(1, 0, 2).reshape(attended.shape)
        return residue.astype(f32) + attended

    def feed(hidden):
        chunk = hidden.shape[0]
        squares = jnp.sum(hidden * hidden, axis=1)
        squares = jnp.sum(spread(squares.reshape(1, chunk), DP, N_DP), axis=(0, 1))
        inverse = lax.rsqrt(squares / D + norm_eps)[:, None]
        normed = (hidden * norm_gain.astype(f32) * inverse).astype(bf16)
        own = spread(normed, ("zl",) + ZY, 2 * N_ZY).reshape(2, N_X, -1, features)
        other = lax.ppermute(own, "c", SWAP)

        def partial(by):
            at = lax.rem(x + by, N_X)
            rows = jnp.concatenate(
                [lax.dynamic_index_in_dim(half, at, 1, False) for half in (own, other)], axis=1
            )
            rows = jnp.concatenate([rows[0], rows[1]], axis=1)
            return jnp.dot(rows, in_weight, preferred_element_type=f32)

        arrived = [shift_x(partial(by).astype(bf16), by) for by in (2, 1, 3)]
        total = partial(0)
        for block in arrived:
            total = total + block.astype(f32)
        return (jax.nn.silu(total[:, :part]) * total[:, part:]).astype(bf16)

    def lower(active, hidden, steps):
        gathered = gather_dp(active, x, z)
        rows = jnp.concatenate([gathered[:, 0], gathered[:, 1]], axis=-1)
        half = rows.shape[1] // 2
        own = rows[:, :half].reshape(-1, units)
        other = rows[:, half:].reshape(-1, units)
        result = (hidden + sum_tp(own, other, down_weight)).astype(bf16)
        return result.reshape(rows_out, len(steps), -1).transpose(1, 0, 2)

    value_heads = [attention(steps) for steps in HALVES]
    hidden = [project(v, steps) for v, steps in zip(value_heads, HALVES)]
    active = [feed(h) for h in hidden]
    results = [lower(a, h, steps) for a, h, steps in zip(active, hidden, HALVES)]
    return jnp.concatenate(results, axis=0)


def solution(mesh):
    split = Mesh(mesh.devices.reshape(4, 2, 2, 4, 2), ("x", "zl", "zh", "y", "c"))
    in_specs = (
        P(DP + TP, None, None),
        P(DP + TP),
        P(DP, None),
        P(DP, None),
        P(None, DP + TP, None, None),
        P(None, DP + TP, None),
        P(TP, None, None),
        P(TP, DP),
        P(None, None, DP),
        P(DP),
        P(DP, TP),
        P(DP, TP),
        P(TP, DP),
    )
    out_specs = P(None, TP, DP)
    return jax.shard_map(local, mesh=split, in_specs=in_specs, out_specs=out_specs, check_vma=False)
```

```python
import jax
import jax.numpy as jnp
from jax import lax
from jax.sharding import Mesh, PartitionSpec as P

D = 7168
QKD = 192
norm_eps = 1e-06

DP = ("x", "zl")
TP = ("zh", "y", "c")
ZY = ("zh", "y")
N_X = 4
N_DP = 8
N_TP = 16
N_ZY = 8
SWAP = [(0, 1), (1, 0)]
bf16 = jnp.bfloat16
f32 = jnp.float32


def exchange(blocks, axes):
    return lax.all_to_all(blocks, axes, 0, 0, tiled=True)


def spread(block, axes, copies):
    return exchange(jnp.broadcast_to(block[None], (copies,) + block.shape), axes)


def shift_x(block, by):
    return lax.ppermute(block, "x", [(i, (i + by) % N_X) for i in range(N_X)])


def gather_dp(block, x, z):
    near = lax.ppermute(block, "zl", SWAP)
    whole = jnp.zeros((N_X, 2) + block.shape, block.dtype)
    for shard, at_z in ((block, z), (near, 1 - z)):
        for by in (2, 1, 3, 0):
            came = shift_x(shard, by) if by else shard
            start = (lax.rem(x + N_X - by, N_X), at_z) + (0,) * block.ndim
            whole = lax.dynamic_update_slice(whole, came[None, None], start)
    return whole


def migrate(cache, slot_row, peer_row, member, own_slot):
    lanes = jnp.arange(N_TP, dtype=jnp.int32)
    outgoing = lax.dynamic_slice_in_dim(cache, own_slot, 1, 0)[0]
    rows, width = outgoing.shape
    pieces = exchange(outgoing.reshape(N_TP, rows // N_TP, width), TP)
    route = (peer_row[None, :] == lanes[:, None]).astype(bf16)
    routed = jnp.einsum(
        "ji,ipc->jpc", route, pieces, preferred_element_type=f32
    ).astype(bf16)
    arrived = exchange(routed, TP).reshape(1, rows, width)
    return lax.dynamic_update_slice_in_dim(cache, arrived, own_slot, 0)


def attend(latents, limit, queries, latent_width):
    positions = jnp.arange(latents.shape[1], dtype=jnp.int32)[None, None, :]
    scores = jnp.einsum("srhc,rlc->rshl", queries, latents, preferred_element_type=f32)
    scores = scores * QKD ** (-0.5)
    seen = positions <= limit[:, :, None]
    scores = jnp.where(seen[:, :, None, :], scores, -jnp.inf)
    expo = jnp.exp(scores - jnp.max(scores, axis=-1, keepdims=True))
    probs = (expo / jnp.sum(expo, axis=-1, keepdims=True)).astype(bf16)
    return jnp.einsum(
        "rshl,rlc->rshc", probs, latents[:, :, :latent_width], preferred_element_type=f32
    ).astype(bf16)


def local(
    cache,
    cache_length,
    move_slot,
    move_peer,
    queries,
    new_latent,
    value_up,
    out_proj,
    residual,
    norm_gain,
    gate_weight,
    up_weight,
    down_weight,
):
    member = lax.axis_index(TP)
    x = lax.axis_index("x")
    z = lax.axis_index("zl")
    core = lax.axis_index("c")
    own_first = core == 0
    lanes = jnp.arange(N_TP, dtype=jnp.int32)
    own_slot = jnp.sum(jnp.where(lanes == member, move_slot[0], 0))
    rows_dev = cache.shape[0]
    heads, latent_width, value_width = value_up.shape
    rows_out = residual.shape[1] // N_TP
    features, units = gate_weight.shape
    part = units // 2

    gain = norm_gain.astype(f32)[:, None]

    def columns(index):
        return jnp.concatenate(
            [
                lax.dynamic_slice_in_dim(weight, index * part, part, 1).astype(f32) * gain
                for weight in (gate_weight, up_weight)
            ],
            axis=1,
        ).astype(bf16)

    kept = columns(z)
    came = lax.ppermute(columns(1 - z), "zl", SWAP)

    latents = migrate(cache, move_slot[0], move_peer[0], member, own_slot)
    positions = jnp.arange(latents.shape[1], dtype=jnp.int32)[None, :]
    steps = new_latent.shape[0]
    for step in range(steps):
        latents = jnp.where(
            (positions == cache_length[:, None] + step)[:, :, None],
            new_latent[step][:, None, :],
            latents,
        )
    limit = cache_length[:, None] + jnp.arange(steps, dtype=jnp.int32)[None, :]
    out = attend(latents, limit, queries, latent_width)
    out = out.reshape(rows_dev, steps, N_TP, heads, latent_width)
    out = out.transpose(2, 0, 1, 3, 4).reshape(N_TP, rows_dev, steps * heads, latent_width)
    by_head = exchange(out, TP).reshape(-1, heads, latent_width)
    by_head, kept, came = lax.optimization_barrier((by_head, kept, came))
    value_heads = jnp.einsum(
        "thl,hlv->thv", by_head, value_up, preferred_element_type=f32
    ).astype(bf16)
    value_heads = value_heads.reshape(2, rows_out * steps, heads * value_width)

    def sum_tp(own, other, weight):
        chunk = own.shape[0] // N_ZY
        away = jnp.dot(other, weight, preferred_element_type=f32).astype(bf16)
        near = lax.ppermute(away, "c", SWAP)
        total = jnp.dot(own, weight, preferred_element_type=f32) + near.astype(f32)
        parts = exchange(total.astype(bf16).reshape(N_ZY, chunk, -1), ZY)
        return jnp.sum(parts.astype(f32), axis=0)

    gathered = gather_dp(value_heads, x, z)
    width = gathered.shape[-1]
    own = lax.dynamic_index_in_dim(gathered, core, 2, False).reshape(-1, width)
    other = lax.dynamic_index_in_dim(gathered, 1 - core, 2, False).reshape(-1, width)
    attended = sum_tp(own, other, out_proj)
    residue = lax.dynamic_slice_in_dim(residual, member * rows_out, rows_out, 1)
    residue = residue.transpose(1, 0, 2).reshape(attended.shape)
    hidden = residue.astype(f32) + attended

    def feed(rows):
        own = spread(rows.astype(bf16), ("zl",) + ZY, 2 * N_ZY)
        own = own.reshape(2, N_X, -1, features)
        other = lax.ppermute(own, "c", SWAP)

        def partial(by):
            at = lax.rem(x + by, N_X)

            def pick(at_z):
                start = (at_z, at, 0, 0)
                size = (1, 1) + own.shape[2:]
                return jnp.concatenate(
                    [lax.dynamic_slice(half, start, size)[0, 0] for half in (own, other)], axis=0
                )

            mine, near = pick(z), pick(1 - z)
            wide = mine.astype(f32)
            squares = jnp.sum(wide * wide, axis=1, keepdims=True)
            wide = near.astype(f32)
            squares = squares + jnp.sum(wide * wide, axis=1, keepdims=True)
            both = jnp.dot(mine, kept, preferred_element_type=f32)
            return both + jnp.dot(near, came, preferred_element_type=f32), squares

        lane = jnp.arange(128)[None, :]
        arrived = []
        for by in (2, 1, 3):
            both, squares = partial(by)
            high = squares.astype(bf16)
            low = (squares - high.astype(f32)).astype(bf16)
            extra = jnp.where(lane == 0, high, jnp.where(lane == 1, low, jnp.zeros_like(low)))
            sent = jnp.concatenate([both.astype(bf16), extra], axis=1)
            arrived.append(shift_x(sent, by).astype(f32))
        total, squares = partial(0)
        for block in arrived:
            total = total + block[:, : 2 * part]
            squares = squares + block[:, 2 * part : 2 * part + 1]
            squares = squares + block[:, 2 * part + 1 : 2 * part + 2]
        inverse = lax.rsqrt(squares / D + norm_eps)
        active = jax.nn.silu(total[:, :part] * inverse) * (total[:, part:] * inverse)
        return active.astype(bf16)

    def lower(active):
        gathered = gather_dp(active, x, z)
        rows = jnp.concatenate([gathered[:, 0], gathered[:, 1]], axis=-1)
        half = rows.shape[1] // 2
        own = rows[:, :half].reshape(-1, units)
        other = rows[:, half:].reshape(-1, units)
        return sum_tp(own, other, down_weight)

    cut = hidden.shape[0] // 2
    active = [feed(hidden[:cut]), feed(hidden[cut:])]
    ffn_out = jnp.concatenate([lower(a) for a in active], axis=0)
    result = (hidden + ffn_out).astype(bf16)
    return result.reshape(rows_out, steps, -1).transpose(1, 0, 2)


def solution(mesh):
    split = Mesh(mesh.devices.reshape(4, 2, 2, 4, 2), ("x", "zl", "zh", "y", "c"))
    in_specs = (
        P(DP + TP, None, None),
        P(DP + TP),
        P(DP, None),
        P(DP, None),
        P(None, DP + TP, None, None),
        P(None, DP + TP, None),
        P(TP, None, None),
        P(TP, DP),
        P(None, None, DP),
        P(DP),
        P(DP, TP),
        P(DP, TP),
        P(TP, DP),
    )
    out_specs = P(None, TP, DP)
    return jax.shard_map(local, mesh=split, in_specs=in_specs, out_specs=out_specs, check_vma=False)
```

```python
import jax
import jax.numpy as jnp
from jax import lax
from jax.experimental import pallas as pl
from jax.experimental.pallas import tpu as pltpu
from jax.sharding import Mesh, PartitionSpec as P

D = 7168
QKD = 192
norm_eps = 1e-06

DP = ("xh", "xl", "zl")
TP = ("zh", "y", "c")
ZY = ("zh", "y")
FOUR = ("xh", "zl")
PAIR = ("xl",) + ZY
N_DP = 8
N_TP = 16
N_ZY = 8
N_FOUR = 4
SWAP = [(0, 1), (1, 0)]
FIRST_ROWS = 384
bf16 = jnp.bfloat16
f32 = jnp.float32
VMEM = 48 * 1024 * 1024


def exchange(blocks, axes):
    return lax.all_to_all(blocks, axes, 0, 0, tiled=True)


def spread(block, axes, copies):
    return exchange(jnp.broadcast_to(block[None], (copies,) + block.shape), axes)


def swap(block, axis):
    return lax.ppermute(block, axis, SWAP)


def params():
    return pltpu.CompilerParams(vmem_limit_bytes=VMEM)


def whole(shape):
    return pl.BlockSpec(shape, lambda *_: (0,) * len(shape))


def leave(ids, cache_t):
    _, entries, length = cache_t.shape
    piece = entries // N_TP

    def body(ids_ref, row_ref, out_ref):
        row = row_ref[0].astype(f32)
        for j in range(N_TP):
            out_ref[j] = row[j * piece : (j + 1) * piece].astype(bf16)

    return pl.pallas_call(
        body,
        grid_spec=pltpu.PrefetchScalarGridSpec(
            num_scalar_prefetch=1,
            grid=(1,),
            in_specs=[pl.BlockSpec((1, entries, length), lambda i, ids: (ids[0], 0, 0))],
            out_specs=whole((N_TP, piece, length)),
        ),
        out_shape=jax.ShapeDtypeStruct((N_TP, piece, length), bf16),
        compiler_params=params(),
        name="leave",
    )(ids, cache_t)


def route(peer, pieces):
    def body(peer_ref, in_ref, out_ref):
        for i in range(N_TP):
            out_ref[peer_ref[i]] = in_ref[i]

    return pl.pallas_call(
        body,
        grid_spec=pltpu.PrefetchScalarGridSpec(
            num_scalar_prefetch=1,
            grid=(1,),
            in_specs=[whole(pieces.shape)],
            out_specs=whole(pieces.shape),
        ),
        out_shape=jax.ShapeDtypeStruct(pieces.shape, bf16),
        compiler_params=params(),
        name="route",
    )(peer, pieces)


def attend(ids, lengths, cache_t, arrived, fresh_t, queries_t, heads, latent_width):
    rows, entries, length = cache_t.shape
    steps, _, _, all_heads = queries_t.shape
    parts = all_heads // heads

    def body(ids_ref, lengths_ref, cache_ref, arrived_ref, fresh_ref, q_ref, out_ref):
        r = pl.program_id(0)
        here = r == ids_ref[0]
        came = jnp.concatenate([arrived_ref[j].astype(f32) for j in range(N_TP)], axis=0)
        latents = jnp.where(here, came, cache_ref[0].astype(f32))
        current = lengths_ref[r]
        position = lax.broadcasted_iota(jnp.int32, (entries, length), 1)
        for s in range(steps):
            token = fresh_ref[0, :, s : s + 1].astype(f32)
            latents = jnp.where(position == current + s, token, latents)
        latents = latents.astype(bf16)
        place = lax.broadcasted_iota(jnp.int32, (all_heads, length), 1)
        outs = []
        for s in range(steps):
            scores = lax.dot_general(
                q_ref[s, 0], latents, (((0,), (0,)), ((), ())), preferred_element_type=f32
            )
            scores = jnp.where(place <= current + s, scores * QKD ** (-0.5), -jnp.inf)
            expo = jnp.exp(scores - jnp.max(scores, axis=-1, keepdims=True))
            probs = (expo / jnp.sum(expo, axis=-1, keepdims=True)).astype(bf16)
            out = lax.dot_general(
                probs, latents[:latent_width], (((1,), (1,)), ((), ())), preferred_element_type=f32
            )
            outs.append(out.reshape(parts, heads, latent_width))
        out_ref[:, 0] = jnp.concatenate(outs, axis=1).astype(bf16)

    return pl.pallas_call(
        body,
        grid_spec=pltpu.PrefetchScalarGridSpec(
            num_scalar_prefetch=2,
            grid=(rows,),
            in_specs=[
                pl.BlockSpec((1, entries, length), lambda r, *_: (r, 0, 0)),
                whole(arrived.shape),
                pl.BlockSpec((1, entries, steps), lambda r, *_: (r, 0, 0)),
                pl.BlockSpec((steps, 1, entries, all_heads), lambda r, *_: (0, r, 0, 0)),
            ],
            out_specs=pl.BlockSpec(
                (parts, 1, steps * heads, latent_width), lambda r, *_: (0, r, 0, 0)
            ),
        ),
        out_shape=jax.ShapeDtypeStruct((parts, rows, steps * heads, latent_width), bf16),
        compiler_params=params(),
        name="attend",
    )(ids, lengths, cache_t, arrived, fresh_t, queries_t)


def project(ids, half, rows, weights, near=None):
    groups, _, count, depth = rows.shape
    width = weights[0].shape[1]
    blocks = len(weights)
    per = groups // 2

    def body(ids_ref, rows_ref, *refs):
        out_ref = refs[-1]
        lhs = rows_ref[...].reshape(per * count, depth)
        for k in range(blocks):
            at = lax.rem(ids_ref[2] + k, blocks)
            total = jnp.dot(lhs, refs[k][...], preferred_element_type=f32)
            if near is not None:
                total = total + refs[blocks][at].astype(f32)
            out_ref[at] = total.astype(bf16)

    block = pl.BlockSpec((blocks, per * count, width), lambda i, ids: (0, i, 0))
    extra = [] if near is None else [near]
    return pl.pallas_call(
        body,
        grid_spec=pltpu.PrefetchScalarGridSpec(
            num_scalar_prefetch=1,
            grid=(2,),
            in_specs=[pl.BlockSpec((per, 1, count, depth), lambda i, ids: (i, half(ids), 0, 0))]
            + [whole(w.shape) for w in weights]
            + [block for _ in extra],
            out_specs=block,
        ),
        out_shape=jax.ShapeDtypeStruct((blocks, groups * count, width), bf16),
        compiler_params=params(),
        name="project",
    )(ids, rows, *weights, *extra)


def widen(ids, own, other, kept, came):
    _, _, chunk, features = own.shape
    columns = kept.shape[1]
    per = 2 * chunk

    def body(ids_ref, own_ref, other_ref, kept_ref, first_ref, second_ref, out_ref):
        pair = ids_ref[2]

        def pick(at):
            return jnp.concatenate(
                [ref[at].reshape(per, features) for ref in (own_ref, other_ref)], axis=0
            )

        mine, near = pick(pair), pick(1 - pair)
        total = jnp.dot(mine, kept_ref[...], preferred_element_type=f32)
        total += jnp.dot(near[:, :FIRST_ROWS], first_ref[...], preferred_element_type=f32)
        total += jnp.dot(near[:, FIRST_ROWS:], second_ref[...], preferred_element_type=f32)
        out_ref[0, :, :columns] = total.astype(bf16)
        squares = jnp.zeros((2 * per, 1), f32)
        for rows in (mine, near):
            wide = rows.astype(f32)
            squares += jnp.sum(wide * wide, axis=1, keepdims=True)
        high = squares.astype(bf16).astype(f32)
        lane = lax.broadcasted_iota(jnp.int32, (2 * per, 128), 1)
        extra = jnp.where(lane == 0, high, jnp.where(lane == 1, squares - high, 0.0))
        out_ref[0, :, columns:] = extra.astype(bf16)

    rows = pl.BlockSpec((2, 2, chunk, features), lambda q, ids: (0, q, 0, 0))
    return pl.pallas_call(
        body,
        grid_spec=pltpu.PrefetchScalarGridSpec(
            num_scalar_prefetch=1,
            grid=(N_FOUR,),
            in_specs=[rows, rows] + [whole(w.shape) for w in (kept,) + came],
            out_specs=pl.BlockSpec((1, 2 * per, columns + 128), lambda q, ids: (q, 0, 0)),
        ),
        out_shape=jax.ShapeDtypeStruct((N_FOUR, 2 * per, columns + 128), bf16),
        compiler_params=params(),
        name="widen",
    )(ids, own, other, kept, *came)


def local(
    cache,
    cache_length,
    move_slot,
    move_peer,
    queries,
    new_latent,
    value_up,
    out_proj,
    residual,
    norm_gain,
    gate_weight,
    up_weight,
    down_weight,
):
    member = lax.axis_index(TP)
    core = lax.axis_index("c")
    pair = lax.axis_index("xl")
    rows_dev = cache.shape[0]
    steps = new_latent.shape[0]
    heads, latent_width, value_width = value_up.shape
    rows_out = residual.shape[1] // N_TP
    chunk = rows_out * steps
    features, units = gate_weight.shape
    part = units // 2

    lanes = jnp.arange(N_TP, dtype=jnp.int32)
    own_slot = jnp.sum(jnp.where(lanes == member, move_slot[0], 0))
    ids = jnp.stack([own_slot, core, pair]).astype(jnp.int32)
    cache_t = cache.transpose(0, 2, 1)
    pieces = exchange(leave(ids, cache_t), TP)

    gain = norm_gain.astype(f32)[:, None]

    def columns(index, low, high):
        return jnp.concatenate(
            [
                lax.dynamic_slice(w, (low, index * part), (high - low, part)).astype(f32)
                * gain[low:high]
                for w in (gate_weight, up_weight)
            ],
            axis=1,
        ).astype(bf16)

    came = (
        swap(columns(1 - pair, 0, FIRST_ROWS), "xl"),
        swap(columns(1 - pair, FIRST_ROWS, features), "xl"),
    )
    kept = columns(pair, 0, features)

    arrived = exchange(route(move_peer[0], pieces), TP)
    out = attend(
        ids,
        cache_length,
        cache_t,
        arrived,
        new_latent.transpose(1, 2, 0),
        queries.transpose(0, 1, 3, 2),
        heads,
        latent_width,
    )
    by_head = exchange(out, TP).reshape(-1, heads, latent_width)
    by_head, kept, came = lax.optimization_barrier((by_head, kept, came))
    value_heads = jnp.einsum(
        "thl,hlv->thv", by_head, value_up, preferred_element_type=f32
    ).astype(bf16)
    value_heads = value_heads.reshape(-1, heads * value_width)

    gathered = spread(value_heads, DP, N_DP).reshape(N_DP, 2, chunk, -1)
    gathered, down_weight = lax.optimization_barrier((gathered, down_weight))
    down_kept = lax.dynamic_slice_in_dim(down_weight, pair * part, part, 0)
    down_came = swap(lax.dynamic_slice_in_dim(down_weight, (1 - pair) * part, part, 0), "xl")
    away = swap(project(ids, lambda i: 1 - i[1], gathered, [out_proj]), "c")
    total = project(ids, lambda i: i[1], gathered, [out_proj], away)
    parts = exchange(total.reshape(N_ZY, chunk, -1), ZY)
    residue = lax.dynamic_slice_in_dim(residual, member * rows_out, rows_out, 1)
    residue = residue.transpose(1, 0, 2).reshape(chunk, -1)
    hidden = residue.astype(f32) + jnp.sum(parts.astype(f32), axis=0)

    own = spread(hidden.astype(bf16), PAIR, 2 * N_ZY).reshape(2, N_ZY, chunk, features)
    other = swap(own, "c")
    sums = exchange(widen(ids, own, other, kept, came), FOUR)
    sums = jnp.sum(sums.astype(f32), axis=0)
    squares = sums[:, units] + sums[:, units + 1]
    inverse = lax.rsqrt(squares / D + norm_eps)[:, None]
    active = jax.nn.silu(sums[:, :part] * inverse) * (sums[:, part:units] * inverse)
    active = spread(active.astype(bf16), FOUR, N_FOUR).reshape(N_FOUR, 2, 2 * chunk, part)

    weights = [down_kept, down_came]
    away = swap(project(ids, lambda i: 1, active, weights), "c")
    total = project(ids, lambda i: 0, active, weights, away)
    parts = exchange(total.reshape(2 * N_ZY, chunk, -1), PAIR)
    result = (hidden + jnp.sum(parts.astype(f32), axis=0)).astype(bf16)
    return result.reshape(rows_out, steps, -1).transpose(1, 0, 2)


def solution(mesh):
    split = Mesh(
        mesh.devices.reshape(2, 2, 2, 2, 4, 2), ("xh", "xl", "zl", "zh", "y", "c")
    )
    in_specs = (
        P(DP + TP, None, None),
        P(DP + TP),
        P(DP, None),
        P(DP, None),
        P(None, DP + TP, None, None),
        P(None, DP + TP, None),
        P(TP, None, None),
        P(TP, DP),
        P(None, None, DP),
        P(DP),
        P(DP, TP),
        P(DP, TP),
        P(TP, DP),
    )
    out_specs = P(None, TP, DP)
    return jax.shard_map(local, mesh=split, in_specs=in_specs, out_specs=out_specs, check_vma=False)
```

```python
import jax
import jax.numpy as jnp
from jax import lax
from jax.experimental import pallas as pl
from jax.experimental.pallas import tpu as pltpu
from jax.sharding import Mesh, PartitionSpec as P

D = 7168
QKD = 192
norm_eps = 1e-06

DP = ("xh", "xl", "zl")
TP = ("zh", "y", "c")
ZY = ("zh", "y")
FOUR = ("xh", "zl")
PAIR = ("xl",) + ZY
N_DP = 8
N_TP = 16
N_ZY = 8
N_FOUR = 4
SWAP = [(0, 1), (1, 0)]
CUTS = (0, 384, 640, 896)
TILE = 384
bf16 = jnp.bfloat16
f32 = jnp.float32
VMEM = 48 * 1024 * 1024


def exchange(blocks, axes):
    return lax.all_to_all(blocks, axes, 0, 0, tiled=True)


def spread(block, axes, copies):
    return exchange(jnp.broadcast_to(block[None], (copies,) + block.shape), axes)


def swap(block, axis):
    return lax.ppermute(block, axis, SWAP)


def params():
    return pltpu.CompilerParams(vmem_limit_bytes=VMEM)


def whole(shape):
    return pl.BlockSpec(shape, lambda *_: (0,) * len(shape))


def leave(ids, cache_t):
    _, entries, length = cache_t.shape
    piece = entries // N_TP

    def body(ids_ref, row_ref, out_ref):
        row = row_ref[0].astype(f32)
        for j in range(N_TP):
            out_ref[j] = row[j * piece : (j + 1) * piece].astype(bf16)

    return pl.pallas_call(
        body,
        grid_spec=pltpu.PrefetchScalarGridSpec(
            num_scalar_prefetch=1,
            grid=(1,),
            in_specs=[pl.BlockSpec((1, entries, length), lambda i, ids: (ids[0], 0, 0))],
            out_specs=whole((N_TP, piece, length)),
        ),
        out_shape=jax.ShapeDtypeStruct((N_TP, piece, length), bf16),
        compiler_params=params(),
        name="leave",
    )(ids, cache_t)


def route(peer, pieces):
    def body(peer_ref, in_ref, out_ref):
        for i in range(N_TP):
            out_ref[peer_ref[i]] = in_ref[i]

    return pl.pallas_call(
        body,
        grid_spec=pltpu.PrefetchScalarGridSpec(
            num_scalar_prefetch=1,
            grid=(1,),
            in_specs=[whole(pieces.shape)],
            out_specs=whole(pieces.shape),
        ),
        out_shape=jax.ShapeDtypeStruct(pieces.shape, bf16),
        compiler_params=params(),
        name="route",
    )(peer, pieces)


def attend(ids, lengths, cache_t, fresh_t, queries_t, heads, latent_width, arrived=None, done=None):
    rows, entries, length = cache_t.shape
    steps, _, _, all_heads = queries_t.shape
    parts = all_heads // heads
    again = arrived is not None

    def slot(r, ids):
        return ids[0] if again else r

    def body(ids_ref, lengths_ref, cache_ref, fresh_ref, q_ref, *refs):
        out_ref = refs[-1]
        current = lengths_ref[slot(pl.program_id(0), ids_ref)]
        if again:
            latents = jnp.concatenate([refs[0][j].astype(f32) for j in range(N_TP)], axis=0)
        else:
            latents = cache_ref[0].astype(f32)
        position = lax.broadcasted_iota(jnp.int32, (entries, length), 1)
        for s in range(steps):
            token = fresh_ref[0, :, s : s + 1].astype(f32)
            latents = jnp.where(position == current + s, token, latents)
        latents = latents.astype(bf16)
        place = lax.broadcasted_iota(jnp.int32, (all_heads, length), 1)
        outs = []
        for s in range(steps):
            scores = lax.dot_general(
                q_ref[s, 0], latents, (((0,), (0,)), ((), ())), preferred_element_type=f32
            )
            scores = jnp.where(place <= current + s, scores * QKD ** (-0.5), -jnp.inf)
            expo = jnp.exp(scores - jnp.max(scores, axis=-1, keepdims=True))
            probs = (expo / jnp.sum(expo, axis=-1, keepdims=True)).astype(bf16)
            out = lax.dot_general(
                probs, latents[:latent_width], (((1,), (1,)), ((), ())), preferred_element_type=f32
            )
            outs.append(out.reshape(parts, heads, latent_width))
        out_ref[:, 0] = jnp.concatenate(outs, axis=1).astype(bf16)

    extra_specs = [whole(arrived.shape), pl.BlockSpec(memory_space=pl.ANY)] if again else []
    extra = [arrived, done] if again else []
    return pl.pallas_call(
        body,
        grid_spec=pltpu.PrefetchScalarGridSpec(
            num_scalar_prefetch=2,
            grid=(1 if again else rows,),
            in_specs=[
                pl.BlockSpec((1, entries, length), lambda r, ids, _: (slot(r, ids), 0, 0)),
                pl.BlockSpec((1, entries, steps), lambda r, ids, _: (slot(r, ids), 0, 0)),
                pl.BlockSpec(
                    (steps, 1, entries, all_heads), lambda r, ids, _: (0, slot(r, ids), 0, 0)
                ),
            ]
            + extra_specs,
            out_specs=pl.BlockSpec(
                (parts, 1, steps * heads, latent_width),
                lambda r, ids, _: (0, slot(r, ids), 0, 0),
            ),
        ),
        out_shape=jax.ShapeDtypeStruct((parts, rows, steps * heads, latent_width), bf16),
        input_output_aliases={6: 0} if again else {},
        compiler_params=params(),
        name="again" if again else "attend",
    )(ids, lengths, cache_t, fresh_t, queries_t, *extra)


def project(ids, half, rows, weights, near=None):
    groups, _, count, depth = rows.shape
    width = weights[0].shape[1]
    blocks = len(weights)
    per = groups // 2

    def body(ids_ref, rows_ref, *refs):
        out_ref = refs[-1]
        lhs = rows_ref[...].reshape(per * count, depth)
        for k in range(blocks):
            at = lax.rem(ids_ref[2] + k, blocks)
            total = jnp.dot(lhs, refs[k][...], preferred_element_type=f32)
            if near is not None:
                total = total + refs[blocks][at].astype(f32)
            out_ref[at] = total.astype(bf16)

    block = pl.BlockSpec((blocks, per * count, width), lambda i, ids: (0, i, 0))
    extra = [] if near is None else [near]
    return pl.pallas_call(
        body,
        grid_spec=pltpu.PrefetchScalarGridSpec(
            num_scalar_prefetch=1,
            grid=(2,),
            in_specs=[pl.BlockSpec((per, 1, count, depth), lambda i, ids: (i, half(ids), 0, 0))]
            + [whole(w.shape) for w in weights]
            + [block for _ in extra],
            out_specs=block,
        ),
        out_shape=jax.ShapeDtypeStruct((blocks, groups * count, width), bf16),
        compiler_params=params(),
        name="project",
    )(ids, rows, *weights, *extra)


def widen(ids, rows, kept, came, side, done=None):
    _, count, chunk, features = rows.shape
    columns = kept.shape[1]
    per = count * chunk // N_FOUR
    starts = [0]
    for w in came:
        starts.append(starts[-1] + w.shape[0])

    def body(ids_ref, rows_ref, kept_ref, *refs):
        out_ref = refs[-1]
        pair = ids_ref[2]
        mine = rows_ref[pair].reshape(count * chunk, features)
        near = rows_ref[1 - pair].reshape(count * chunk, features)
        for at in range(0, columns, TILE):
            tile = slice(at, at + TILE)
            total = jnp.dot(mine, kept_ref[:, tile], preferred_element_type=f32)
            for k in range(len(came)):
                total += jnp.dot(
                    near[:, starts[k] : starts[k + 1]],
                    refs[k][:, tile],
                    preferred_element_type=f32,
                )
            out_ref[:, 0, :, tile] = total.astype(bf16).reshape(N_FOUR, per, TILE)
        squares = jnp.zeros((count * chunk, 1), f32)
        for half in (mine, near):
            wide = half.astype(f32)
            squares += jnp.sum(wide * wide, axis=1, keepdims=True)
        high = squares.astype(bf16).astype(f32)
        lane = lax.broadcasted_iota(jnp.int32, (count * chunk, 128), 1)
        extra = jnp.where(lane == 0, high, jnp.where(lane == 1, squares - high, 0.0))
        out_ref[:, 0, :, columns:] = extra.astype(bf16).reshape(N_FOUR, per, 128)

    last = [] if done is None else [done]
    return pl.pallas_call(
        body,
        grid_spec=pltpu.PrefetchScalarGridSpec(
            num_scalar_prefetch=1,
            grid=(1,),
            in_specs=[whole(rows.shape)]
            + [whole(w.shape) for w in (kept,) + came]
            + [pl.BlockSpec(memory_space=pl.ANY) for _ in last],
            out_specs=pl.BlockSpec(
                (N_FOUR, 1, per, columns + 128), lambda i, ids: (0, side, 0, 0)
            ),
        ),
        out_shape=jax.ShapeDtypeStruct((N_FOUR, 2, per, columns + 128), bf16),
        input_output_aliases={3 + len(came): 0} if last else {},
        compiler_params=params(),
        name="widen",
    )(ids, rows, kept, *came, *last)


def local(
    cache,
    cache_length,
    move_slot,
    move_peer,
    queries,
    new_latent,
    value_up,
    out_proj,
    residual,
    norm_gain,
    gate_weight,
    up_weight,
    down_weight,
):
    member = lax.axis_index(TP)
    core = lax.axis_index("c")
    pair = lax.axis_index("xl")
    rows_dev = cache.shape[0]
    steps = new_latent.shape[0]
    heads, latent_width, value_width = value_up.shape
    rows_out = residual.shape[1] // N_TP
    chunk = rows_out * steps
    features, units = gate_weight.shape
    part = units // 2

    lanes = jnp.arange(N_TP, dtype=jnp.int32)
    own_slot = jnp.sum(jnp.where(lanes == member, move_slot[0], 0))
    ids = jnp.stack([own_slot, core, pair]).astype(jnp.int32)
    cache_t = cache.transpose(0, 2, 1)
    pieces = exchange(leave(ids, cache_t), TP)

    gain = norm_gain.astype(f32)[:, None]

    def columns(index, low, high):
        return jnp.concatenate(
            [
                lax.dynamic_slice(w, (low, index * part), (high - low, part)).astype(f32)
                * gain[low:high]
                for w in (gate_weight, up_weight)
            ],
            axis=1,
        ).astype(bf16)

    sent = [columns(1 - pair, low, high) for low, high in zip(CUTS[:-1], CUTS[1:])]
    kept = columns(pair, 0, features)
    came = [swap(sent[0], "xl"), swap(sent[1], "xl")]

    arrived = exchange(route(move_peer[0], pieces), TP)
    fresh_t = new_latent.transpose(1, 2, 0)
    queries_t = queries.transpose(0, 1, 3, 2)
    out = attend(ids, cache_length, cache_t, fresh_t, queries_t, heads, latent_width)
    out = attend(
        ids, cache_length, cache_t, fresh_t, queries_t, heads, latent_width, arrived, out
    )
    out, came[0] = lax.optimization_barrier((out, came[0]))
    by_head = exchange(out, TP).reshape(-1, heads, latent_width)
    by_head, kept, came[1] = lax.optimization_barrier((by_head, kept, came[1]))
    value_heads = jnp.einsum(
        "thl,hlv->thv", by_head, value_up, preferred_element_type=f32
    ).astype(bf16)
    value_heads = value_heads.reshape(-1, heads * value_width)

    gathered = spread(value_heads, DP, N_DP).reshape(N_DP, 2, chunk, -1)
    down_sent = lax.dynamic_slice_in_dim(down_weight, (1 - pair) * part, part, 0)
    gathered, sent[2], down_sent = lax.optimization_barrier((gathered, sent[2], down_sent))
    down_kept = lax.dynamic_slice_in_dim(down_weight, pair * part, part, 0)
    down_came = swap(down_sent, "xl")
    came.append(swap(sent[2], "xl"))
    away = swap(project(ids, lambda i: 1 - i[1], gathered, [out_proj]), "c")
    total = project(ids, lambda i: i[1], gathered, [out_proj], away)
    parts = exchange(total.reshape(N_ZY, chunk, -1), ZY)
    parts, down_came, came[2] = lax.optimization_barrier((parts, down_came, came[2]))
    residue = lax.dynamic_slice_in_dim(residual, member * rows_out, rows_out, 1)
    residue = residue.transpose(1, 0, 2).reshape(chunk, -1)
    hidden = residue.astype(f32) + jnp.sum(parts.astype(f32), axis=0)

    own = spread(hidden.astype(bf16), PAIR, 2 * N_ZY).reshape(2, N_ZY, chunk, features)
    other = swap(own, "c")
    came = tuple(came)
    wide = widen(ids, own, kept, came, 0)
    wide = widen(ids, other, kept, came, 1, wide)
    sums = exchange(wide.reshape(N_FOUR, 4 * chunk, -1), FOUR)
    sums = jnp.sum(sums.astype(f32), axis=0)
    squares = sums[:, units] + sums[:, units + 1]
    inverse = lax.rsqrt(squares / D + norm_eps)[:, None]
    active = jax.nn.silu(sums[:, :part] * inverse) * (sums[:, part:units] * inverse)
    active = spread(active.astype(bf16), FOUR, N_FOUR).reshape(N_FOUR, 2, 2 * chunk, part)

    weights = [down_kept, down_came]
    away = swap(project(ids, lambda i: 1, active, weights), "c")
    total = project(ids, lambda i: 0, active, weights, away)
    parts = exchange(total.reshape(2 * N_ZY, chunk, -1), PAIR)
    result = (hidden + jnp.sum(parts.astype(f32), axis=0)).astype(bf16)
    return result.reshape(rows_out, steps, -1).transpose(1, 0, 2)


def solution(mesh):
    split = Mesh(
        mesh.devices.reshape(2, 2, 2, 2, 4, 2), ("xh", "xl", "zl", "zh", "y", "c")
    )
    in_specs = (
        P(DP + TP, None, None),
        P(DP + TP),
        P(DP, None),
        P(DP, None),
        P(None, DP + TP, None, None),
        P(None, DP + TP, None),
        P(TP, None, None),
        P(TP, DP),
        P(None, None, DP),
        P(DP),
        P(DP, TP),
        P(DP, TP),
        P(TP, DP),
    )
    out_specs = P(None, TP, DP)
    return jax.shard_map(local, mesh=split, in_specs=in_specs, out_specs=out_specs, check_vma=False)
```

```python
import jax
import jax.numpy as jnp
from jax import lax
from jax.experimental import pallas as pl
from jax.experimental.pallas import tpu as pltpu
from jax.sharding import Mesh, PartitionSpec as P

D = 7168
QKD = 192
norm_eps = 1e-06

DP = ("xh", "xl", "zl")
TP = ("zh", "y", "c")
ZY = ("zh", "y")
FOUR = ("xh", "zl")
PAIR = ("xl",) + ZY
N_DP = 8
N_TP = 16
N_ZY = 8
N_FOUR = 4
SWAP = [(0, 1), (1, 0)]
CUTS = (0, 640, 896)
TILE = 384
bf16 = jnp.bfloat16
f32 = jnp.float32
VMEM = 48 * 1024 * 1024


def exchange(blocks, axes):
    return lax.all_to_all(blocks, axes, 0, 0, tiled=True)


def spread(block, axes, copies):
    return exchange(jnp.broadcast_to(block[None], (copies,) + block.shape), axes)


def swap(block, axis):
    return lax.ppermute(block, axis, SWAP)


def params():
    return pltpu.CompilerParams(vmem_limit_bytes=VMEM)


def whole(shape):
    return pl.BlockSpec(shape, lambda *_: (0,) * len(shape))


def leave(ids, cache_t):
    _, entries, length = cache_t.shape
    piece = entries // N_TP

    def body(ids_ref, row_ref, out_ref):
        row = row_ref[0].astype(f32)
        for j in range(N_TP):
            out_ref[j] = row[j * piece : (j + 1) * piece].astype(bf16)

    return pl.pallas_call(
        body,
        grid_spec=pltpu.PrefetchScalarGridSpec(
            num_scalar_prefetch=1,
            grid=(1,),
            in_specs=[pl.BlockSpec((1, entries, length), lambda i, ids: (ids[0], 0, 0))],
            out_specs=whole((N_TP, piece, length)),
        ),
        out_shape=jax.ShapeDtypeStruct((N_TP, piece, length), bf16),
        compiler_params=params(),
        name="leave",
    )(ids, cache_t)


def route(peer, pieces):
    def body(peer_ref, in_ref, out_ref):
        for i in range(N_TP):
            out_ref[peer_ref[i]] = in_ref[i]

    return pl.pallas_call(
        body,
        grid_spec=pltpu.PrefetchScalarGridSpec(
            num_scalar_prefetch=1,
            grid=(1,),
            in_specs=[whole(pieces.shape)],
            out_specs=whole(pieces.shape),
        ),
        out_shape=jax.ShapeDtypeStruct(pieces.shape, bf16),
        compiler_params=params(),
        name="route",
    )(peer, pieces)


def attend(ids, lengths, cache_t, fresh_t, queries_t, heads, latent_width, arrived=None, done=None):
    rows, entries, length = cache_t.shape
    steps, _, _, all_heads = queries_t.shape
    parts = all_heads // heads
    again = arrived is not None

    def slot(r, ids):
        return ids[0] if again else r

    def body(ids_ref, lengths_ref, cache_ref, fresh_ref, q_ref, *refs):
        out_ref = refs[-1]
        current = lengths_ref[slot(pl.program_id(0), ids_ref)]
        if again:
            latents = jnp.concatenate([refs[0][j].astype(f32) for j in range(N_TP)], axis=0)
        else:
            latents = cache_ref[0].astype(f32)
        position = lax.broadcasted_iota(jnp.int32, (entries, length), 1)
        for s in range(steps):
            token = fresh_ref[0, :, s : s + 1].astype(f32)
            latents = jnp.where(position == current + s, token, latents)
        latents = latents.astype(bf16)
        place = lax.broadcasted_iota(jnp.int32, (all_heads, length), 1)
        outs = []
        for s in range(steps):
            scores = lax.dot_general(
                q_ref[s, 0], latents, (((0,), (0,)), ((), ())), preferred_element_type=f32
            )
            scores = jnp.where(place <= current + s, scores * QKD ** (-0.5), -jnp.inf)
            expo = jnp.exp(scores - jnp.max(scores, axis=-1, keepdims=True))
            probs = (expo / jnp.sum(expo, axis=-1, keepdims=True)).astype(bf16)
            out = lax.dot_general(
                probs, latents[:latent_width], (((1,), (1,)), ((), ())), preferred_element_type=f32
            )
            outs.append(out.reshape(parts, heads, latent_width))
        out_ref[:, 0] = jnp.concatenate(outs, axis=1).astype(bf16)

    extra_specs = [whole(arrived.shape), pl.BlockSpec(memory_space=pl.ANY)] if again else []
    extra = [arrived, done] if again else []
    return pl.pallas_call(
        body,
        grid_spec=pltpu.PrefetchScalarGridSpec(
            num_scalar_prefetch=2,
            grid=(1 if again else rows,),
            in_specs=[
                pl.BlockSpec((1, entries, length), lambda r, ids, _: (slot(r, ids), 0, 0)),
                pl.BlockSpec((1, entries, steps), lambda r, ids, _: (slot(r, ids), 0, 0)),
                pl.BlockSpec(
                    (steps, 1, entries, all_heads), lambda r, ids, _: (0, slot(r, ids), 0, 0)
                ),
            ]
            + extra_specs,
            out_specs=pl.BlockSpec(
                (parts, 1, steps * heads, latent_width),
                lambda r, ids, _: (0, slot(r, ids), 0, 0),
            ),
        ),
        out_shape=jax.ShapeDtypeStruct((parts, rows, steps * heads, latent_width), bf16),
        input_output_aliases={6: 0} if again else {},
        compiler_params=params(),
        name="again" if again else "attend",
    )(ids, lengths, cache_t, fresh_t, queries_t, *extra)


def project(ids, half, rows, weights, near=None):
    groups, _, count, depth = rows.shape
    width = weights[0].shape[1]
    blocks = len(weights)
    per = groups // 2

    def body(ids_ref, rows_ref, *refs):
        out_ref = refs[-1]
        lhs = rows_ref[...].reshape(per * count, depth)
        for k in range(blocks):
            at = lax.rem(ids_ref[2] + k, blocks)
            total = jnp.dot(lhs, refs[k][...], preferred_element_type=f32)
            if near is not None:
                total = total + refs[blocks][at].astype(f32)
            out_ref[at] = total.astype(bf16)

    block = pl.BlockSpec((blocks, per * count, width), lambda i, ids: (0, i, 0))
    extra = [] if near is None else [near]
    return pl.pallas_call(
        body,
        grid_spec=pltpu.PrefetchScalarGridSpec(
            num_scalar_prefetch=1,
            grid=(2,),
            in_specs=[pl.BlockSpec((per, 1, count, depth), lambda i, ids: (i, half(ids), 0, 0))]
            + [whole(w.shape) for w in weights]
            + [block for _ in extra],
            out_specs=block,
        ),
        out_shape=jax.ShapeDtypeStruct((blocks, groups * count, width), bf16),
        compiler_params=params(),
        name="project",
    )(ids, rows, *weights, *extra)


def widen(ids, rows, kept, came, side, done=None):
    _, count, chunk, features = rows.shape
    columns = kept.shape[1]
    per = count * chunk // N_FOUR
    starts = [0]
    for w in came:
        starts.append(starts[-1] + w.shape[0])

    def body(ids_ref, rows_ref, kept_ref, *refs):
        out_ref = refs[-1]
        pair = ids_ref[2]
        mine = rows_ref[pair].reshape(count * chunk, features)
        near = rows_ref[1 - pair].reshape(count * chunk, features)
        for at in range(0, columns, TILE):
            tile = slice(at, at + TILE)
            total = jnp.dot(mine, kept_ref[:, tile], preferred_element_type=f32)
            for k in range(len(came)):
                total += jnp.dot(
                    near[:, starts[k] : starts[k + 1]],
                    refs[k][:, tile],
                    preferred_element_type=f32,
                )
            out_ref[:, 0, :, tile] = total.astype(bf16).reshape(N_FOUR, per, TILE)
        squares = jnp.zeros((count * chunk, 1), f32)
        for half in (mine, near):
            wide = half.astype(f32)
            squares += jnp.sum(wide * wide, axis=1, keepdims=True)
        high = squares.astype(bf16).astype(f32)
        lane = lax.broadcasted_iota(jnp.int32, (count * chunk, 128), 1)
        extra = jnp.where(lane == 0, high, jnp.where(lane == 1, squares - high, 0.0))
        out_ref[:, 0, :, columns:] = extra.astype(bf16).reshape(N_FOUR, per, 128)

    last = [] if done is None else [done]
    return pl.pallas_call(
        body,
        grid_spec=pltpu.PrefetchScalarGridSpec(
            num_scalar_prefetch=1,
            grid=(1,),
            in_specs=[whole(rows.shape)]
            + [whole(w.shape) for w in (kept,) + came]
            + [pl.BlockSpec(memory_space=pl.ANY) for _ in last],
            out_specs=pl.BlockSpec(
                (N_FOUR, 1, per, columns + 128), lambda i, ids: (0, side, 0, 0)
            ),
        ),
        out_shape=jax.ShapeDtypeStruct((N_FOUR, 2, per, columns + 128), bf16),
        input_output_aliases={3 + len(came): 0} if last else {},
        compiler_params=params(),
        name="widen",
    )(ids, rows, kept, *came, *last)


def local(
    cache,
    cache_length,
    move_slot,
    move_peer,
    queries,
    new_latent,
    value_up,
    out_proj,
    residual,
    norm_gain,
    gate_weight,
    up_weight,
    down_weight,
):
    member = lax.axis_index(TP)
    core = lax.axis_index("c")
    pair = lax.axis_index("xl")
    rows_dev = cache.shape[0]
    steps = new_latent.shape[0]
    heads, latent_width, value_width = value_up.shape
    rows_out = residual.shape[1] // N_TP
    chunk = rows_out * steps
    features, units = gate_weight.shape
    part = units // 2

    lanes = jnp.arange(N_TP, dtype=jnp.int32)
    own_slot = jnp.sum(jnp.where(lanes == member, move_slot[0], 0))
    ids = jnp.stack([own_slot, core, pair]).astype(jnp.int32)
    cache_t = cache.transpose(0, 2, 1)
    leaving, gate_weight, up_weight = lax.optimization_barrier(
        (leave(ids, cache_t), gate_weight, up_weight)
    )
    pieces = exchange(leaving, TP)

    gain = norm_gain.astype(f32)[:, None]

    def columns(index, low, high):
        return jnp.concatenate(
            [
                lax.dynamic_slice(w, (low, index * part), (high - low, part)).astype(f32)
                * gain[low:high]
                for w in (gate_weight, up_weight)
            ],
            axis=1,
        ).astype(bf16)

    sent = [columns(1 - pair, low, high) for low, high in zip(CUTS[:-1], CUTS[1:])]
    kept = columns(pair, 0, features)
    came = [swap(sent[0], "xl"), swap(sent[1], "xl")]

    arrived = exchange(route(move_peer[0], pieces), TP)
    fresh_t = new_latent.transpose(1, 2, 0)
    queries_t = queries.transpose(0, 1, 3, 2)
    out = attend(ids, cache_length, cache_t, fresh_t, queries_t, heads, latent_width)
    out = attend(
        ids, cache_length, cache_t, fresh_t, queries_t, heads, latent_width, arrived, out
    )
    out, came[0] = lax.optimization_barrier((out, came[0]))
    by_head = exchange(out, TP).reshape(-1, heads, latent_width)
    by_head, kept, came[1] = lax.optimization_barrier((by_head, kept, came[1]))
    value_heads = jnp.einsum(
        "thl,hlv->thv", by_head, value_up, preferred_element_type=f32
    ).astype(bf16)
    value_heads = value_heads.reshape(-1, heads * value_width)

    gathered = spread(value_heads, DP, N_DP).reshape(N_DP, 2, chunk, -1)
    away = swap(project(ids, lambda i: 1 - i[1], gathered, [out_proj]), "c")
    total = project(ids, lambda i: i[1], gathered, [out_proj], away)
    parts = exchange(total.reshape(N_ZY, chunk, -1), ZY)
    residue = lax.dynamic_slice_in_dim(residual, member * rows_out, rows_out, 1)
    residue = residue.transpose(1, 0, 2).reshape(chunk, -1)
    hidden = residue.astype(f32) + jnp.sum(parts.astype(f32), axis=0)

    own = spread(hidden.astype(bf16), PAIR, 2 * N_ZY).reshape(2, N_ZY, chunk, features)
    other = swap(own, "c")
    came = tuple(came)
    wide = widen(ids, own, kept, came, 0)
    wide = widen(ids, other, kept, came, 1, wide)
    sums = exchange(wide.reshape(N_FOUR, 4 * chunk, -1), FOUR)
    sums = jnp.sum(sums.astype(f32), axis=0)
    squares = sums[:, units] + sums[:, units + 1]
    inverse = lax.rsqrt(squares / D + norm_eps)[:, None]
    active = jax.nn.silu(sums[:, :part] * inverse) * (sums[:, part:units] * inverse)
    active = active.astype(bf16).reshape(2, 2 * chunk, part)
    active = spread(active, DP, N_DP).reshape(2, 2, 2, 2, 2 * chunk, part)
    active = jnp.concatenate([active[:, 0], active[:, 1]], axis=-1)
    active = active.reshape(N_FOUR, 2, 2 * chunk, units)
    away = swap(project(ids, lambda i: 1, active, [down_weight]), "c")
    total = project(ids, lambda i: 0, active, [down_weight], away)
    parts = exchange(total.reshape(N_ZY, chunk, -1), ZY)
    result = (hidden + jnp.sum(parts.astype(f32), axis=0)).astype(bf16)
    return result.reshape(rows_out, steps, -1).transpose(1, 0, 2)


def solution(mesh):
    split = Mesh(
        mesh.devices.reshape(2, 2, 2, 2, 4, 2), ("xh", "xl", "zl", "zh", "y", "c")
    )
    in_specs = (
        P(DP + TP, None, None),
        P(DP + TP),
        P(DP, None),
        P(DP, None),
        P(None, DP + TP, None, None),
        P(None, DP + TP, None),
        P(TP, None, None),
        P(TP, DP),
        P(None, None, DP),
        P(DP),
        P(DP, TP),
        P(DP, TP),
        P(TP, DP),
    )
    out_specs = P(None, TP, DP)
    return jax.shard_map(local, mesh=split, in_specs=in_specs, out_specs=out_specs, check_vma=False)
```

```python
import jax
import jax.numpy as jnp
from jax import lax
from jax.experimental import pallas as pl
from jax.experimental.pallas import tpu as pltpu
from jax.sharding import Mesh, PartitionSpec as P

D = 7168
QKD = 192
norm_eps = 1e-06

DP = ("xh", "xl", "zl")
TP = ("zh", "y", "c")
ZY = ("zh", "y")
PAIR = ("xl",) + ZY
N_DP = 8
N_TP = 16
N_ZY = 8
SWAP = [(0, 1), (1, 0)]
CUTS = (0, 384, 896)
TILE = 384
bf16 = jnp.bfloat16
f32 = jnp.float32
VMEM = 48 * 1024 * 1024


def exchange(blocks, axes):
    return lax.all_to_all(blocks, axes, 0, 0, tiled=True)


def spread(block, axes, copies):
    return exchange(jnp.broadcast_to(block[None], (copies,) + block.shape), axes)


def swap(block, axis):
    return lax.ppermute(block, axis, SWAP)


def params():
    return pltpu.CompilerParams(vmem_limit_bytes=VMEM)


def whole(shape):
    return pl.BlockSpec(shape, lambda *_: (0,) * len(shape))


def leave(ids, cache_t):
    _, entries, length = cache_t.shape
    piece = entries // N_TP

    def body(ids_ref, row_ref, out_ref):
        row = row_ref[0].astype(f32)
        for j in range(N_TP):
            out_ref[j] = row[j * piece : (j + 1) * piece].astype(bf16)

    return pl.pallas_call(
        body,
        grid_spec=pltpu.PrefetchScalarGridSpec(
            num_scalar_prefetch=1,
            grid=(1,),
            in_specs=[pl.BlockSpec((1, entries, length), lambda i, ids: (ids[0], 0, 0))],
            out_specs=whole((N_TP, piece, length)),
        ),
        out_shape=jax.ShapeDtypeStruct((N_TP, piece, length), bf16),
        compiler_params=params(),
        name="leave",
    )(ids, cache_t)


def route(peer, pieces):
    def body(peer_ref, in_ref, out_ref):
        for i in range(N_TP):
            out_ref[peer_ref[i]] = in_ref[i]

    return pl.pallas_call(
        body,
        grid_spec=pltpu.PrefetchScalarGridSpec(
            num_scalar_prefetch=1,
            grid=(1,),
            in_specs=[whole(pieces.shape)],
            out_specs=whole(pieces.shape),
        ),
        out_shape=jax.ShapeDtypeStruct(pieces.shape, bf16),
        compiler_params=params(),
        name="route",
    )(peer, pieces)


def attend(ids, lengths, cache_t, fresh_t, queries_t, heads, latent_width, arrived=None, done=None):
    rows, entries, length = cache_t.shape
    steps, _, _, all_heads = queries_t.shape
    parts = all_heads // heads
    again = arrived is not None

    def slot(r, ids):
        return ids[0] if again else r

    def body(ids_ref, lengths_ref, cache_ref, fresh_ref, q_ref, *refs):
        out_ref = refs[-1]
        current = lengths_ref[slot(pl.program_id(0), ids_ref)]
        if again:
            latents = jnp.concatenate([refs[0][j].astype(f32) for j in range(N_TP)], axis=0)
        else:
            latents = cache_ref[0].astype(f32)
        position = lax.broadcasted_iota(jnp.int32, (entries, length), 1)
        for s in range(steps):
            token = fresh_ref[0, :, s : s + 1].astype(f32)
            latents = jnp.where(position == current + s, token, latents)
        latents = latents.astype(bf16)
        place = lax.broadcasted_iota(jnp.int32, (all_heads, length), 1)
        outs = []
        for s in range(steps):
            scores = lax.dot_general(
                q_ref[s, 0], latents, (((0,), (0,)), ((), ())), preferred_element_type=f32
            )
            scores = jnp.where(place <= current + s, scores * QKD ** (-0.5), -jnp.inf)
            expo = jnp.exp(scores - jnp.max(scores, axis=-1, keepdims=True))
            probs = (expo / jnp.sum(expo, axis=-1, keepdims=True)).astype(bf16)
            out = lax.dot_general(
                probs, latents[:latent_width], (((1,), (1,)), ((), ())), preferred_element_type=f32
            )
            outs.append(out.reshape(parts, heads, latent_width))
        out_ref[:, 0] = jnp.concatenate(outs, axis=1).astype(bf16)

    extra_specs = [whole(arrived.shape), pl.BlockSpec(memory_space=pl.ANY)] if again else []
    extra = [arrived, done] if again else []
    return pl.pallas_call(
        body,
        grid_spec=pltpu.PrefetchScalarGridSpec(
            num_scalar_prefetch=2,
            grid=(1 if again else rows,),
            in_specs=[
                pl.BlockSpec((1, entries, length), lambda r, ids, _: (slot(r, ids), 0, 0)),
                pl.BlockSpec((1, entries, steps), lambda r, ids, _: (slot(r, ids), 0, 0)),
                pl.BlockSpec(
                    (steps, 1, entries, all_heads), lambda r, ids, _: (0, slot(r, ids), 0, 0)
                ),
            ]
            + extra_specs,
            out_specs=pl.BlockSpec(
                (parts, 1, steps * heads, latent_width),
                lambda r, ids, _: (0, slot(r, ids), 0, 0),
            ),
        ),
        out_shape=jax.ShapeDtypeStruct((parts, rows, steps * heads, latent_width), bf16),
        input_output_aliases={6: 0} if again else {},
        compiler_params=params(),
        name="again" if again else "attend",
    )(ids, lengths, cache_t, fresh_t, queries_t, *extra)


def project(ids, half, rows, weights, cuts, near=None):
    groups, _, count, depth = rows.shape
    width = weights[0].shape[1]
    blocks = len(weights)
    per = groups // cuts

    def body(ids_ref, rows_ref, *refs):
        out_ref = refs[-1]
        lhs = rows_ref[...].reshape(per * count, depth)
        for k in range(blocks):
            at = lax.rem(ids_ref[2] + k, blocks)
            total = jnp.dot(lhs, refs[k][...], preferred_element_type=f32)
            total = total.reshape(per, count, width)
            if near is not None:
                total = total + refs[blocks][:, at].astype(f32)
            out_ref[:, at] = total.astype(bf16)

    block = pl.BlockSpec((per, blocks, count, width), lambda i, ids: (i, 0, 0, 0))
    extra = [] if near is None else [near]
    return pl.pallas_call(
        body,
        grid_spec=pltpu.PrefetchScalarGridSpec(
            num_scalar_prefetch=1,
            grid=(cuts,),
            in_specs=[pl.BlockSpec((per, 1, count, depth), lambda i, ids: (i, half(ids), 0, 0))]
            + [whole(w.shape) for w in weights]
            + [block for _ in extra],
            out_specs=block,
        ),
        out_shape=jax.ShapeDtypeStruct((groups, blocks, count, width), bf16),
        compiler_params=params(),
        name="project",
    )(ids, rows, *weights, *extra)


def widen(ids, rows, kept, came, side, done=None):
    halves, chunks, _, count, features = rows.shape
    columns = kept.shape[1]
    every = halves * chunks * count
    starts = [0]
    for w in came:
        starts.append(starts[-1] + w.shape[0])

    def body(ids_ref, rows_ref, kept_ref, *refs):
        out_ref = refs[-1]
        pair = ids_ref[2]
        mine = rows_ref[:, :, pair].reshape(every, features)
        near = rows_ref[:, :, 1 - pair].reshape(every, features)

        def put(tile, value):
            value = value.astype(bf16).reshape(halves, chunks, count, value.shape[1])
            for h in range(halves):
                out_ref[:, 0, h, :, tile] = value[h]

        for at in range(0, columns, TILE):
            tile = slice(at, at + TILE)
            total = jnp.dot(mine, kept_ref[:, tile], preferred_element_type=f32)
            for k in range(len(came)):
                total += jnp.dot(
                    near[:, starts[k] : starts[k + 1]],
                    refs[k][:, tile],
                    preferred_element_type=f32,
                )
            put(tile, total)
        squares = jnp.zeros((every, 1), f32)
        for block in (mine, near):
            wide = block.astype(f32)
            squares += jnp.sum(wide * wide, axis=1, keepdims=True)
        high = squares.astype(bf16).astype(f32)
        lane = lax.broadcasted_iota(jnp.int32, (every, 128), 1)
        extra = jnp.where(lane == 0, high, jnp.where(lane == 1, squares - high, 0.0))
        put(slice(columns, columns + 128), extra)

    last = [] if done is None else [done]
    return pl.pallas_call(
        body,
        grid_spec=pltpu.PrefetchScalarGridSpec(
            num_scalar_prefetch=1,
            grid=(1,),
            in_specs=[whole(rows.shape)]
            + [whole(w.shape) for w in (kept,) + came]
            + [pl.BlockSpec(memory_space=pl.ANY) for _ in last],
            out_specs=pl.BlockSpec(
                (chunks, 1, halves, count, columns + 128), lambda i, ids: (0, side, 0, 0, 0)
            ),
        ),
        out_shape=jax.ShapeDtypeStruct((chunks, 2, halves, count, columns + 128), bf16),
        input_output_aliases={3 + len(came): 0} if last else {},
        compiler_params=params(),
        name="widen",
    )(ids, rows, kept, *came, *last)


def local(
    cache,
    cache_length,
    move_slot,
    move_peer,
    queries,
    new_latent,
    value_up,
    out_proj,
    residual,
    norm_gain,
    gate_weight,
    up_weight,
    down_weight,
):
    member = lax.axis_index(TP)
    core = lax.axis_index("c")
    pair = lax.axis_index("xl")
    steps = new_latent.shape[0]
    heads, latent_width, value_width = value_up.shape
    rows_out = residual.shape[1] // N_TP
    chunk = rows_out * steps
    count = chunk // 2
    units = gate_weight.shape[1]

    def by_pair(mine, other):
        first = pair == 0
        return jnp.stack([jnp.where(first, mine, other), jnp.where(first, other, mine)])

    def at_pair(blocks):
        return lax.dynamic_index_in_dim(blocks, pair, 0, False)

    def at_other(blocks):
        return lax.dynamic_index_in_dim(blocks, 1 - pair, 0, False)

    out_came = swap(out_proj, "xl")
    lanes = jnp.arange(N_TP, dtype=jnp.int32)
    own_slot = jnp.sum(jnp.where(lanes == member, move_slot[0], 0))
    ids = jnp.stack([own_slot, core, pair]).astype(jnp.int32)
    cache_t = cache.transpose(0, 2, 1)
    pieces = exchange(leave(ids, cache_t), TP)
    pieces, gate_weight, up_weight = lax.optimization_barrier((pieces, gate_weight, up_weight))

    gain = norm_gain.astype(f32)[:, None]

    def scaled(low, high, first, second):
        weight = jnp.where(pair == 0, first[low:high], second[low:high])
        return (weight.astype(f32) * gain[low:high]).astype(bf16)

    sent = [
        scaled(low, high, up_weight, gate_weight) for low, high in zip(CUTS[:-1], CUTS[1:])
    ]
    kept = scaled(0, CUTS[-1], gate_weight, up_weight)
    came = [swap(sent[0], "xl")]

    arrived = exchange(route(move_peer[0], pieces), TP)
    fresh_t = new_latent.transpose(1, 2, 0)
    queries_t = queries.transpose(0, 1, 3, 2)
    out = attend(ids, cache_length, cache_t, fresh_t, queries_t, heads, latent_width)
    out = attend(
        ids, cache_length, cache_t, fresh_t, queries_t, heads, latent_width, arrived, out
    )
    out, out_came = lax.optimization_barrier((out, out_came))
    by_head = exchange(out, TP).reshape(-1, heads, latent_width)
    by_head, kept, came[0] = lax.optimization_barrier((by_head, kept, came[0]))
    value_heads = jnp.einsum(
        "thl,hlv->thv", by_head, value_up, preferred_element_type=f32
    ).astype(bf16)

    value_heads = value_heads.reshape(2, 2, count, heads * value_width).transpose(1, 0, 2, 3)
    value_heads = jnp.broadcast_to(
        value_heads[None, :, None], (2, 2, 2) + value_heads.shape[1:]
    ).reshape((N_DP,) + value_heads.shape[1:])
    gathered = exchange(value_heads, DP)
    gathered, sent[1] = lax.optimization_barrier((gathered, sent[1]))
    came.append(swap(sent[1], "xl"))
    weights = [out_proj, out_came]
    away = swap(project(ids, lambda i: 1 - i[1], gathered, weights, 1), "c")
    total = project(ids, lambda i: i[1], gathered, weights, 1, away)
    parts = exchange(total, ZY)
    parts, came[1] = lax.optimization_barrier((parts, came[1]))
    residue = lax.dynamic_slice_in_dim(residual, member * rows_out, rows_out, 1)
    residue = residue.transpose(1, 0, 2).reshape(2, count, -1)
    residue = by_pair(at_pair(residue), swap(at_other(residue), "xl"))
    hidden = residue.astype(f32) + jnp.sum(parts.astype(f32), axis=0)

    own = spread(hidden.astype(bf16), PAIR, 2 * N_ZY).reshape((2, N_ZY) + hidden.shape)
    other = swap(own, "c")
    came = tuple(came)
    wide = widen(ids, own, kept, came, 0)
    wide = widen(ids, other, kept, came, 1, wide)
    sums = exchange(wide.reshape(N_DP, 2 * chunk, -1), DP)
    sums = jnp.sum(sums.reshape(2, 2, 2, 2 * chunk, -1).astype(f32), axis=(0, 2))
    squares = sums[0, :, units] + sums[0, :, units + 1]
    inverse = lax.rsqrt(squares / D + norm_eps)[:, None]
    active = jax.nn.silu(sums[0, :, :units] * inverse) * (sums[1, :, :units] * inverse)
    active = spread(active.astype(bf16), DP, N_DP).reshape(N_DP, 2, chunk, units)

    away = swap(project(ids, lambda i: 1, active, [down_weight], 2), "c")
    total = project(ids, lambda i: 0, active, [down_weight], 2, away)
    parts = exchange(total.reshape(N_ZY, chunk, -1), ZY)
    hidden = by_pair(at_pair(hidden), swap(at_other(hidden), "xl")).reshape(chunk, -1)
    result = (hidden + jnp.sum(parts.astype(f32), axis=0)).astype(bf16)
    return result.reshape(rows_out, steps, -1).transpose(1, 0, 2)


def solution(mesh):
    split = Mesh(
        mesh.devices.reshape(2, 2, 2, 2, 4, 2), ("xh", "xl", "zl", "zh", "y", "c")
    )
    in_specs = (
        P(DP + TP, None, None),
        P(DP + TP),
        P(DP, None),
        P(DP, None),
        P(None, DP + TP, None, None),
        P(None, DP + TP, None),
        P(TP, None, None),
        P(TP, DP),
        P(None, None, DP),
        P(DP),
        P(DP, TP),
        P(DP, TP),
        P(TP, DP),
    )
    out_specs = P(None, TP, DP)
    return jax.shard_map(local, mesh=split, in_specs=in_specs, out_specs=out_specs, check_vma=False)
```

```python
import jax
import jax.numpy as jnp
from jax import lax
from jax.experimental import pallas as pl
from jax.experimental.pallas import tpu as pltpu
from jax.sharding import Mesh, PartitionSpec as P

D = 7168
QKD = 192
norm_eps = 1e-06

DP = ("xh", "xl", "zl")
TP = ("zh", "y", "c")
ZY = ("zh", "y")
PAIR = ("xl",) + ZY
N_DP = 8
N_TP = 16
N_ZY = 8
SWAP = [(0, 1), (1, 0)]
CUTS = (0, 256, 896)
TILE = 384
bf16 = jnp.bfloat16
f32 = jnp.float32
VMEM = 60 * 1024 * 1024


def exchange(blocks, axes):
    return lax.all_to_all(blocks, axes, 0, 0, tiled=True)


def spread(block, axes, copies):
    return exchange(jnp.broadcast_to(block[None], (copies,) + block.shape), axes)


def swap(block, axis):
    return lax.ppermute(block, axis, SWAP)


def params():
    return pltpu.CompilerParams(vmem_limit_bytes=VMEM)


def whole(shape):
    return pl.BlockSpec(shape, lambda *_: (0,) * len(shape))


def leave(ids, cache_t):
    _, entries, length = cache_t.shape
    piece = entries // N_TP

    def body(ids_ref, row_ref, out_ref):
        row = row_ref[0].astype(f32)
        for j in range(N_TP):
            out_ref[j] = row[j * piece : (j + 1) * piece].astype(bf16)

    return pl.pallas_call(
        body,
        grid_spec=pltpu.PrefetchScalarGridSpec(
            num_scalar_prefetch=1,
            grid=(1,),
            in_specs=[pl.BlockSpec((1, entries, length), lambda i, ids: (ids[0], 0, 0))],
            out_specs=whole((N_TP, piece, length)),
        ),
        out_shape=jax.ShapeDtypeStruct((N_TP, piece, length), bf16),
        compiler_params=params(),
        name="leave",
    )(ids, cache_t)


def route(peer, pieces):
    def body(peer_ref, in_ref, out_ref):
        for i in range(N_TP):
            out_ref[peer_ref[i]] = in_ref[i]

    return pl.pallas_call(
        body,
        grid_spec=pltpu.PrefetchScalarGridSpec(
            num_scalar_prefetch=1,
            grid=(1,),
            in_specs=[whole(pieces.shape)],
            out_specs=whole(pieces.shape),
        ),
        out_shape=jax.ShapeDtypeStruct(pieces.shape, bf16),
        compiler_params=params(),
        name="route",
    )(peer, pieces)


def attend(ids, lengths, cache_t, fresh_t, queries_t, heads, latent_width, arrived=None, done=None):
    rows, entries, length = cache_t.shape
    steps, _, _, all_heads = queries_t.shape
    chips = all_heads // (2 * heads)
    again = arrived is not None

    def slot(r, ids):
        return ids[0] if again else r

    def body(ids_ref, lengths_ref, cache_ref, fresh_ref, q_ref, *refs):
        out_ref = refs[-1]
        row = slot(pl.program_id(0), ids_ref)
        current = lengths_ref[row]
        if again:
            latents = jnp.concatenate([refs[0][j].astype(f32) for j in range(N_TP)], axis=0)
        else:
            latents = cache_ref[0].astype(f32)
        position = lax.broadcasted_iota(jnp.int32, (entries, length), 1)
        for s in range(steps):
            token = fresh_ref[0, :, s : s + 1].astype(f32)
            latents = jnp.where(position == current + s, token, latents)
        latents = latents.astype(bf16)
        place = lax.broadcasted_iota(jnp.int32, (all_heads, length), 1)
        outs = []
        for s in range(steps):
            scores = lax.dot_general(
                q_ref[s, 0], latents, (((0,), (0,)), ((), ())), preferred_element_type=f32
            )
            scores = jnp.where(place <= current + s, scores * QKD ** (-0.5), -jnp.inf)
            expo = jnp.exp(scores - jnp.max(scores, axis=-1, keepdims=True))
            probs = (expo / jnp.sum(expo, axis=-1, keepdims=True)).astype(bf16)
            out = lax.dot_general(
                probs, latents[:latent_width], (((1,), (1,)), ((), ())), preferred_element_type=f32
            )
            out = out.reshape(chips, 2, heads, latent_width)
            turned = jnp.concatenate([out[:, 1:], out[:, :1]], axis=1)
            out = jnp.where(row >= rows // 2, turned, out)
            outs.append(out.reshape(chips, 2 * heads, latent_width))
        out_ref[:, 0, 0] = jnp.concatenate(outs, axis=1).astype(bf16)

    extra_specs = [whole(arrived.shape), pl.BlockSpec(memory_space=pl.ANY)] if again else []
    extra = [arrived, done] if again else []
    return pl.pallas_call(
        body,
        grid_spec=pltpu.PrefetchScalarGridSpec(
            num_scalar_prefetch=2,
            grid=(1 if again else rows,),
            in_specs=[
                pl.BlockSpec((1, entries, length), lambda r, ids, _: (slot(r, ids), 0, 0)),
                pl.BlockSpec((1, entries, steps), lambda r, ids, _: (slot(r, ids), 0, 0)),
                pl.BlockSpec(
                    (steps, 1, entries, all_heads), lambda r, ids, _: (0, slot(r, ids), 0, 0)
                ),
            ]
            + extra_specs,
            out_specs=pl.BlockSpec(
                (chips, 1, 1, 2 * steps * heads, latent_width),
                lambda r, ids, _: (
                    0,
                    lax.div(slot(r, ids), rows // 2),
                    lax.rem(slot(r, ids), rows // 2),
                    0,
                    0,
                ),
            ),
        ),
        out_shape=jax.ShapeDtypeStruct(
            (chips, 2, rows // 2, 2 * steps * heads, latent_width), bf16
        ),
        input_output_aliases={6: 0} if again else {},
        compiler_params=params(),
        name="again" if again else "attend",
    )(ids, lengths, cache_t, fresh_t, queries_t, *extra)


def project(ids, rows, weights, cuts):
    groups, count, depth = rows.shape
    width = weights[0][0].shape[1]
    blocks = len(weights)
    per = groups // cuts
    flat = [w for weight in weights for w in weight]

    def body(ids_ref, rows_ref, *refs):
        out_ref = refs[-1]
        lhs = rows_ref[...].reshape(per * count, depth)
        n = 0
        for k in range(blocks):
            total, start = 0.0, 0
            for w in weights[k]:
                stop = start + w.shape[0]
                total += jnp.dot(lhs[:, start:stop], refs[n][...], preferred_element_type=f32)
                n, start = n + 1, stop
            at = lax.rem(ids_ref[1] + k, blocks)
            out_ref[:, at] = total.astype(bf16).reshape(per, count, width)

    return pl.pallas_call(
        body,
        grid_spec=pltpu.PrefetchScalarGridSpec(
            num_scalar_prefetch=1,
            grid=(cuts,),
            in_specs=[pl.BlockSpec((per, count, depth), lambda i, ids: (i, 0, 0))]
            + [whole(w.shape) for w in flat],
            out_specs=pl.BlockSpec((per, blocks, count, width), lambda i, ids: (i, 0, 0, 0)),
        ),
        out_shape=jax.ShapeDtypeStruct((groups, blocks, count, width), bf16),
        compiler_params=params(),
        name="project",
    )(ids, rows, *flat)


def widen(ids, rows, kept, came):
    halves, chunks, _, count, features = rows.shape
    width = kept[0].shape[1]
    columns = width * len(kept)
    every = halves * chunks * count
    weights = [w for own, rest in zip(kept, came) for w in [own] + rest]

    def body(ids_ref, rows_ref, *refs):
        out_ref = refs[-1]
        pair = ids_ref[1]
        mine = rows_ref[:, :, pair].reshape(every, features)
        near = rows_ref[:, :, 1 - pair].reshape(every, features)

        def put(tile, value):
            value = value.astype(bf16).reshape(halves, chunks, count, value.shape[1])
            for h in range(halves):
                out_ref[:, h, :, tile] = value[h]

        n = 0
        for k in range(len(kept)):
            for at in range(0, width, TILE):
                tile = slice(at, at + TILE)
                total = jnp.dot(mine, refs[n][:, tile], preferred_element_type=f32)
                start = 0
                for m, w in enumerate(came[k]):
                    stop = start + w.shape[0]
                    total += jnp.dot(
                        near[:, start:stop], refs[n + 1 + m][:, tile], preferred_element_type=f32
                    )
                    start = stop
                put(slice(k * width + at, k * width + at + TILE), total)
            n += 1 + len(came[k])
        squares = jnp.zeros((every, 1), f32)
        for block in (mine, near):
            wide = block.astype(f32)
            squares += jnp.sum(wide * wide, axis=1, keepdims=True)
        high = squares.astype(bf16).astype(f32)
        lane = lax.broadcasted_iota(jnp.int32, (every, 128), 1)
        extra = jnp.where(lane == 0, high, jnp.where(lane == 1, squares - high, 0.0))
        put(slice(columns, columns + 128), extra)

    return pl.pallas_call(
        body,
        grid_spec=pltpu.PrefetchScalarGridSpec(
            num_scalar_prefetch=1,
            grid=(1,),
            in_specs=[whole(rows.shape)] + [whole(w.shape) for w in weights],
            out_specs=whole((chunks, halves, count, columns + 128)),
        ),
        out_shape=jax.ShapeDtypeStruct((chunks, halves, count, columns + 128), bf16),
        compiler_params=params(),
        name="widen",
    )(ids, rows, *weights)


def local(
    cache,
    cache_length,
    move_slot,
    move_peer,
    queries,
    new_latent,
    value_up,
    out_proj,
    residual,
    norm_gain,
    gate_weight,
    up_weight,
    down_weight,
):
    member = lax.axis_index(TP)
    core = lax.axis_index("c")
    pair = lax.axis_index("xl")
    steps = new_latent.shape[0]
    heads, latent_width, value_width = value_up.shape
    rows_out = residual.shape[1] // N_TP
    chunk = rows_out * steps
    count = chunk // 2
    features, units = gate_weight.shape

    def by_pair(mine, other):
        first = pair == 0
        return jnp.stack([jnp.where(first, mine, other), jnp.where(first, other, mine)])

    def at_pair(blocks):
        return lax.dynamic_index_in_dim(blocks, pair, 0, False)

    def at_other(blocks):
        return lax.dynamic_index_in_dim(blocks, 1 - pair, 0, False)

    out_came = swap(out_proj, "xl")
    value_ups = jnp.concatenate([value_up, swap(value_up, "c")], axis=0)
    downs = [down_weight, swap(down_weight, "c")]
    lanes = jnp.arange(N_TP, dtype=jnp.int32)
    own_slot = jnp.sum(jnp.where(lanes == member, move_slot[0], 0))
    ids = jnp.stack([own_slot, pair]).astype(jnp.int32)
    cache_t = cache.transpose(0, 2, 1)
    pieces = exchange(leave(ids, cache_t), TP)
    pieces, gate_weight, up_weight = lax.optimization_barrier((pieces, gate_weight, up_weight))

    gain = norm_gain.astype(f32)[:, None]

    def scaled(low, high, first, second):
        weight = jnp.where(pair == 0, first[low:high], second[low:high])
        return (weight.astype(f32) * gain[low:high]).astype(bf16)

    sent = [
        scaled(low, high, up_weight, gate_weight) for low, high in zip(CUTS[:-1], CUTS[1:])
    ]
    kept = scaled(0, CUTS[-1], gate_weight, up_weight)
    arrived = exchange(route(move_peer[0], pieces), TP)
    fresh_t = new_latent.transpose(1, 2, 0)
    queries_t = queries.transpose(0, 1, 3, 2)
    out = attend(ids, cache_length, cache_t, fresh_t, queries_t, heads, latent_width)
    out = attend(
        ids, cache_length, cache_t, fresh_t, queries_t, heads, latent_width, arrived, out
    )
    out, out_came, sent[0] = lax.optimization_barrier((out, out_came, sent[0]))
    came = [swap(sent[0], "xl")]
    out_weights = [[w, swap(w, "c")] for w in (out_proj, out_came)]
    kept = [kept, swap(kept, "c")]
    out = out.reshape((N_TP,) + out.shape[2:])
    by_head = exchange(out, TP).reshape(-1, 2 * heads, latent_width)
    by_head, kept, came, out_weights, value_ups = lax.optimization_barrier(
        (by_head, kept, came, out_weights, value_ups)
    )
    value_heads = jnp.einsum(
        "thl,hlv->thv", by_head, value_ups, preferred_element_type=f32
    ).astype(bf16)

    value_heads = value_heads.reshape(2, 2, count // 2, 2 * heads * value_width)
    value_heads = value_heads.transpose(1, 0, 2, 3).reshape(2, count, -1)
    value_heads = jnp.broadcast_to(
        value_heads[None, :, None], (2, 2, 2) + value_heads.shape[1:]
    ).reshape((N_DP,) + value_heads.shape[1:])
    gathered = exchange(value_heads, DP)
    gathered, sent[1] = lax.optimization_barrier((gathered, sent[1]))
    came.append(swap(sent[1], "xl"))
    parts = exchange(project(ids, gathered, out_weights, 1), ZY)
    parts, came[1] = lax.optimization_barrier((parts, came[1]))
    came = [came, [swap(w, "c") for w in came]]
    residue = lax.dynamic_slice_in_dim(residual, lax.div(member, 2) * 2 * rows_out, 2 * rows_out, 1)
    residue = residue.reshape(steps, 2, 2, rows_out // 8, 2, 2, features)
    residue = lax.dynamic_index_in_dim(residue, core, 4, False)
    residue = residue.transpose(2, 1, 3, 4, 0, 5).reshape(2, count, features)
    residue = by_pair(at_pair(residue), swap(at_other(residue), "xl"))
    hidden = residue.astype(f32) + jnp.sum(parts.astype(f32), axis=0)

    rows = spread(hidden.astype(bf16), PAIR, 2 * N_ZY).reshape((2, N_ZY) + hidden.shape)
    sums = exchange(widen(ids, rows, kept, came).reshape(N_DP, chunk, -1), DP)
    sums = jnp.sum(sums.reshape(2, 2, 2, chunk, -1).astype(f32), axis=(0, 2))
    squares = sums[0, :, 2 * units] + sums[0, :, 2 * units + 1]
    inverse = lax.rsqrt(squares / D + norm_eps)[:, None]
    active = sums[:, :, : 2 * units] * inverse
    active = (jax.nn.silu(active[0]) * active[1]).astype(bf16)
    parts = exchange(project(ids, spread(active, DP, N_DP), [downs], 2)[:, 0], ZY)
    hidden = by_pair(at_pair(hidden), swap(at_other(hidden), "xl")).reshape(chunk, -1)
    result = (hidden + jnp.sum(parts.astype(f32), axis=0)).astype(bf16)

    result = result.reshape(2, 2, rows_out // 8, 2, steps, features)
    mine = lax.dynamic_index_in_dim(result, core, 1, False)
    near = swap(lax.dynamic_index_in_dim(result, 1 - core, 1, False), "c")
    first = core == 0
    result = jnp.stack([jnp.where(first, mine, near), jnp.where(first, near, mine)])
    return result.transpose(4, 1, 2, 0, 3, 5).reshape(steps, rows_out, features)


def solution(mesh):
    split = Mesh(
        mesh.devices.reshape(2, 2, 2, 2, 4, 2), ("xh", "xl", "zl", "zh", "y", "c")
    )
    in_specs = (
        P(DP + TP, None, None),
        P(DP + TP),
        P(DP, None),
        P(DP, None),
        P(None, DP + TP, None, None),
        P(None, DP + TP, None),
        P(TP, None, None),
        P(TP, DP),
        P(None, None, DP),
        P(DP),
        P(DP, TP),
        P(DP, TP),
        P(TP, DP),
    )
    out_specs = P(None, TP, DP)
    return jax.shard_map(local, mesh=split, in_specs=in_specs, out_specs=out_specs, check_vma=False)
```

```python
import jax
import jax.numpy as jnp
from jax import lax
from jax.experimental import pallas as pl
from jax.experimental.pallas import tpu as pltpu
from jax.sharding import Mesh, PartitionSpec as P

D = 7168
QKD = 192
norm_eps = 1e-06

DP = ("xh", "xl", "zl")
TP = ("zh", "y", "c")
ZY = ("zh", "y")
PAIR = ("xl",) + ZY
N_DP = 8
N_TP = 16
N_ZY = 8
SWAP = [(0, 1), (1, 0)]
CUTS = (0, 384, 896)
TILE = 768
bf16 = jnp.bfloat16
f32 = jnp.float32
MIB = 1024 * 1024


def exchange(blocks, axes):
    return lax.all_to_all(blocks, axes, 0, 0, tiled=True)


def spread(block, axes, copies):
    return exchange(jnp.broadcast_to(block[None], (copies,) + block.shape), axes)


def swap(block, axis):
    return lax.ppermute(block, axis, SWAP)


def params(mib):
    return pltpu.CompilerParams(vmem_limit_bytes=mib * MIB)


def whole(shape):
    return pl.BlockSpec(shape, lambda *_: (0,) * len(shape))


def leave(slots, cache_t):
    _, entries, length = cache_t.shape
    piece = entries // N_TP

    def body(slots_ref, cache_ref, out_ref, row_ref, sem):
        slot = slots_ref[lax.axis_index(TP)]
        copy = pltpu.make_async_copy(cache_ref.at[slot], row_ref, sem)
        copy.start()
        copy.wait()
        row = row_ref[...].astype(f32)
        for j in range(N_TP):
            out_ref[j] = row[j * piece : (j + 1) * piece].astype(bf16)

    return pl.pallas_call(
        body,
        grid_spec=pltpu.PrefetchScalarGridSpec(
            num_scalar_prefetch=1,
            grid=(1,),
            in_specs=[pl.BlockSpec(memory_space=pl.ANY)],
            out_specs=whole((N_TP, piece, length)),
            scratch_shapes=[pltpu.VMEM((entries, length), bf16), pltpu.SemaphoreType.DMA],
        ),
        out_shape=jax.ShapeDtypeStruct((N_TP, piece, length), bf16),
        compiler_params=params(60),
        name="leave",
    )(slots, cache_t)


def route(peer, pieces):
    def body(peer_ref, in_ref, out_ref):
        for i in range(N_TP):
            out_ref[peer_ref[i]] = in_ref[i]

    return pl.pallas_call(
        body,
        grid_spec=pltpu.PrefetchScalarGridSpec(
            num_scalar_prefetch=1,
            grid=(1,),
            in_specs=[whole(pieces.shape)],
            out_specs=whole(pieces.shape),
        ),
        out_shape=jax.ShapeDtypeStruct(pieces.shape, bf16),
        compiler_params=params(40),
        name="route",
    )(peer, pieces)


def attend(ids, lengths, cache_t, fresh_t, queries_t, heads, latent_width, arrived=None, done=None):
    rows, entries, length = cache_t.shape
    steps, _, _, all_heads = queries_t.shape
    chips = all_heads // (2 * heads)
    again = arrived is not None

    def slot(r, ids):
        return ids[0] if again else r

    def body(ids_ref, lengths_ref, fresh_ref, q_ref, *refs):
        out_ref = refs[-1]
        row = slot(pl.program_id(0), ids_ref)
        current = lengths_ref[row]
        if again:
            latents = jnp.concatenate([refs[0][j].astype(f32) for j in range(N_TP)], axis=0)
        else:
            latents = refs[0][0].astype(f32)
        position = lax.broadcasted_iota(jnp.int32, (entries, length), 1)
        for s in range(steps):
            token = fresh_ref[0, :, s : s + 1].astype(f32)
            latents = jnp.where(position == current + s, token, latents)
        latents = latents.astype(bf16)
        place = lax.broadcasted_iota(jnp.int32, (all_heads, length), 1)
        outs = []
        for s in range(steps):
            scores = lax.dot_general(
                q_ref[s, 0], latents, (((0,), (0,)), ((), ())), preferred_element_type=f32
            )
            scores = jnp.where(place <= current + s, scores * QKD ** (-0.5), -jnp.inf)
            expo = jnp.exp(scores - jnp.max(scores, axis=-1, keepdims=True))
            probs = (expo / jnp.sum(expo, axis=-1, keepdims=True)).astype(bf16)
            out = lax.dot_general(
                probs, latents[:latent_width], (((1,), (1,)), ((), ())), preferred_element_type=f32
            )
            out = out.reshape(chips, 2, heads, latent_width)
            turned = jnp.concatenate([out[:, 1:], out[:, :1]], axis=1)
            out = jnp.where(row >= rows // 2, turned, out)
            outs.append(out.reshape(chips, 2 * heads, latent_width))
        out_ref[:, 0, 0] = jnp.concatenate(outs, axis=1).astype(bf16)

    if again:
        extra_specs = [whole(arrived.shape), pl.BlockSpec(memory_space=pl.ANY)]
        extra = [arrived, done]
    else:
        extra_specs = [pl.BlockSpec((1, entries, length), lambda r, *_: (r, 0, 0))]
        extra = [cache_t]
    return pl.pallas_call(
        body,
        grid_spec=pltpu.PrefetchScalarGridSpec(
            num_scalar_prefetch=2,
            grid=(1 if again else rows,),
            in_specs=[
                pl.BlockSpec((1, entries, steps), lambda r, ids, _: (slot(r, ids), 0, 0)),
                pl.BlockSpec(
                    (steps, 1, entries, all_heads), lambda r, ids, _: (0, slot(r, ids), 0, 0)
                ),
            ]
            + extra_specs,
            out_specs=pl.BlockSpec(
                (chips, 1, 1, 2 * steps * heads, latent_width),
                lambda r, ids, _: (
                    0,
                    lax.div(slot(r, ids), rows // 2),
                    lax.rem(slot(r, ids), rows // 2),
                    0,
                    0,
                ),
            ),
        ),
        out_shape=jax.ShapeDtypeStruct(
            (chips, 2, rows // 2, 2 * steps * heads, latent_width), bf16
        ),
        input_output_aliases={5: 0} if again else {},
        compiler_params=params(60),
        name="again" if again else "attend",
    )(ids, lengths, fresh_t, queries_t, *extra)


def project(ids, rows, weight, blocks):
    groups, count, depth = rows.shape
    width = weight.shape[1] // blocks

    def body(ids_ref, rows_ref, weight_ref, out_ref):
        lhs = rows_ref[...].reshape(groups * count, depth)
        total = jnp.dot(lhs, weight_ref[...], preferred_element_type=f32)
        out_ref[:, 0] = total.astype(bf16).reshape(groups, count, width)

    return pl.pallas_call(
        body,
        grid_spec=pltpu.PrefetchScalarGridSpec(
            num_scalar_prefetch=1,
            grid=(blocks,),
            in_specs=[
                whole(rows.shape),
                pl.BlockSpec((depth, width), lambda k, ids: (0, k)),
            ],
            out_specs=pl.BlockSpec(
                (groups, 1, count, width), lambda k, ids: (0, lax.rem(ids[1] + k, blocks), 0, 0)
            ),
        ),
        out_shape=jax.ShapeDtypeStruct((groups, blocks, count, width), bf16),
        compiler_params=params(40),
        name="project",
    )(ids, rows, weight)


def widen(ids, rows, weight):
    halves, chunks, blocks, count, features = rows.shape
    depth, columns = weight.shape
    every = halves * chunks * count

    def body(ids_ref, rows_ref, weight_ref, out_ref, lhs_ref):
        tile = pl.program_id(0)

        def put(at, value):
            value = value.astype(bf16).reshape(halves, chunks, count, value.shape[1])
            for h in range(halves):
                out_ref[:, h, :, at] = value[h]

        @pl.when(tile == 0)
        def _():
            squares = jnp.zeros((every, 1), f32)
            for k in range(blocks):
                block = rows_ref[:, :, lax.rem(ids_ref[1] + k, blocks)].reshape(every, features)
                lhs_ref[:, k * features : (k + 1) * features] = block
                wide = block.astype(f32)
                squares += jnp.sum(wide * wide, axis=1, keepdims=True)
            high = squares.astype(bf16).astype(f32)
            lane = lax.broadcasted_iota(jnp.int32, (every, 128), 1)
            extra = jnp.where(lane == 0, high, jnp.where(lane == 1, squares - high, 0.0))
            put(slice(columns, columns + 128), extra)

        total = jnp.dot(lhs_ref[...], weight_ref[...], preferred_element_type=f32)
        put(pl.ds(pl.multiple_of(tile * TILE, 128), TILE), total)

    return pl.pallas_call(
        body,
        grid_spec=pltpu.PrefetchScalarGridSpec(
            num_scalar_prefetch=1,
            grid=(columns // TILE,),
            in_specs=[
                whole(rows.shape),
                pl.BlockSpec((depth, TILE), lambda k, ids: (0, k)),
            ],
            out_specs=whole((chunks, halves, count, columns + 128)),
            scratch_shapes=[pltpu.VMEM((every, depth), bf16)],
        ),
        out_shape=jax.ShapeDtypeStruct((chunks, halves, count, columns + 128), bf16),
        compiler_params=params(40),
        name="widen",
    )(ids, rows, weight)


def local(
    cache,
    cache_length,
    move_slot,
    move_peer,
    queries,
    new_latent,
    value_up,
    out_proj,
    residual,
    norm_gain,
    gate_weight,
    up_weight,
    down_weight,
):
    member = lax.axis_index(TP)
    core = lax.axis_index("c")
    pair = lax.axis_index("xl")
    steps = new_latent.shape[0]
    heads, latent_width, value_width = value_up.shape
    rows_out = residual.shape[1] // N_TP
    chunk = rows_out * steps
    count = chunk // 2
    features, units = gate_weight.shape

    def by_pair(mine, other):
        first = pair == 0
        return jnp.stack([jnp.where(first, mine, other), jnp.where(first, other, mine)])

    def at_pair(blocks):
        return lax.dynamic_index_in_dim(blocks, pair, 0, False)

    def at_other(blocks):
        return lax.dynamic_index_in_dim(blocks, 1 - pair, 0, False)

    out_came = swap(out_proj, "xl")
    value_ups = jnp.concatenate([value_up, swap(value_up, "c")], axis=0)
    downs = jnp.concatenate([down_weight, swap(down_weight, "c")], axis=0)
    residue = lax.dynamic_slice_in_dim(residual, lax.div(member, 2) * 2 * rows_out, 2 * rows_out, 1)
    residue = residue.reshape(steps, 2, 2, rows_out // 8, 2, 2, features)
    residue = lax.dynamic_index_in_dim(residue, core, 4, False)
    residue = residue.transpose(2, 1, 3, 4, 0, 5).reshape(2, count, features)
    residue_came = swap(at_other(residue), "xl")
    lanes = jnp.arange(N_TP, dtype=jnp.int32)
    own_slot = jnp.sum(jnp.where(lanes == member, move_slot[0], 0))
    ids = jnp.stack([own_slot, pair]).astype(jnp.int32)
    cache_t = cache.transpose(0, 2, 1)
    pieces = exchange(leave(move_slot[0], cache_t), TP)
    pieces, gate_weight, up_weight = lax.optimization_barrier((pieces, gate_weight, up_weight))

    gain = norm_gain.astype(f32)[:, None]

    def scaled(low, high, first, second):
        weight = jnp.where(pair == 0, first[low:high], second[low:high])
        return (weight.astype(f32) * gain[low:high]).astype(bf16)

    sent = [
        scaled(low, high, up_weight, gate_weight) for low, high in zip(CUTS[:-1], CUTS[1:])
    ]
    kept = scaled(0, CUTS[-1], gate_weight, up_weight)
    arrived = exchange(route(move_peer[0], pieces), TP)
    fresh_t = new_latent.transpose(1, 2, 0)
    queries_t = queries.transpose(0, 1, 3, 2)
    out = attend(ids, cache_length, cache_t, fresh_t, queries_t, heads, latent_width)
    out = attend(
        ids, cache_length, cache_t, fresh_t, queries_t, heads, latent_width, arrived, out
    )
    out, out_came, sent[0] = lax.optimization_barrier((out, out_came, sent[0]))
    came = [swap(sent[0], "xl")]
    out_weights = jnp.concatenate(
        [jnp.concatenate([w, swap(w, "c")], axis=0) for w in (out_proj, out_came)], axis=1
    )
    kept = [kept, swap(kept, "c")]
    out = out.reshape((N_TP,) + out.shape[2:])
    by_head = exchange(out, TP).reshape(-1, 2 * heads, latent_width)
    by_head, kept, came, out_weights, value_ups, residue_came, downs = lax.optimization_barrier(
        (by_head, kept, came, out_weights, value_ups, residue_came, downs)
    )
    value_heads = jnp.einsum(
        "thl,hlv->thv", by_head, value_ups, preferred_element_type=f32
    ).astype(bf16)

    value_heads = value_heads.reshape(2, 2, count // 2, 2 * heads * value_width)
    value_heads = value_heads.transpose(1, 0, 2, 3).reshape(2, count, -1)
    value_heads = jnp.broadcast_to(
        value_heads[None, :, None], (2, 2, 2) + value_heads.shape[1:]
    ).reshape((N_DP,) + value_heads.shape[1:])
    gathered = exchange(value_heads, DP)
    gathered, sent[1] = lax.optimization_barrier((gathered, sent[1]))
    came.append(swap(sent[1], "xl"))
    parts = exchange(project(ids, gathered, out_weights, 2), ZY)
    parts, came[1] = lax.optimization_barrier((parts, came[1]))
    in_weight = jnp.concatenate(
        [
            jnp.concatenate([own, swap(own, "c") if k else kept[1]], axis=1)
            for k, own in enumerate([kept[0]] + came)
        ],
        axis=0,
    )
    residue = by_pair(at_pair(residue), residue_came)
    hidden = residue.astype(f32) + jnp.sum(parts.astype(f32), axis=0)

    rows = spread(hidden.astype(bf16), PAIR, 2 * N_ZY).reshape((2, N_ZY) + hidden.shape)
    rows, in_weight = lax.optimization_barrier((rows, in_weight))
    sums = exchange(widen(ids, rows, in_weight).reshape(N_DP, chunk, -1), DP)
    sums = jnp.sum(sums.reshape(2, 2, 2, chunk, -1).astype(f32), axis=(0, 2))
    squares = sums[0, :, 2 * units] + sums[0, :, 2 * units + 1]
    inverse = lax.rsqrt(squares / D + norm_eps)[:, None]
    active = sums[:, :, : 2 * units] * inverse
    active = (jax.nn.silu(active[0]) * active[1]).astype(bf16)
    parts = exchange(project(ids, spread(active, DP, N_DP), downs, 1)[:, 0], ZY)
    hidden = by_pair(at_pair(hidden), swap(at_other(hidden), "xl")).reshape(chunk, -1)
    result = (hidden + jnp.sum(parts.astype(f32), axis=0)).astype(bf16)

    result = result.reshape(2, 2, rows_out // 8, 2, steps, features)
    mine = lax.dynamic_index_in_dim(result, core, 1, False)
    near = swap(lax.dynamic_index_in_dim(result, 1 - core, 1, False), "c")
    first = core == 0
    result = jnp.stack([jnp.where(first, mine, near), jnp.where(first, near, mine)])
    return result.transpose(4, 1, 2, 0, 3, 5).reshape(steps, rows_out, features)


def solution(mesh):
    split = Mesh(
        mesh.devices.reshape(2, 2, 2, 2, 4, 2), ("xh", "xl", "zl", "zh", "y", "c")
    )
    in_specs = (
        P(DP + TP, None, None),
        P(DP + TP),
        P(DP, None),
        P(DP, None),
        P(None, DP + TP, None, None),
        P(None, DP + TP, None),
        P(TP, None, None),
        P(TP, DP),
        P(None, None, DP),
        P(DP),
        P(DP, TP),
        P(DP, TP),
        P(TP, DP),
    )
    out_specs = P(None, TP, DP)
    return jax.shard_map(local, mesh=split, in_specs=in_specs, out_specs=out_specs, check_vma=False)
```

```python
import jax
import jax.numpy as jnp
from jax import lax
from jax.experimental import pallas as pl
from jax.experimental.pallas import tpu as pltpu
from jax.sharding import Mesh, PartitionSpec as P

D = 7168
QKD = 192
norm_eps = 1e-06

DP = ("xh", "xl", "zl")
TP = ("zh", "y", "c")
ZY = ("zh", "y")
PAIR = ("xl",) + ZY
N_DP = 8
N_TP = 16
N_ZY = 8
SWAP = [(0, 1), (1, 0)]
CUTS = (0, 384, 896)
TILE = 768
bf16 = jnp.bfloat16
f32 = jnp.float32
MIB = 1024 * 1024


def exchange(blocks, axes):
    return lax.all_to_all(blocks, axes, 0, 0, tiled=True)


def spread(block, axes, copies):
    return exchange(jnp.broadcast_to(block[None], (copies,) + block.shape), axes)


def swap(block, axis):
    return lax.ppermute(block, axis, SWAP)


def params(mib):
    return pltpu.CompilerParams(vmem_limit_bytes=mib * MIB)


def whole(shape):
    return pl.BlockSpec(shape, lambda *_: (0,) * len(shape))


def leave(slots, cache_t):
    _, entries, length = cache_t.shape
    piece = entries // N_TP

    def body(slots_ref, cache_ref, out_ref, row_ref, sem):
        slot = slots_ref[lax.axis_index(TP)]
        copy = pltpu.make_async_copy(cache_ref.at[slot], row_ref, sem)
        copy.start()
        copy.wait()
        row = row_ref[...].astype(f32)
        for j in range(N_TP):
            out_ref[j] = row[j * piece : (j + 1) * piece].astype(bf16)

    return pl.pallas_call(
        body,
        grid_spec=pltpu.PrefetchScalarGridSpec(
            num_scalar_prefetch=1,
            grid=(1,),
            in_specs=[pl.BlockSpec(memory_space=pl.ANY)],
            out_specs=whole((N_TP, piece, length)),
            scratch_shapes=[pltpu.VMEM((entries, length), bf16), pltpu.SemaphoreType.DMA],
        ),
        out_shape=jax.ShapeDtypeStruct((N_TP, piece, length), bf16),
        compiler_params=params(60),
        name="leave",
    )(slots, cache_t)


def route(peer, pieces):
    def body(peer_ref, in_ref, out_ref):
        for i in range(N_TP):
            out_ref[peer_ref[i]] = in_ref[i]

    return pl.pallas_call(
        body,
        grid_spec=pltpu.PrefetchScalarGridSpec(
            num_scalar_prefetch=1,
            grid=(1,),
            in_specs=[whole(pieces.shape)],
            out_specs=whole(pieces.shape),
        ),
        out_shape=jax.ShapeDtypeStruct(pieces.shape, bf16),
        compiler_params=params(40),
        name="route",
    )(peer, pieces)


def attend(ids, lengths, cache_t, fresh_t, queries_t, heads, latent_width, arrived=None, done=None):
    rows, entries, length = cache_t.shape
    steps, _, _, all_heads = queries_t.shape
    chips = all_heads // (2 * heads)
    again = arrived is not None

    def slot(r, ids):
        return ids[0] if again else r

    def body(ids_ref, lengths_ref, fresh_ref, q_ref, *refs):
        out_ref = refs[-1]
        row = slot(pl.program_id(0), ids_ref)
        current = lengths_ref[row]
        if again:
            latents = jnp.concatenate([refs[0][j].astype(f32) for j in range(N_TP)], axis=0)
        else:
            latents = refs[0][0].astype(f32)
        position = lax.broadcasted_iota(jnp.int32, (entries, length), 1)
        for s in range(steps):
            token = fresh_ref[0, :, s : s + 1].astype(f32)
            latents = jnp.where(position == current + s, token, latents)
        latents = latents.astype(bf16)
        place = lax.broadcasted_iota(jnp.int32, (all_heads, length), 1)
        outs = []
        for s in range(steps):
            scores = lax.dot_general(
                q_ref[s, 0], latents, (((0,), (0,)), ((), ())), preferred_element_type=f32
            )
            scores = jnp.where(place <= current + s, scores * QKD ** (-0.5), -jnp.inf)
            expo = jnp.exp(scores - jnp.max(scores, axis=-1, keepdims=True))
            probs = (expo / jnp.sum(expo, axis=-1, keepdims=True)).astype(bf16)
            out = lax.dot_general(
                probs, latents[:latent_width], (((1,), (1,)), ((), ())), preferred_element_type=f32
            )
            out = out.reshape(chips, 2, heads, latent_width)
            turned = jnp.concatenate([out[:, 1:], out[:, :1]], axis=1)
            out = jnp.where(row >= rows // 2, turned, out)
            outs.append(out.reshape(chips, 2 * heads, latent_width))
        out_ref[:, 0, 0] = jnp.concatenate(outs, axis=1).astype(bf16)

    if again:
        extra_specs = [whole(arrived.shape), pl.BlockSpec(memory_space=pl.ANY)]
        extra = [arrived, done]
    else:
        extra_specs = [pl.BlockSpec((1, entries, length), lambda r, *_: (r, 0, 0))]
        extra = [cache_t]
    return pl.pallas_call(
        body,
        grid_spec=pltpu.PrefetchScalarGridSpec(
            num_scalar_prefetch=2,
            grid=(1 if again else rows,),
            in_specs=[
                pl.BlockSpec((1, entries, steps), lambda r, ids, _: (slot(r, ids), 0, 0)),
                pl.BlockSpec(
                    (steps, 1, entries, all_heads), lambda r, ids, _: (0, slot(r, ids), 0, 0)
                ),
            ]
            + extra_specs,
            out_specs=pl.BlockSpec(
                (chips, 1, 1, 2 * steps * heads, latent_width),
                lambda r, ids, _: (
                    0,
                    lax.div(slot(r, ids), rows // 2),
                    lax.rem(slot(r, ids), rows // 2),
                    0,
                    0,
                ),
            ),
        ),
        out_shape=jax.ShapeDtypeStruct(
            (chips, 2, rows // 2, 2 * steps * heads, latent_width), bf16
        ),
        input_output_aliases={5: 0} if again else {},
        compiler_params=params(60),
        name="again" if again else "attend",
    )(ids, lengths, fresh_t, queries_t, *extra)


def project(ids, rows, weight, blocks):
    groups, count, depth = rows.shape
    width = weight.shape[1] // blocks

    def body(ids_ref, rows_ref, weight_ref, out_ref):
        lhs = rows_ref[...].reshape(groups * count, depth)
        total = jnp.dot(lhs, weight_ref[...], preferred_element_type=f32)
        out_ref[:, 0] = total.astype(bf16).reshape(groups, count, width)

    return pl.pallas_call(
        body,
        grid_spec=pltpu.PrefetchScalarGridSpec(
            num_scalar_prefetch=1,
            grid=(blocks,),
            in_specs=[
                whole(rows.shape),
                pl.BlockSpec((depth, width), lambda k, ids: (0, k)),
            ],
            out_specs=pl.BlockSpec(
                (groups, 1, count, width), lambda k, ids: (0, lax.rem(ids[1] + k, blocks), 0, 0)
            ),
        ),
        out_shape=jax.ShapeDtypeStruct((groups, blocks, count, width), bf16),
        compiler_params=params(40),
        name="project",
    )(ids, rows, weight)


def fetches(refs, blocks, weight_ref, sems):
    copies, n, left = [], 0, 0
    for column in blocks:
        top = 0
        for w in column:
            at = weight_ref.at[pl.ds(top, w.shape[0]), pl.ds(left, w.shape[1])]
            copies.append(pltpu.make_async_copy(refs[n], at, sems.at[n]))
            n, top = n + 1, top + w.shape[0]
        left += column[0].shape[1]
    return copies


def combine(ids, rows, blocks):
    groups, count, depth = rows.shape
    width = blocks[0][0].shape[1]
    flat = [w for column in blocks for w in column]
    half = len(flat) // 2

    def body(ids_ref, rows_ref, *refs):
        out_ref, weight_ref, sems = refs[len(flat) :]
        copies = fetches(refs, blocks, weight_ref, sems)
        for copy in copies:
            copy.start()
        lhs = rows_ref[...].reshape(groups * count, depth)
        for k in range(2):
            for copy in copies[k * half : (k + 1) * half]:
                copy.wait()
            total = jnp.dot(
                lhs, weight_ref[:, k * width : (k + 1) * width], preferred_element_type=f32
            )
            at = lax.rem(ids_ref[1] + k, 2)
            out_ref[:, at] = total.astype(bf16).reshape(groups, count, width)

    return pl.pallas_call(
        body,
        grid_spec=pltpu.PrefetchScalarGridSpec(
            num_scalar_prefetch=1,
            grid=(1,),
            in_specs=[whole(rows.shape)] + [pl.BlockSpec(memory_space=pl.ANY) for _ in flat],
            out_specs=whole((groups, 2, count, width)),
            scratch_shapes=[
                pltpu.VMEM((depth, 2 * width), bf16),
                pltpu.SemaphoreType.DMA((len(flat),)),
            ],
        ),
        out_shape=jax.ShapeDtypeStruct((groups, 2, count, width), bf16),
        compiler_params=params(60),
        name="combine",
    )(ids, rows, *flat)


def widen(ids, rows, blocks):
    halves, chunks, parts, count, features = rows.shape
    depth = parts * features
    columns = sum(column[0].shape[1] for column in blocks)
    every = halves * chunks * count
    flat = [w for column in blocks for w in column]
    half = len(flat) // 2

    def body(ids_ref, rows_ref, *refs):
        out_ref, lhs_ref, weight_ref, sems = refs[len(flat) :]
        copies = fetches(refs, blocks, weight_ref, sems)
        for copy in copies:
            copy.start()

        def put(at, value):
            value = value.astype(bf16).reshape(halves, chunks, count, value.shape[1])
            for h in range(halves):
                out_ref[:, h, :, at] = value[h]

        squares = jnp.zeros((every, 1), f32)
        for k in range(parts):
            block = rows_ref[:, :, lax.rem(ids_ref[1] + k, parts)].reshape(every, features)
            lhs_ref[:, k * features : (k + 1) * features] = block
            wide = block.astype(f32)
            squares += jnp.sum(wide * wide, axis=1, keepdims=True)
        high = squares.astype(bf16).astype(f32)
        lane = lax.broadcasted_iota(jnp.int32, (every, 128), 1)
        extra = jnp.where(lane == 0, high, jnp.where(lane == 1, squares - high, 0.0))
        put(slice(columns, columns + 128), extra)

        for copy in copies[:half]:
            copy.wait()
        for at in range(0, columns, TILE):
            if at == TILE:
                for copy in copies[half:]:
                    copy.wait()
            tile = slice(at, at + TILE)
            put(tile, jnp.dot(lhs_ref[...], weight_ref[:, tile], preferred_element_type=f32))

    return pl.pallas_call(
        body,
        grid_spec=pltpu.PrefetchScalarGridSpec(
            num_scalar_prefetch=1,
            grid=(1,),
            in_specs=[whole(rows.shape)] + [pl.BlockSpec(memory_space=pl.ANY) for _ in flat],
            out_specs=whole((chunks, halves, count, columns + 128)),
            scratch_shapes=[
                pltpu.VMEM((every, depth), bf16),
                pltpu.VMEM((depth, columns), bf16),
                pltpu.SemaphoreType.DMA((len(flat),)),
            ],
        ),
        out_shape=jax.ShapeDtypeStruct((chunks, halves, count, columns + 128), bf16),
        compiler_params=params(60),
        name="widen",
    )(ids, rows, *flat)


def local(
    cache,
    cache_length,
    move_slot,
    move_peer,
    queries,
    new_latent,
    value_up,
    out_proj,
    residual,
    norm_gain,
    gate_weight,
    up_weight,
    down_weight,
):
    member = lax.axis_index(TP)
    core = lax.axis_index("c")
    pair = lax.axis_index("xl")
    steps = new_latent.shape[0]
    heads, latent_width, value_width = value_up.shape
    rows_out = residual.shape[1] // N_TP
    chunk = rows_out * steps
    count = chunk // 2
    features, units = gate_weight.shape

    def by_pair(mine, other):
        first = pair == 0
        return jnp.stack([jnp.where(first, mine, other), jnp.where(first, other, mine)])

    def at_pair(blocks):
        return lax.dynamic_index_in_dim(blocks, pair, 0, False)

    def at_other(blocks):
        return lax.dynamic_index_in_dim(blocks, 1 - pair, 0, False)

    out_came = swap(out_proj, "xl")
    value_ups = jnp.concatenate([value_up, swap(value_up, "c")], axis=0)
    downs = jnp.concatenate([down_weight, swap(down_weight, "c")], axis=0)
    residue = lax.dynamic_slice_in_dim(residual, lax.div(member, 2) * 2 * rows_out, 2 * rows_out, 1)
    residue = residue.reshape(steps, 2, 2, rows_out // 8, 2, 2, features)
    residue = lax.dynamic_index_in_dim(residue, core, 4, False)
    residue = residue.transpose(2, 1, 3, 4, 0, 5).reshape(2, count, features)
    residue_came = swap(at_other(residue), "xl")
    lanes = jnp.arange(N_TP, dtype=jnp.int32)
    own_slot = jnp.sum(jnp.where(lanes == member, move_slot[0], 0))
    ids = jnp.stack([own_slot, pair]).astype(jnp.int32)
    cache_t = cache.transpose(0, 2, 1)
    pieces = exchange(leave(move_slot[0], cache_t), TP)
    pieces, gate_weight, up_weight = lax.optimization_barrier((pieces, gate_weight, up_weight))

    gain = norm_gain.astype(f32)[:, None]

    def scaled(low, high, first, second):
        weight = jnp.where(pair == 0, first[low:high], second[low:high])
        return (weight.astype(f32) * gain[low:high]).astype(bf16)

    sent = [
        scaled(low, high, up_weight, gate_weight) for low, high in zip(CUTS[:-1], CUTS[1:])
    ]
    kept = scaled(0, CUTS[-1], gate_weight, up_weight)
    arrived = exchange(route(move_peer[0], pieces), TP)
    arrived, kept, sent[0], value_ups = lax.optimization_barrier(
        (arrived, kept, sent[0], value_ups)
    )
    fresh_t = new_latent.transpose(1, 2, 0)
    queries_t = queries.transpose(0, 1, 3, 2)
    out = attend(ids, cache_length, cache_t, fresh_t, queries_t, heads, latent_width)
    out = attend(
        ids, cache_length, cache_t, fresh_t, queries_t, heads, latent_width, arrived, out
    )
    out, out_came = lax.optimization_barrier((out, out_came))
    came = [swap(sent[0], "xl")]
    out_weights = [[w, swap(w, "c")] for w in (out_proj, out_came)]
    kept = [kept, swap(kept, "c")]
    out = out.reshape((N_TP,) + out.shape[2:])
    by_head = exchange(out, TP).reshape(-1, 2 * heads, latent_width)
    by_head, kept, came, out_weights, residue_came = lax.optimization_barrier(
        (by_head, kept, came, out_weights, residue_came)
    )
    value_heads = jnp.einsum(
        "thl,hlv->thv", by_head, value_ups, preferred_element_type=f32
    ).astype(bf16)

    value_heads = value_heads.reshape(2, 2, count // 2, 2 * heads * value_width)
    value_heads = value_heads.transpose(1, 0, 2, 3).reshape(2, count, -1)
    value_heads = jnp.broadcast_to(
        value_heads[None, :, None], (2, 2, 2) + value_heads.shape[1:]
    ).reshape((N_DP,) + value_heads.shape[1:])
    gathered = exchange(value_heads, DP)
    gathered, sent[1] = lax.optimization_barrier((gathered, sent[1]))
    came.append(swap(sent[1], "xl"))
    parts = exchange(combine(ids, gathered, out_weights), ZY)
    parts, came[1] = lax.optimization_barrier((parts, came[1]))
    in_weights = [[kept[0]] + came, [kept[1]] + [swap(w, "c") for w in came]]
    residue = by_pair(at_pair(residue), residue_came)
    hidden = residue.astype(f32) + jnp.sum(parts.astype(f32), axis=0)

    rows = spread(hidden.astype(bf16), PAIR, 2 * N_ZY).reshape((2, N_ZY) + hidden.shape)
    rows, in_weights = lax.optimization_barrier((rows, in_weights))
    sums = exchange(widen(ids, rows, in_weights).reshape(N_DP, chunk, -1), DP)
    sums, downs = lax.optimization_barrier((sums, downs))
    sums = jnp.sum(sums.reshape(2, 2, 2, chunk, -1).astype(f32), axis=(0, 2))
    squares = sums[0, :, 2 * units] + sums[0, :, 2 * units + 1]
    inverse = lax.rsqrt(squares / D + norm_eps)[:, None]
    active = sums[:, :, : 2 * units] * inverse
    active = (jax.nn.silu(active[0]) * active[1]).astype(bf16)
    parts = exchange(project(ids, spread(active, DP, N_DP), downs, 1)[:, 0], ZY)
    hidden = by_pair(at_pair(hidden), swap(at_other(hidden), "xl")).reshape(chunk, -1)
    result = (hidden + jnp.sum(parts.astype(f32), axis=0)).astype(bf16)

    result = result.reshape(2, 2, rows_out // 8, 2, steps, features)
    mine = lax.dynamic_index_in_dim(result, core, 1, False)
    near = swap(lax.dynamic_index_in_dim(result, 1 - core, 1, False), "c")
    first = core == 0
    result = jnp.stack([jnp.where(first, mine, near), jnp.where(first, near, mine)])
    return result.transpose(4, 1, 2, 0, 3, 5).reshape(steps, rows_out, features)


def solution(mesh):
    split = Mesh(
        mesh.devices.reshape(2, 2, 2, 2, 4, 2), ("xh", "xl", "zl", "zh", "y", "c")
    )
    in_specs = (
        P(DP + TP, None, None),
        P(DP + TP),
        P(DP, None),
        P(DP, None),
        P(None, DP + TP, None, None),
        P(None, DP + TP, None),
        P(TP, None, None),
        P(TP, DP),
        P(None, None, DP),
        P(DP),
        P(DP, TP),
        P(DP, TP),
        P(TP, DP),
    )
    out_specs = P(None, TP, DP)
    return jax.shard_map(local, mesh=split, in_specs=in_specs, out_specs=out_specs, check_vma=False)
```

```python
import jax
import jax.numpy as jnp
from jax import lax
from jax.experimental import pallas as pl
from jax.experimental.pallas import tpu as pltpu
from jax.sharding import Mesh, PartitionSpec as P

D = 7168
QKD = 192
norm_eps = 1e-06

DP = ("xh", "xl", "zl")
TP = ("zh", "y", "c")
ZY = ("zh", "y")
PAIR = ("xl",) + ZY
N_DP = 8
N_TP = 16
N_ZY = 8
SWAP = [(0, 1), (1, 0)]
CUTS = (0, 256, 768, 896)
TILE = 768
bf16 = jnp.bfloat16
f32 = jnp.float32
MIB = 1024 * 1024


def exchange(blocks, axes):
    return lax.all_to_all(blocks, axes, 0, 0, tiled=True)


def spread(block, axes, copies):
    return exchange(jnp.broadcast_to(block[None], (copies,) + block.shape), axes)


def swap(block, axis):
    return lax.ppermute(block, axis, SWAP)


def params(mib):
    return pltpu.CompilerParams(vmem_limit_bytes=mib * MIB)


def whole(shape):
    return pl.BlockSpec(shape, lambda *_: (0,) * len(shape))


def leave(slots, cache_t):
    _, entries, length = cache_t.shape
    piece = entries // N_TP

    def body(slots_ref, cache_ref, out_ref, row_ref, sem):
        slot = slots_ref[lax.axis_index(TP)]
        copy = pltpu.make_async_copy(cache_ref.at[slot], row_ref, sem)
        copy.start()
        copy.wait()
        row = row_ref[...].astype(f32)
        for j in range(N_TP):
            out_ref[j] = row[j * piece : (j + 1) * piece].astype(bf16)

    return pl.pallas_call(
        body,
        grid_spec=pltpu.PrefetchScalarGridSpec(
            num_scalar_prefetch=1,
            grid=(1,),
            in_specs=[pl.BlockSpec(memory_space=pl.ANY)],
            out_specs=whole((N_TP, piece, length)),
            scratch_shapes=[pltpu.VMEM((entries, length), bf16), pltpu.SemaphoreType.DMA],
        ),
        out_shape=jax.ShapeDtypeStruct((N_TP, piece, length), bf16),
        compiler_params=params(60),
        name="leave",
    )(slots, cache_t)


def route(peer, pieces):
    def body(peer_ref, in_ref, out_ref):
        for i in range(N_TP):
            out_ref[peer_ref[i]] = in_ref[i]

    return pl.pallas_call(
        body,
        grid_spec=pltpu.PrefetchScalarGridSpec(
            num_scalar_prefetch=1,
            grid=(1,),
            in_specs=[whole(pieces.shape)],
            out_specs=whole(pieces.shape),
        ),
        out_shape=jax.ShapeDtypeStruct(pieces.shape, bf16),
        compiler_params=params(40),
        name="route",
    )(peer, pieces)


def attend(ids, lengths, cache_t, fresh_t, queries_t, heads, latent_width, arrived=None, done=None):
    rows, entries, length = cache_t.shape
    steps, _, _, all_heads = queries_t.shape
    chips = all_heads // (2 * heads)
    again = arrived is not None

    def slot(r, ids):
        return ids[0] if again else r

    def body(ids_ref, lengths_ref, fresh_ref, q_ref, *refs):
        out_ref = refs[-1]
        row = slot(pl.program_id(0), ids_ref)
        current = lengths_ref[row]
        if again:
            latents = jnp.concatenate([refs[0][j].astype(f32) for j in range(N_TP)], axis=0)
        else:
            latents = refs[0][0].astype(f32)
        position = lax.broadcasted_iota(jnp.int32, (entries, length), 1)
        for s in range(steps):
            token = fresh_ref[0, :, s : s + 1].astype(f32)
            latents = jnp.where(position == current + s, token, latents)
        latents = latents.astype(bf16)
        place = lax.broadcasted_iota(jnp.int32, (all_heads, length), 1)
        outs = []
        for s in range(steps):
            scores = lax.dot_general(
                q_ref[s, 0], latents, (((0,), (0,)), ((), ())), preferred_element_type=f32
            )
            scores = jnp.where(place <= current + s, scores * QKD ** (-0.5), -jnp.inf)
            expo = jnp.exp(scores - jnp.max(scores, axis=-1, keepdims=True))
            probs = (expo / jnp.sum(expo, axis=-1, keepdims=True)).astype(bf16)
            out = lax.dot_general(
                probs, latents[:latent_width], (((1,), (1,)), ((), ())), preferred_element_type=f32
            )
            out = out.reshape(chips, 2, heads, latent_width)
            turned = jnp.concatenate([out[:, 1:], out[:, :1]], axis=1)
            out = jnp.where(row >= rows // 2, turned, out)
            outs.append(out.reshape(chips, 2 * heads, latent_width))
        out_ref[:, 0, 0] = jnp.concatenate(outs, axis=1).astype(bf16)

    if again:
        extra_specs = [whole(arrived.shape), pl.BlockSpec(memory_space=pl.ANY)]
        extra = [arrived, done]
    else:
        extra_specs = [pl.BlockSpec((1, entries, length), lambda r, *_: (r, 0, 0))]
        extra = [cache_t]
    return pl.pallas_call(
        body,
        grid_spec=pltpu.PrefetchScalarGridSpec(
            num_scalar_prefetch=2,
            grid=(1 if again else rows,),
            in_specs=[
                pl.BlockSpec((1, entries, steps), lambda r, ids, _: (slot(r, ids), 0, 0)),
                pl.BlockSpec(
                    (steps, 1, entries, all_heads), lambda r, ids, _: (0, slot(r, ids), 0, 0)
                ),
            ]
            + extra_specs,
            out_specs=pl.BlockSpec(
                (chips, 1, 1, 2 * steps * heads, latent_width),
                lambda r, ids, _: (
                    0,
                    lax.div(slot(r, ids), rows // 2),
                    lax.rem(slot(r, ids), rows // 2),
                    0,
                    0,
                ),
            ),
        ),
        out_shape=jax.ShapeDtypeStruct(
            (chips, 2, rows // 2, 2 * steps * heads, latent_width), bf16
        ),
        input_output_aliases={5: 0} if again else {},
        compiler_params=params(60),
        name="again" if again else "attend",
    )(ids, lengths, fresh_t, queries_t, *extra)


def join(blocks):
    flat = [w for column in blocks for w in column]
    depth = sum(w.shape[0] for w in blocks[0])
    width = sum(column[0].shape[1] for column in blocks)

    def body(*refs):
        out_ref, sems = refs[len(flat) :]
        copies, left = [], 0
        for column in blocks:
            top = 0
            for w in column:
                at = out_ref.at[pl.ds(top, w.shape[0]), pl.ds(left, w.shape[1])]
                n = len(copies)
                copies.append(pltpu.make_async_copy(refs[n], at, sems.at[n]))
                top += w.shape[0]
            left += column[0].shape[1]
        for copy in copies:
            copy.start()
        for copy in copies:
            copy.wait()

    return pl.pallas_call(
        body,
        in_specs=[pl.BlockSpec(memory_space=pl.ANY) for _ in flat],
        out_specs=pl.BlockSpec(memory_space=pl.ANY),
        scratch_shapes=[pltpu.SemaphoreType.DMA((len(flat),))],
        out_shape=jax.ShapeDtypeStruct((depth, width), bf16),
        compiler_params=params(8),
        name="join",
    )(*flat)


def project(ids, rows, weight, blocks):
    groups, count, depth = rows.shape
    width = weight.shape[1] // blocks

    def body(ids_ref, rows_ref, weight_ref, out_ref):
        lhs = rows_ref[...].reshape(groups * count, depth)
        total = jnp.dot(lhs, weight_ref[...], preferred_element_type=f32)
        out_ref[:, 0] = total.astype(bf16).reshape(groups, count, width)

    return pl.pallas_call(
        body,
        grid_spec=pltpu.PrefetchScalarGridSpec(
            num_scalar_prefetch=1,
            grid=(blocks,),
            in_specs=[
                whole(rows.shape),
                pl.BlockSpec((depth, width), lambda k, ids: (0, k)),
            ],
            out_specs=pl.BlockSpec(
                (groups, 1, count, width), lambda k, ids: (0, lax.rem(ids[1] + k, blocks), 0, 0)
            ),
        ),
        out_shape=jax.ShapeDtypeStruct((groups, blocks, count, width), bf16),
        compiler_params=params(40),
        name="project",
    )(ids, rows, weight)


def widen(ids, rows, weight):
    halves, chunks, blocks, count, features = rows.shape
    depth, columns = weight.shape
    every = halves * chunks * count

    def body(ids_ref, rows_ref, weight_ref, out_ref, lhs_ref):
        tile = pl.program_id(0)

        def put(at, value):
            value = value.astype(bf16).reshape(halves, chunks, count, value.shape[1])
            for h in range(halves):
                out_ref[:, h, :, at] = value[h]

        @pl.when(tile == 0)
        def _():
            squares = jnp.zeros((every, 1), f32)
            for k in range(blocks):
                block = rows_ref[:, :, lax.rem(ids_ref[1] + k, blocks)].reshape(every, features)
                lhs_ref[:, k * features : (k + 1) * features] = block
                wide = block.astype(f32)
                squares += jnp.sum(wide * wide, axis=1, keepdims=True)
            high = squares.astype(bf16).astype(f32)
            lane = lax.broadcasted_iota(jnp.int32, (every, 128), 1)
            extra = jnp.where(lane == 0, high, jnp.where(lane == 1, squares - high, 0.0))
            put(slice(columns, columns + 128), extra)

        total = jnp.dot(lhs_ref[...], weight_ref[...], preferred_element_type=f32)
        put(pl.ds(pl.multiple_of(tile * TILE, 128), TILE), total)

    return pl.pallas_call(
        body,
        grid_spec=pltpu.PrefetchScalarGridSpec(
            num_scalar_prefetch=1,
            grid=(columns // TILE,),
            in_specs=[
                whole(rows.shape),
                pl.BlockSpec((depth, TILE), lambda k, ids: (0, k)),
            ],
            out_specs=whole((chunks, halves, count, columns + 128)),
            scratch_shapes=[pltpu.VMEM((every, depth), bf16)],
        ),
        out_shape=jax.ShapeDtypeStruct((chunks, halves, count, columns + 128), bf16),
        compiler_params=params(40),
        name="widen",
    )(ids, rows, weight)


def local(
    cache,
    cache_length,
    move_slot,
    move_peer,
    queries,
    new_latent,
    value_up,
    out_proj,
    residual,
    norm_gain,
    gate_weight,
    up_weight,
    down_weight,
):
    member = lax.axis_index(TP)
    core = lax.axis_index("c")
    pair = lax.axis_index("xl")
    steps = new_latent.shape[0]
    heads, latent_width, value_width = value_up.shape
    rows_out = residual.shape[1] // N_TP
    chunk = rows_out * steps
    count = chunk // 2
    features, units = gate_weight.shape

    def by_pair(mine, other):
        first = pair == 0
        return jnp.stack([jnp.where(first, mine, other), jnp.where(first, other, mine)])

    def at_pair(blocks):
        return lax.dynamic_index_in_dim(blocks, pair, 0, False)

    def at_other(blocks):
        return lax.dynamic_index_in_dim(blocks, 1 - pair, 0, False)

    out_came = swap(out_proj, "xl")
    value_ups = jnp.concatenate([value_up, swap(value_up, "c")], axis=0)
    downs = jnp.concatenate([down_weight, swap(down_weight, "c")], axis=0)
    residue = lax.dynamic_slice_in_dim(residual, lax.div(member, 2) * 2 * rows_out, 2 * rows_out, 1)
    residue = residue.reshape(steps, 2, 2, rows_out // 8, 2, 2, features)
    residue = lax.dynamic_index_in_dim(residue, core, 4, False)
    residue = residue.transpose(2, 1, 3, 4, 0, 5).reshape(2, count, features)
    residue_came = swap(at_other(residue), "xl")
    lanes = jnp.arange(N_TP, dtype=jnp.int32)
    own_slot = jnp.sum(jnp.where(lanes == member, move_slot[0], 0))
    ids = jnp.stack([own_slot, pair]).astype(jnp.int32)
    cache_t = cache.transpose(0, 2, 1)
    leaving, ids = lax.optimization_barrier((leave(move_slot[0], cache_t), ids))
    pieces = exchange(leaving, TP)
    fresh_t = new_latent.transpose(1, 2, 0)
    queries_t = queries.transpose(0, 1, 3, 2)
    out = attend(ids, cache_length, cache_t, fresh_t, queries_t, heads, latent_width)
    pieces, out, gate_weight, up_weight = lax.optimization_barrier(
        (pieces, out, gate_weight, up_weight)
    )

    gain = norm_gain.astype(f32)[:, None]

    def scaled(low, high, first, second):
        weight = jnp.where(pair == 0, first[low:high], second[low:high])
        return (weight.astype(f32) * gain[low:high]).astype(bf16)

    sent = [
        scaled(low, high, up_weight, gate_weight) for low, high in zip(CUTS[:-1], CUTS[1:])
    ]
    kept = scaled(0, CUTS[-1], gate_weight, up_weight)
    arrived = exchange(route(move_peer[0], pieces), TP)
    arrived, kept, sent[0], value_ups = lax.optimization_barrier(
        (arrived, kept, sent[0], value_ups)
    )
    out = attend(
        ids, cache_length, cache_t, fresh_t, queries_t, heads, latent_width, arrived, out
    )
    out, out_came = lax.optimization_barrier((out, out_came))
    came = [swap(sent[0], "xl")]
    out_weights = join([[w, swap(w, "c")] for w in (out_proj, out_came)])
    kept = [kept, swap(kept, "c")]
    out = out.reshape((N_TP,) + out.shape[2:])
    by_head = exchange(out, TP).reshape(-1, 2 * heads, latent_width)
    by_head, kept, came, out_weights, residue_came = lax.optimization_barrier(
        (by_head, kept, came, out_weights, residue_came)
    )
    value_heads = jnp.einsum(
        "thl,hlv->thv", by_head, value_ups, preferred_element_type=f32
    ).astype(bf16)

    value_heads = value_heads.reshape(2, 2, count // 2, 2 * heads * value_width)
    value_heads = value_heads.transpose(1, 0, 2, 3).reshape(2, count, -1)
    value_heads = jnp.broadcast_to(
        value_heads[None, :, None], (2, 2, 2) + value_heads.shape[1:]
    ).reshape((N_DP,) + value_heads.shape[1:])
    gathered = exchange(value_heads, DP)
    gathered, sent[1] = lax.optimization_barrier((gathered, sent[1]))
    came.append(swap(sent[1], "xl"))
    parts = exchange(project(ids, gathered, out_weights, 2), ZY)
    parts, came[1], sent[2] = lax.optimization_barrier((parts, came[1], sent[2]))
    came.append(swap(sent[2], "xl"))
    in_weight = join([[kept[0]] + came, [kept[1]] + [swap(w, "c") for w in came]])
    residue = by_pair(at_pair(residue), residue_came)
    hidden = residue.astype(f32) + jnp.sum(parts.astype(f32), axis=0)

    rows = spread(hidden.astype(bf16), PAIR, 2 * N_ZY).reshape((2, N_ZY) + hidden.shape)
    rows, in_weight = lax.optimization_barrier((rows, in_weight))
    sums = exchange(widen(ids, rows, in_weight).reshape(N_DP, chunk, -1), DP)
    sums, downs = lax.optimization_barrier((sums, downs))
    sums = jnp.sum(sums.reshape(2, 2, 2, chunk, -1).astype(f32), axis=(0, 2))
    squares = sums[0, :, 2 * units] + sums[0, :, 2 * units + 1]
    inverse = lax.rsqrt(squares / D + norm_eps)[:, None]
    active = sums[:, :, : 2 * units] * inverse
    active = (jax.nn.silu(active[0]) * active[1]).astype(bf16)
    parts = exchange(project(ids, spread(active, DP, N_DP), downs, 1)[:, 0], ZY)
    hidden = by_pair(at_pair(hidden), swap(at_other(hidden), "xl")).reshape(chunk, -1)
    result = (hidden + jnp.sum(parts.astype(f32), axis=0)).astype(bf16)

    result = result.reshape(2, 2, rows_out // 8, 2, steps, features)
    mine = lax.dynamic_index_in_dim(result, core, 1, False)
    near = swap(lax.dynamic_index_in_dim(result, 1 - core, 1, False), "c")
    first = core == 0
    result = jnp.stack([jnp.where(first, mine, near), jnp.where(first, near, mine)])
    return result.transpose(4, 1, 2, 0, 3, 5).reshape(steps, rows_out, features)


def solution(mesh):
    split = Mesh(
        mesh.devices.reshape(2, 2, 2, 2, 4, 2), ("xh", "xl", "zl", "zh", "y", "c")
    )
    in_specs = (
        P(DP + TP, None, None),
        P(DP + TP),
        P(DP, None),
        P(DP, None),
        P(None, DP + TP, None, None),
        P(None, DP + TP, None),
        P(TP, None, None),
        P(TP, DP),
        P(None, None, DP),
        P(DP),
        P(DP, TP),
        P(DP, TP),
        P(TP, DP),
    )
    out_specs = P(None, TP, DP)
    return jax.shard_map(local, mesh=split, in_specs=in_specs, out_specs=out_specs, check_vma=False)
```

```python
import jax
import jax.numpy as jnp
from jax import lax
from jax.experimental import pallas as pl
from jax.experimental.pallas import tpu as pltpu
from jax.sharding import Mesh, PartitionSpec as P

D = 7168
QKD = 192
norm_eps = 1e-06

DP = ("xh", "xl", "zl")
TP = ("zh", "y", "c")
ZY = ("zh", "y")
PAIR = ("xl",) + ZY
N_DP = 8
N_TP = 16
N_ZY = 8
SWAP = [(0, 1), (1, 0)]
CUTS = (0, 384, 896)
OUT_CUTS = (0, 480, 864, 1024)
TILE = 768
bf16 = jnp.bfloat16
f32 = jnp.float32
MIB = 1024 * 1024


def exchange(blocks, axes):
    return lax.all_to_all(blocks, axes, 0, 0, tiled=True)


def spread(block, axes, copies):
    return exchange(jnp.broadcast_to(block[None], (copies,) + block.shape), axes)


def swap(block, axis):
    return lax.ppermute(block, axis, SWAP)


def params(mib):
    return pltpu.CompilerParams(vmem_limit_bytes=mib * MIB)


def whole(shape):
    return pl.BlockSpec(shape, lambda *_: (0,) * len(shape))


def leave(slots, cache_t):
    _, entries, length = cache_t.shape
    piece = entries // N_TP

    def body(slots_ref, cache_ref, out_ref, row_ref, sem):
        slot = slots_ref[lax.axis_index(TP)]
        copy = pltpu.make_async_copy(cache_ref.at[slot], row_ref, sem)
        copy.start()
        copy.wait()
        row = row_ref[...].astype(f32)
        for j in range(N_TP):
            out_ref[j] = row[j * piece : (j + 1) * piece].astype(bf16)

    return pl.pallas_call(
        body,
        grid_spec=pltpu.PrefetchScalarGridSpec(
            num_scalar_prefetch=1,
            grid=(1,),
            in_specs=[pl.BlockSpec(memory_space=pl.ANY)],
            out_specs=whole((N_TP, piece, length)),
            scratch_shapes=[pltpu.VMEM((entries, length), bf16), pltpu.SemaphoreType.DMA],
        ),
        out_shape=jax.ShapeDtypeStruct((N_TP, piece, length), bf16),
        compiler_params=params(60),
        name="leave",
    )(slots, cache_t)


def route(peer, pieces):
    def body(peer_ref, in_ref, out_ref):
        for i in range(N_TP):
            out_ref[peer_ref[i]] = in_ref[i]

    return pl.pallas_call(
        body,
        grid_spec=pltpu.PrefetchScalarGridSpec(
            num_scalar_prefetch=1,
            grid=(1,),
            in_specs=[whole(pieces.shape)],
            out_specs=whole(pieces.shape),
        ),
        out_shape=jax.ShapeDtypeStruct(pieces.shape, bf16),
        compiler_params=params(40),
        name="route",
    )(peer, pieces)


def attend(ids, lengths, cache_t, fresh_t, queries_t, heads, latent_width, arrived=None, done=None):
    rows, entries, length = cache_t.shape
    steps, _, _, all_heads = queries_t.shape
    chips = all_heads // (2 * heads)
    again = arrived is not None

    def slot(r, ids):
        return ids[0] if again else r

    def body(ids_ref, lengths_ref, fresh_ref, q_ref, *refs):
        out_ref = refs[-1]
        row = slot(pl.program_id(0), ids_ref)
        current = lengths_ref[row]
        if again:
            latents = jnp.concatenate([refs[0][j].astype(f32) for j in range(N_TP)], axis=0)
        else:
            latents = refs[0][0].astype(f32)
        position = lax.broadcasted_iota(jnp.int32, (entries, length), 1)
        for s in range(steps):
            token = fresh_ref[0, :, s : s + 1].astype(f32)
            latents = jnp.where(position == current + s, token, latents)
        latents = latents.astype(bf16)
        place = lax.broadcasted_iota(jnp.int32, (all_heads, length), 1)
        outs = []
        for s in range(steps):
            scores = lax.dot_general(
                q_ref[s, 0], latents, (((0,), (0,)), ((), ())), preferred_element_type=f32
            )
            scores = jnp.where(place <= current + s, scores * QKD ** (-0.5), -jnp.inf)
            expo = jnp.exp(scores - jnp.max(scores, axis=-1, keepdims=True))
            probs = (expo / jnp.sum(expo, axis=-1, keepdims=True)).astype(bf16)
            out = lax.dot_general(
                probs, latents[:latent_width], (((1,), (1,)), ((), ())), preferred_element_type=f32
            )
            out = out.reshape(chips, 2, heads, latent_width)
            turned = jnp.concatenate([out[:, 1:], out[:, :1]], axis=1)
            out = jnp.where(row >= rows // 2, turned, out)
            outs.append(out.reshape(chips, 2 * heads, latent_width))
        out_ref[:, 0, 0] = jnp.concatenate(outs, axis=1).astype(bf16)

    if again:
        extra_specs = [whole(arrived.shape), pl.BlockSpec(memory_space=pl.ANY)]
        extra = [arrived, done]
    else:
        extra_specs = [pl.BlockSpec((1, entries, length), lambda r, *_: (r, 0, 0))]
        extra = [cache_t]
    return pl.pallas_call(
        body,
        grid_spec=pltpu.PrefetchScalarGridSpec(
            num_scalar_prefetch=2,
            grid=(1 if again else rows,),
            in_specs=[
                pl.BlockSpec((1, entries, steps), lambda r, ids, _: (slot(r, ids), 0, 0)),
                pl.BlockSpec(
                    (steps, 1, entries, all_heads), lambda r, ids, _: (0, slot(r, ids), 0, 0)
                ),
            ]
            + extra_specs,
            out_specs=pl.BlockSpec(
                (chips, 1, 1, 2 * steps * heads, latent_width),
                lambda r, ids, _: (
                    0,
                    lax.div(slot(r, ids), rows // 2),
                    lax.rem(slot(r, ids), rows // 2),
                    0,
                    0,
                ),
            ),
        ),
        out_shape=jax.ShapeDtypeStruct(
            (chips, 2, rows // 2, 2 * steps * heads, latent_width), bf16
        ),
        input_output_aliases={5: 0} if again else {},
        compiler_params=params(60),
        name="again" if again else "attend",
    )(ids, lengths, fresh_t, queries_t, *extra)


def project(ids, rows, weight, blocks):
    groups, count, depth = rows.shape
    width = weight.shape[1] // blocks

    def body(ids_ref, rows_ref, weight_ref, out_ref):
        lhs = rows_ref[...].reshape(groups * count, depth)
        total = jnp.dot(lhs, weight_ref[...], preferred_element_type=f32)
        out_ref[:, 0] = total.astype(bf16).reshape(groups, count, width)

    return pl.pallas_call(
        body,
        grid_spec=pltpu.PrefetchScalarGridSpec(
            num_scalar_prefetch=1,
            grid=(blocks,),
            in_specs=[
                whole(rows.shape),
                pl.BlockSpec((depth, width), lambda k, ids: (0, k)),
            ],
            out_specs=pl.BlockSpec(
                (groups, 1, count, width), lambda k, ids: (0, lax.rem(ids[1] + k, blocks), 0, 0)
            ),
        ),
        out_shape=jax.ShapeDtypeStruct((groups, blocks, count, width), bf16),
        compiler_params=params(40),
        name="project",
    )(ids, rows, weight)


def fetches(refs, blocks, weight_ref, sems):
    copies, n, left = [], 0, 0
    for column in blocks:
        top = 0
        for w in column:
            at = weight_ref.at[pl.ds(top, w.shape[0]), pl.ds(left, w.shape[1])]
            copies.append(pltpu.make_async_copy(refs[n], at, sems.at[n]))
            n, top = n + 1, top + w.shape[0]
        left += column[0].shape[1]
    return copies


def combine(ids, rows, blocks):
    groups, count, depth = rows.shape
    width = blocks[0][0].shape[1]
    flat = [w for column in blocks for w in column]
    ends = [0, len(blocks[0]), len(flat)]

    def body(ids_ref, rows_ref, *refs):
        out_ref, weight_ref, sems = refs[len(flat) :]
        copies = fetches(refs, blocks, weight_ref, sems)
        for copy in copies:
            copy.start()
        lhs = rows_ref[...].reshape(groups * count, depth)
        for k in range(2):
            for copy in copies[ends[k] : ends[k + 1]]:
                copy.wait()
            total = jnp.dot(
                lhs, weight_ref[:, k * width : (k + 1) * width], preferred_element_type=f32
            )
            at = lax.rem(ids_ref[1] + k, 2)
            out_ref[:, at] = total.astype(bf16).reshape(groups, count, width)

    return pl.pallas_call(
        body,
        grid_spec=pltpu.PrefetchScalarGridSpec(
            num_scalar_prefetch=1,
            grid=(1,),
            in_specs=[whole(rows.shape)] + [pl.BlockSpec(memory_space=pl.ANY) for _ in flat],
            out_specs=whole((groups, 2, count, width)),
            scratch_shapes=[
                pltpu.VMEM((depth, 2 * width), bf16),
                pltpu.SemaphoreType.DMA((len(flat),)),
            ],
        ),
        out_shape=jax.ShapeDtypeStruct((groups, 2, count, width), bf16),
        compiler_params=params(60),
        name="combine",
    )(ids, rows, *flat)


def widen(ids, rows, blocks):
    halves, chunks, parts, count, features = rows.shape
    depth = parts * features
    columns = sum(column[0].shape[1] for column in blocks)
    every = halves * chunks * count
    flat = [w for column in blocks for w in column]
    half = len(flat) // 2

    def body(ids_ref, rows_ref, *refs):
        out_ref, lhs_ref, weight_ref, sems = refs[len(flat) :]
        copies = fetches(refs, blocks, weight_ref, sems)
        for copy in copies:
            copy.start()

        def put(at, value):
            value = value.astype(bf16).reshape(halves, chunks, count, value.shape[1])
            for h in range(halves):
                out_ref[:, h, :, at] = value[h]

        squares = jnp.zeros((every, 1), f32)
        for k in range(parts):
            block = rows_ref[:, :, lax.rem(ids_ref[1] + k, parts)].reshape(every, features)
            lhs_ref[:, k * features : (k + 1) * features] = block
            wide = block.astype(f32)
            squares += jnp.sum(wide * wide, axis=1, keepdims=True)
        high = squares.astype(bf16).astype(f32)
        lane = lax.broadcasted_iota(jnp.int32, (every, 128), 1)
        extra = jnp.where(lane == 0, high, jnp.where(lane == 1, squares - high, 0.0))
        put(slice(columns, columns + 128), extra)

        for copy in copies[:half]:
            copy.wait()
        for at in range(0, columns, TILE):
            if at == TILE:
                for copy in copies[half:]:
                    copy.wait()
            tile = slice(at, at + TILE)
            put(tile, jnp.dot(lhs_ref[...], weight_ref[:, tile], preferred_element_type=f32))

    return pl.pallas_call(
        body,
        grid_spec=pltpu.PrefetchScalarGridSpec(
            num_scalar_prefetch=1,
            grid=(1,),
            in_specs=[whole(rows.shape)] + [pl.BlockSpec(memory_space=pl.ANY) for _ in flat],
            out_specs=whole((chunks, halves, count, columns + 128)),
            scratch_shapes=[
                pltpu.VMEM((every, depth), bf16),
                pltpu.VMEM((depth, columns), bf16),
                pltpu.SemaphoreType.DMA((len(flat),)),
            ],
        ),
        out_shape=jax.ShapeDtypeStruct((chunks, halves, count, columns + 128), bf16),
        compiler_params=params(32),
        name="widen",
    )(ids, rows, *flat)


def local(
    cache,
    cache_length,
    move_slot,
    move_peer,
    queries,
    new_latent,
    value_up,
    out_proj,
    residual,
    norm_gain,
    gate_weight,
    up_weight,
    down_weight,
):
    member = lax.axis_index(TP)
    core = lax.axis_index("c")
    pair = lax.axis_index("xl")
    steps = new_latent.shape[0]
    heads, latent_width, value_width = value_up.shape
    rows_out = residual.shape[1] // N_TP
    chunk = rows_out * steps
    count = chunk // 2
    features, units = gate_weight.shape

    def by_pair(mine, other):
        first = pair == 0
        return jnp.stack([jnp.where(first, mine, other), jnp.where(first, other, mine)])

    def at_pair(blocks):
        return lax.dynamic_index_in_dim(blocks, pair, 0, False)

    def at_other(blocks):
        return lax.dynamic_index_in_dim(blocks, 1 - pair, 0, False)

    out_came = [swap(out_proj[: OUT_CUTS[1]], "xl")]
    value_ups = jnp.concatenate([value_up, swap(value_up, "c")], axis=0)
    lanes = jnp.arange(N_TP, dtype=jnp.int32)
    cache_t = cache.transpose(0, 2, 1)
    leaving, slots, out_late = lax.optimization_barrier(
        (leave(move_slot[0], cache_t), move_slot[0], out_proj)
    )
    for low, high in zip(OUT_CUTS[1:-1], OUT_CUTS[2:]):
        out_came.append(swap(out_late[low:high], "xl"))
    pieces = exchange(leaving, TP)
    own_slot = jnp.sum(jnp.where(lanes == member, slots, 0))
    ids = jnp.stack([own_slot, pair]).astype(jnp.int32)
    fresh_t = new_latent.transpose(1, 2, 0)
    queries_t = queries.transpose(0, 1, 3, 2)
    out = attend(ids, cache_length, cache_t, fresh_t, queries_t, heads, latent_width)
    pieces, out, out_came[0], gate_weight, up_weight = lax.optimization_barrier(
        (pieces, out, out_came[0], gate_weight, up_weight)
    )

    gain = norm_gain.astype(f32)[:, None]

    def scaled(low, high, first, second):
        weight = jnp.where(pair == 0, first[low:high], second[low:high])
        return (weight.astype(f32) * gain[low:high]).astype(bf16)

    sent = [
        scaled(low, high, up_weight, gate_weight) for low, high in zip(CUTS[:-1], CUTS[1:])
    ]
    kept = scaled(0, CUTS[-1], gate_weight, up_weight)
    arrived = exchange(route(move_peer[0], pieces), TP)
    arrived, kept, sent[0], value_ups, out_came[1] = lax.optimization_barrier(
        (arrived, kept, sent[0], value_ups, out_came[1])
    )
    out = attend(
        ids, cache_length, cache_t, fresh_t, queries_t, heads, latent_width, arrived, out
    )
    out, out_came[2] = lax.optimization_barrier((out, out_came[2]))
    came = [swap(sent[0], "xl")]
    out = out.reshape((N_TP,) + out.shape[2:])
    by_head = exchange(out, TP).reshape(-1, 2 * heads, latent_width)
    by_head, kept, came[0], out_came, out_late, residual = lax.optimization_barrier(
        (by_head, kept, came[0], out_came, out_late, residual)
    )
    out_weights = [ws + [swap(w, "c") for w in ws] for ws in ([out_late], out_came)]
    out_weights[0][1], residual = lax.optimization_barrier((out_weights[0][1], residual))
    residue = lax.dynamic_slice_in_dim(residual, lax.div(member, 2) * 2 * rows_out, 2 * rows_out, 1)
    residue = residue.reshape(steps, 2, 2, rows_out // 8, 2, 2, features)
    residue = lax.dynamic_index_in_dim(residue, core, 4, False)
    residue = residue.transpose(2, 1, 3, 4, 0, 5).reshape(2, count, features)
    residue = by_pair(at_pair(residue), swap(at_other(residue), "xl"))
    value_heads = jnp.einsum(
        "thl,hlv->thv", by_head, value_ups, preferred_element_type=f32
    ).astype(bf16)

    value_heads = value_heads.reshape(2, 2, count // 2, 2 * heads * value_width)
    value_heads = value_heads.transpose(1, 0, 2, 3).reshape(2, count, -1)
    value_heads = jnp.broadcast_to(
        value_heads[None, :, None], (2, 2, 2) + value_heads.shape[1:]
    ).reshape((N_DP,) + value_heads.shape[1:])
    gathered = exchange(value_heads, DP)
    gathered, sent[1], kept, down_weight, residue, out_weights = lax.optimization_barrier(
        (gathered, sent[1], kept, down_weight, residue, out_weights)
    )
    kept = [kept, swap(kept, "c")]
    came.append(swap(sent[1], "xl"))
    parts = exchange(combine(ids, gathered, out_weights), ZY)
    parts, came[1] = lax.optimization_barrier((parts, came[1]))
    in_weights = [[kept[0]] + came, [kept[1]] + [swap(w, "c") for w in came]]
    hidden = residue.astype(f32) + jnp.sum(parts.astype(f32), axis=0)

    rows = spread(hidden.astype(bf16), PAIR, 2 * N_ZY).reshape((2, N_ZY) + hidden.shape)
    rows, in_weights, down_weight = lax.optimization_barrier((rows, in_weights, down_weight))
    downs = jnp.concatenate([down_weight, swap(down_weight, "c")], axis=0)
    sums = exchange(widen(ids, rows, in_weights).reshape(N_DP, chunk, -1), DP)
    sums = jnp.sum(sums.reshape(2, 2, 2, chunk, -1).astype(f32), axis=(0, 2))
    squares = sums[0, :, 2 * units] + sums[0, :, 2 * units + 1]
    inverse = lax.rsqrt(squares / D + norm_eps)[:, None]
    active = sums[:, :, : 2 * units] * inverse
    active = (jax.nn.silu(active[0]) * active[1]).astype(bf16)
    parts = exchange(project(ids, spread(active, DP, N_DP), downs, 1)[:, 0], ZY)
    hidden = by_pair(at_pair(hidden), swap(at_other(hidden), "xl")).reshape(chunk, -1)
    result = (hidden + jnp.sum(parts.astype(f32), axis=0)).astype(bf16)

    result = result.reshape(2, 2, rows_out // 8, 2, steps, features)
    mine = lax.dynamic_index_in_dim(result, core, 1, False)
    near = swap(lax.dynamic_index_in_dim(result, 1 - core, 1, False), "c")
    first = core == 0
    result = jnp.stack([jnp.where(first, mine, near), jnp.where(first, near, mine)])
    return result.transpose(4, 1, 2, 0, 3, 5).reshape(steps, rows_out, features)


def solution(mesh):
    split = Mesh(
        mesh.devices.reshape(2, 2, 2, 2, 4, 2), ("xh", "xl", "zl", "zh", "y", "c")
    )
    in_specs = (
        P(DP + TP, None, None),
        P(DP + TP),
        P(DP, None),
        P(DP, None),
        P(None, DP + TP, None, None),
        P(None, DP + TP, None),
        P(TP, None, None),
        P(TP, DP),
        P(None, None, DP),
        P(DP),
        P(DP, TP),
        P(DP, TP),
        P(TP, DP),
    )
    out_specs = P(None, TP, DP)
    return jax.shard_map(local, mesh=split, in_specs=in_specs, out_specs=out_specs, check_vma=False)
```

```python
import jax
import jax.numpy as jnp
from jax import lax
from jax.experimental import pallas as pl
from jax.experimental.pallas import tpu as pltpu
from jax.sharding import Mesh, PartitionSpec as P

D = 7168
QKD = 192
norm_eps = 1e-06

DP = ("xh", "xl", "zl")
TP = ("zh", "y", "c")
ZY = ("zh", "y")
PAIR = ("xl",) + ZY
N_DP = 8
N_TP = 16
N_ZY = 8
SWAP = [(0, 1), (1, 0)]
CUT = 384
TILE = 768
bf16 = jnp.bfloat16
f32 = jnp.float32
MIB = 1024 * 1024


def exchange(blocks, axes):
    return lax.all_to_all(blocks, axes, 0, 0, tiled=True)


def spread(block, axes, copies):
    return exchange(jnp.broadcast_to(block[None], (copies,) + block.shape), axes)


def swap(block, axis):
    return lax.ppermute(block, axis, SWAP)


def params(mib):
    return pltpu.CompilerParams(vmem_limit_bytes=mib * MIB)


def whole(shape):
    return pl.BlockSpec(shape, lambda *_: (0,) * len(shape))


def leave(slots, cache_t):
    _, entries, length = cache_t.shape
    piece = entries // N_TP

    def body(slots_ref, cache_ref, out_ref, row_ref, sem):
        slot = slots_ref[lax.axis_index(TP)]
        copy = pltpu.make_async_copy(cache_ref.at[slot], row_ref, sem)
        copy.start()
        copy.wait()
        row = row_ref[...].astype(f32)
        for j in range(N_TP):
            out_ref[j] = row[j * piece : (j + 1) * piece].astype(bf16)

    return pl.pallas_call(
        body,
        grid_spec=pltpu.PrefetchScalarGridSpec(
            num_scalar_prefetch=1,
            grid=(1,),
            in_specs=[pl.BlockSpec(memory_space=pl.ANY)],
            out_specs=whole((N_TP, piece, length)),
            scratch_shapes=[pltpu.VMEM((entries, length), bf16), pltpu.SemaphoreType.DMA],
        ),
        out_shape=jax.ShapeDtypeStruct((N_TP, piece, length), bf16),
        compiler_params=params(60),
        name="leave",
    )(slots, cache_t)


def route(peer, pieces):
    def body(peer_ref, in_ref, out_ref):
        for i in range(N_TP):
            out_ref[peer_ref[i]] = in_ref[i]

    return pl.pallas_call(
        body,
        grid_spec=pltpu.PrefetchScalarGridSpec(
            num_scalar_prefetch=1,
            grid=(1,),
            in_specs=[whole(pieces.shape)],
            out_specs=whole(pieces.shape),
        ),
        out_shape=jax.ShapeDtypeStruct(pieces.shape, bf16),
        compiler_params=params(40),
        name="route",
    )(peer, pieces)


def attend(ids, lengths, cache_t, fresh_t, queries_t, heads, latent_width, arrived=None, done=None):
    rows, entries, length = cache_t.shape
    steps, _, _, all_heads = queries_t.shape
    chips = all_heads // (2 * heads)
    again = arrived is not None

    def slot(r, ids):
        return ids[0] if again else r

    def body(ids_ref, lengths_ref, fresh_ref, q_ref, *refs):
        out_ref = refs[-1]
        row = slot(pl.program_id(0), ids_ref)
        current = lengths_ref[row]
        if again:
            latents = jnp.concatenate([refs[0][j].astype(f32) for j in range(N_TP)], axis=0)
        else:
            latents = refs[0][0].astype(f32)
        position = lax.broadcasted_iota(jnp.int32, (entries, length), 1)
        for s in range(steps):
            token = fresh_ref[0, :, s : s + 1].astype(f32)
            latents = jnp.where(position == current + s, token, latents)
        latents = latents.astype(bf16)
        place = lax.broadcasted_iota(jnp.int32, (all_heads, length), 1)
        outs = []
        for s in range(steps):
            scores = lax.dot_general(
                q_ref[s, 0], latents, (((0,), (0,)), ((), ())), preferred_element_type=f32
            )
            scores = jnp.where(place <= current + s, scores * QKD ** (-0.5), -jnp.inf)
            expo = jnp.exp(scores - jnp.max(scores, axis=-1, keepdims=True))
            probs = (expo / jnp.sum(expo, axis=-1, keepdims=True)).astype(bf16)
            out = lax.dot_general(
                probs, latents[:latent_width], (((1,), (1,)), ((), ())), preferred_element_type=f32
            )
            out = out.reshape(chips, 2, heads, latent_width)
            turned = jnp.concatenate([out[:, 1:], out[:, :1]], axis=1)
            out = jnp.where(row >= rows // 2, turned, out)
            outs.append(out.reshape(chips, 2 * heads, latent_width))
        out_ref[:, 0, 0] = jnp.concatenate(outs, axis=1).astype(bf16)

    if again:
        extra_specs = [whole(arrived.shape), pl.BlockSpec(memory_space=pl.ANY)]
        extra = [arrived, done]
    else:
        extra_specs = [pl.BlockSpec((1, entries, length), lambda r, *_: (r, 0, 0))]
        extra = [cache_t]
    return pl.pallas_call(
        body,
        grid_spec=pltpu.PrefetchScalarGridSpec(
            num_scalar_prefetch=2,
            grid=(1 if again else rows,),
            in_specs=[
                pl.BlockSpec((1, entries, steps), lambda r, ids, _: (slot(r, ids), 0, 0)),
                pl.BlockSpec(
                    (steps, 1, entries, all_heads), lambda r, ids, _: (0, slot(r, ids), 0, 0)
                ),
            ]
            + extra_specs,
            out_specs=pl.BlockSpec(
                (chips, 1, 1, 2 * steps * heads, latent_width),
                lambda r, ids, _: (
                    0,
                    lax.div(slot(r, ids), rows // 2),
                    lax.rem(slot(r, ids), rows // 2),
                    0,
                    0,
                ),
            ),
        ),
        out_shape=jax.ShapeDtypeStruct(
            (chips, 2, rows // 2, 2 * steps * heads, latent_width), bf16
        ),
        input_output_aliases={5: 0} if again else {},
        compiler_params=params(60),
        name="again" if again else "attend",
    )(ids, lengths, fresh_t, queries_t, *extra)


def project(ids, rows, weight, blocks):
    groups, count, depth = rows.shape
    width = weight.shape[1] // blocks

    def body(ids_ref, rows_ref, weight_ref, out_ref):
        lhs = rows_ref[...].reshape(groups * count, depth)
        total = jnp.dot(lhs, weight_ref[...], preferred_element_type=f32)
        out_ref[:, 0] = total.astype(bf16).reshape(groups, count, width)

    return pl.pallas_call(
        body,
        grid_spec=pltpu.PrefetchScalarGridSpec(
            num_scalar_prefetch=1,
            grid=(blocks,),
            in_specs=[
                whole(rows.shape),
                pl.BlockSpec((depth, width), lambda k, ids: (0, k)),
            ],
            out_specs=pl.BlockSpec(
                (groups, 1, count, width), lambda k, ids: (0, lax.rem(ids[1] + k, blocks), 0, 0)
            ),
        ),
        out_shape=jax.ShapeDtypeStruct((groups, blocks, count, width), bf16),
        compiler_params=params(40),
        name="project",
    )(ids, rows, weight)


def fetches(refs, blocks, weight_ref, sems):
    copies, n, left = [], 0, 0
    for column in blocks:
        top = 0
        for w in column:
            at = weight_ref.at[pl.ds(top, w.shape[0]), pl.ds(left, w.shape[1])]
            copies.append(pltpu.make_async_copy(refs[n], at, sems.at[n]))
            n, top = n + 1, top + w.shape[0]
        left += column[0].shape[1]
    return copies


def combine(ids, rows, blocks):
    groups, count, depth = rows.shape
    width = blocks[0][0].shape[1]
    flat = [w for column in blocks for w in column]
    half = len(flat) // 2

    def body(ids_ref, rows_ref, *refs):
        out_ref, weight_ref, sems = refs[len(flat) :]
        copies = fetches(refs, blocks, weight_ref, sems)
        for copy in copies:
            copy.start()
        lhs = rows_ref[...].reshape(groups * count, depth)
        for k in range(2):
            for copy in copies[k * half : (k + 1) * half]:
                copy.wait()
            total = jnp.dot(
                lhs, weight_ref[:, k * width : (k + 1) * width], preferred_element_type=f32
            )
            at = lax.rem(ids_ref[1] + k, 2)
            out_ref[:, at] = total.astype(bf16).reshape(groups, count, width)

    return pl.pallas_call(
        body,
        grid_spec=pltpu.PrefetchScalarGridSpec(
            num_scalar_prefetch=1,
            grid=(1,),
            in_specs=[whole(rows.shape)] + [pl.BlockSpec(memory_space=pl.ANY) for _ in flat],
            out_specs=whole((groups, 2, count, width)),
            scratch_shapes=[
                pltpu.VMEM((depth, 2 * width), bf16),
                pltpu.SemaphoreType.DMA((len(flat),)),
            ],
        ),
        out_shape=jax.ShapeDtypeStruct((groups, 2, count, width), bf16),
        compiler_params=params(60),
        name="combine",
    )(ids, rows, *flat)


def widen(ids, rows, weight):
    halves, chunks, blocks, count, features = rows.shape
    depth, columns = weight.shape
    every = halves * chunks * count

    def body(ids_ref, rows_ref, weight_ref, out_ref, lhs_ref):
        tile = pl.program_id(0)

        def put(at, value):
            value = value.astype(bf16).reshape(halves, chunks, count, value.shape[1])
            for h in range(halves):
                out_ref[:, h, :, at] = value[h]

        @pl.when(tile == 0)
        def _():
            squares = jnp.zeros((every, 1), f32)
            for k in range(blocks):
                block = rows_ref[:, :, lax.rem(ids_ref[1] + k, blocks)].reshape(every, features)
                lhs_ref[:, k * features : (k + 1) * features] = block
                wide = block.astype(f32)
                squares += jnp.sum(wide * wide, axis=1, keepdims=True)
            high = squares.astype(bf16).astype(f32)
            lane = lax.broadcasted_iota(jnp.int32, (every, 128), 1)
            extra = jnp.where(lane == 0, high, jnp.where(lane == 1, squares - high, 0.0))
            put(slice(columns, columns + 128), extra)

        total = jnp.dot(lhs_ref[...], weight_ref[...], preferred_element_type=f32)
        put(pl.ds(pl.multiple_of(tile * TILE, 128), TILE), total)

    return pl.pallas_call(
        body,
        grid_spec=pltpu.PrefetchScalarGridSpec(
            num_scalar_prefetch=1,
            grid=(columns // TILE,),
            in_specs=[
                whole(rows.shape),
                pl.BlockSpec((depth, TILE), lambda k, ids: (0, k)),
            ],
            out_specs=whole((chunks, halves, count, columns + 128)),
            scratch_shapes=[pltpu.VMEM((every, depth), bf16)],
        ),
        out_shape=jax.ShapeDtypeStruct((chunks, halves, count, columns + 128), bf16),
        compiler_params=params(40),
        name="widen",
    )(ids, rows, weight)


def local(
    cache,
    cache_length,
    move_slot,
    move_peer,
    queries,
    new_latent,
    value_up,
    out_proj,
    residual,
    norm_gain,
    gate_weight,
    up_weight,
    down_weight,
):
    member = lax.axis_index(TP)
    core = lax.axis_index("c")
    pair = lax.axis_index("xl")
    steps = new_latent.shape[0]
    heads, latent_width, value_width = value_up.shape
    rows_out = residual.shape[1] // N_TP
    chunk = rows_out * steps
    count = chunk // 2
    features, units = gate_weight.shape

    def by_pair(mine, other):
        first = pair == 0
        return jnp.stack([jnp.where(first, mine, other), jnp.where(first, other, mine)])

    def at_pair(blocks):
        return lax.dynamic_index_in_dim(blocks, pair, 0, False)

    def at_other(blocks):
        return lax.dynamic_index_in_dim(blocks, 1 - pair, 0, False)

    out_came = swap(out_proj, "xl")
    value_ups = jnp.concatenate([value_up, swap(value_up, "c")], axis=0)
    lanes = jnp.arange(N_TP, dtype=jnp.int32)
    own_slot = jnp.sum(jnp.where(lanes == member, move_slot[0], 0))
    ids = jnp.stack([own_slot, pair]).astype(jnp.int32)
    cache_t = cache.transpose(0, 2, 1)
    pieces = exchange(leave(move_slot[0], cache_t), TP)
    pieces, gate_weight, up_weight = lax.optimization_barrier((pieces, gate_weight, up_weight))

    gain = norm_gain.astype(f32)[:, None]

    def scaled(low, high, first, second):
        weight = jnp.where(pair == 0, first[low:high], second[low:high])
        return (weight.astype(f32) * gain[low:high]).astype(bf16)

    kept = scaled(0, features, gate_weight, up_weight)
    sent = scaled(0, CUT, up_weight, gate_weight)
    arrived = exchange(route(move_peer[0], pieces), TP)
    arrived, kept, sent, value_ups = lax.optimization_barrier((arrived, kept, sent, value_ups))
    fresh_t = new_latent.transpose(1, 2, 0)
    queries_t = queries.transpose(0, 1, 3, 2)
    out = attend(ids, cache_length, cache_t, fresh_t, queries_t, heads, latent_width)
    out = attend(
        ids, cache_length, cache_t, fresh_t, queries_t, heads, latent_width, arrived, out
    )
    out, out_came, out_proj, down_weight = lax.optimization_barrier(
        (out, out_came, out_proj, down_weight)
    )
    came = [swap(sent, "xl")]
    out_near = swap(out_proj, "c")
    out_weights = [[out_proj, out_near], [out_came, swap(out_came, "c")]]
    out = out.reshape((N_TP,) + out.shape[2:])
    by_head = exchange(out, TP).reshape(-1, 2 * heads, latent_width)

    downs = jnp.concatenate([down_weight, swap(down_weight, "c")], axis=0)
    out_weights[0][1], gate_weight, up_weight, residual = lax.optimization_barrier(
        (out_near, gate_weight, up_weight, residual)
    )
    sent = scaled(CUT, features, up_weight, gate_weight)
    residue = lax.dynamic_slice_in_dim(residual, lax.div(member, 2) * 2 * rows_out, 2 * rows_out, 1)
    residue = residue.reshape(steps, 2, 2, rows_out // 8, 2, 2, features)
    residue = lax.dynamic_index_in_dim(residue, core, 4, False)
    residue = residue.transpose(2, 1, 3, 4, 0, 5).reshape(2, count, features)
    residue = [at_pair(residue), at_other(residue)]
    by_head, kept, came, sent, downs, residue, out_weights = lax.optimization_barrier(
        (by_head, kept, came, sent, downs, residue, out_weights)
    )
    value_heads = jnp.einsum(
        "thl,hlv->thv", by_head, value_ups, preferred_element_type=f32
    ).astype(bf16)

    value_heads = value_heads.reshape(2, 2, count // 2, 2 * heads * value_width)
    value_heads = value_heads.transpose(1, 0, 2, 3).reshape(2, count, -1)
    value_heads = jnp.broadcast_to(
        value_heads[None, :, None], (2, 2, 2) + value_heads.shape[1:]
    ).reshape((N_DP,) + value_heads.shape[1:])
    gathered = exchange(value_heads, DP)
    gathered, sent, kept, residue = lax.optimization_barrier((gathered, sent, kept, residue))
    came.append(swap(sent, "xl"))
    residue[1] = swap(residue[1], "xl")
    parts = exchange(combine(ids, gathered, out_weights), ZY)
    parts, came, kept, residue = lax.optimization_barrier((parts, came, kept, residue))
    kept = [kept, swap(kept, "c")]
    in_weight = jnp.concatenate(
        [
            jnp.concatenate([own, swap(own, "c") if k else kept[1]], axis=1)
            for k, own in enumerate([kept[0]] + came)
        ],
        axis=0,
    )
    hidden = by_pair(*residue).astype(f32) + jnp.sum(parts.astype(f32), axis=0)

    rows = spread(hidden.astype(bf16), PAIR, 2 * N_ZY).reshape((2, N_ZY) + hidden.shape)
    near = swap(at_other(hidden), "xl")
    near, in_weight = lax.optimization_barrier((near, in_weight))
    rows, near = lax.optimization_barrier((rows, near))
    sums = exchange(widen(ids, rows, in_weight).reshape(N_DP, chunk, -1), DP)
    sums = jnp.sum(sums.reshape(2, 2, 2, chunk, -1).astype(f32), axis=(0, 2))
    squares = sums[0, :, 2 * units] + sums[0, :, 2 * units + 1]
    inverse = lax.rsqrt(squares / D + norm_eps)[:, None]
    active = sums[:, :, : 2 * units] * inverse
    active = (jax.nn.silu(active[0]) * active[1]).astype(bf16)
    parts = exchange(project(ids, spread(active, DP, N_DP), downs, 1)[:, 0], ZY)
    hidden = by_pair(at_pair(hidden), near).reshape(chunk, -1)
    result = (hidden + jnp.sum(parts.astype(f32), axis=0)).astype(bf16)

    result = result.reshape(2, 2, rows_out // 8, 2, steps, features)
    mine = lax.dynamic_index_in_dim(result, core, 1, False)
    near = swap(lax.dynamic_index_in_dim(result, 1 - core, 1, False), "c")
    first = core == 0
    result = jnp.stack([jnp.where(first, mine, near), jnp.where(first, near, mine)])
    return result.transpose(4, 1, 2, 0, 3, 5).reshape(steps, rows_out, features)


def solution(mesh):
    split = Mesh(
        mesh.devices.reshape(2, 2, 2, 2, 4, 2), ("xh", "xl", "zl", "zh", "y", "c")
    )
    in_specs = (
        P(DP + TP, None, None),
        P(DP + TP),
        P(DP, None),
        P(DP, None),
        P(None, DP + TP, None, None),
        P(None, DP + TP, None),
        P(TP, None, None),
        P(TP, DP),
        P(None, None, DP),
        P(DP),
        P(DP, TP),
        P(DP, TP),
        P(TP, DP),
    )
    out_specs = P(None, TP, DP)
    return jax.shard_map(local, mesh=split, in_specs=in_specs, out_specs=out_specs, check_vma=False)
```

```python
import jax
import jax.numpy as jnp
from jax import lax
from jax.experimental import pallas as pl
from jax.experimental.pallas import tpu as pltpu
from jax.sharding import Mesh, PartitionSpec as P

D = 7168
QKD = 192
norm_eps = 1e-06

DP = ("xh", "xl", "zl")
TP = ("zh", "y", "c")
ZY = ("zh", "y")
PAIR = ("xl",) + ZY
N_DP = 8
N_TP = 16
N_ZY = 8
SWAP = [(0, 1), (1, 0)]
CUT = 384
TILE = 768
bf16 = jnp.bfloat16
f32 = jnp.float32
MIB = 1024 * 1024


def exchange(blocks, axes):
    return lax.all_to_all(blocks, axes, 0, 0, tiled=True)


def spread(block, axes, copies):
    return exchange(jnp.broadcast_to(block[None], (copies,) + block.shape), axes)


def swap(block, axis):
    return lax.ppermute(block, axis, SWAP)


def params(mib):
    return pltpu.CompilerParams(vmem_limit_bytes=mib * MIB)


def whole(shape):
    return pl.BlockSpec(shape, lambda *_: (0,) * len(shape))


def leave(slots, cache_t):
    _, entries, length = cache_t.shape
    piece = entries // N_TP

    def body(slots_ref, cache_ref, out_ref, row_ref, sem):
        slot = slots_ref[lax.axis_index(TP)]
        copy = pltpu.make_async_copy(cache_ref.at[slot], row_ref, sem)
        copy.start()
        copy.wait()
        row = row_ref[...].astype(f32)
        for j in range(N_TP):
            out_ref[j] = row[j * piece : (j + 1) * piece].astype(bf16)

    return pl.pallas_call(
        body,
        grid_spec=pltpu.PrefetchScalarGridSpec(
            num_scalar_prefetch=1,
            grid=(1,),
            in_specs=[pl.BlockSpec(memory_space=pl.ANY)],
            out_specs=whole((N_TP, piece, length)),
            scratch_shapes=[pltpu.VMEM((entries, length), bf16), pltpu.SemaphoreType.DMA],
        ),
        out_shape=jax.ShapeDtypeStruct((N_TP, piece, length), bf16),
        compiler_params=params(60),
        name="leave",
    )(slots, cache_t)


def route(peer, pieces):
    def body(peer_ref, in_ref, out_ref):
        for i in range(N_TP):
            out_ref[peer_ref[i]] = in_ref[i]

    return pl.pallas_call(
        body,
        grid_spec=pltpu.PrefetchScalarGridSpec(
            num_scalar_prefetch=1,
            grid=(1,),
            in_specs=[whole(pieces.shape)],
            out_specs=whole(pieces.shape),
        ),
        out_shape=jax.ShapeDtypeStruct(pieces.shape, bf16),
        compiler_params=params(40),
        name="route",
    )(peer, pieces)


def attend(ids, lengths, cache_t, fresh_t, queries_t, heads, latent_width, arrived=None, done=None):
    rows, entries, length = cache_t.shape
    steps, _, _, all_heads = queries_t.shape
    chips = all_heads // (2 * heads)
    again = arrived is not None

    def slot(r, ids):
        return ids[0] if again else r

    def body(ids_ref, lengths_ref, fresh_ref, q_ref, *refs):
        out_ref = refs[-1]
        row = slot(pl.program_id(0), ids_ref)
        current = lengths_ref[row]
        if again:
            latents = jnp.concatenate([refs[0][j].astype(f32) for j in range(N_TP)], axis=0)
        else:
            latents = refs[0][0].astype(f32)
        position = lax.broadcasted_iota(jnp.int32, (entries, length), 1)
        for s in range(steps):
            token = fresh_ref[0, :, s : s + 1].astype(f32)
            latents = jnp.where(position == current + s, token, latents)
        latents = latents.astype(bf16)
        place = lax.broadcasted_iota(jnp.int32, (all_heads, length), 1)
        outs = []
        for s in range(steps):
            scores = lax.dot_general(
                q_ref[s, 0], latents, (((0,), (0,)), ((), ())), preferred_element_type=f32
            )
            scores = jnp.where(place <= current + s, scores * QKD ** (-0.5), -jnp.inf)
            expo = jnp.exp(scores - jnp.max(scores, axis=-1, keepdims=True))
            probs = (expo / jnp.sum(expo, axis=-1, keepdims=True)).astype(bf16)
            out = lax.dot_general(
                probs, latents[:latent_width], (((1,), (1,)), ((), ())), preferred_element_type=f32
            )
            out = out.reshape(chips, 2, heads, latent_width)
            turned = jnp.concatenate([out[:, 1:], out[:, :1]], axis=1)
            out = jnp.where(row >= rows // 2, turned, out)
            outs.append(out.reshape(chips, 2 * heads, latent_width))
        out_ref[:, 0, 0] = jnp.concatenate(outs, axis=1).astype(bf16)

    if again:
        extra_specs = [whole(arrived.shape), pl.BlockSpec(memory_space=pl.ANY)]
        extra = [arrived, done]
    else:
        extra_specs = [pl.BlockSpec((1, entries, length), lambda r, *_: (r, 0, 0))]
        extra = [cache_t]
    return pl.pallas_call(
        body,
        grid_spec=pltpu.PrefetchScalarGridSpec(
            num_scalar_prefetch=2,
            grid=(1 if again else rows,),
            in_specs=[
                pl.BlockSpec((1, entries, steps), lambda r, ids, _: (slot(r, ids), 0, 0)),
                pl.BlockSpec(
                    (steps, 1, entries, all_heads), lambda r, ids, _: (0, slot(r, ids), 0, 0)
                ),
            ]
            + extra_specs,
            out_specs=pl.BlockSpec(
                (chips, 1, 1, 2 * steps * heads, latent_width),
                lambda r, ids, _: (
                    0,
                    lax.div(slot(r, ids), rows // 2),
                    lax.rem(slot(r, ids), rows // 2),
                    0,
                    0,
                ),
            ),
        ),
        out_shape=jax.ShapeDtypeStruct(
            (chips, 2, rows // 2, 2 * steps * heads, latent_width), bf16
        ),
        input_output_aliases={5: 0} if again else {},
        compiler_params=params(60),
        name="again" if again else "attend",
    )(ids, lengths, fresh_t, queries_t, *extra)


def project(ids, rows, weight, blocks):
    groups, count, depth = rows.shape
    width = weight.shape[1] // blocks

    def body(ids_ref, rows_ref, weight_ref, out_ref):
        lhs = rows_ref[...].reshape(groups * count, depth)
        total = jnp.dot(lhs, weight_ref[...], preferred_element_type=f32)
        out_ref[:, 0] = total.astype(bf16).reshape(groups, count, width)

    return pl.pallas_call(
        body,
        grid_spec=pltpu.PrefetchScalarGridSpec(
            num_scalar_prefetch=1,
            grid=(blocks,),
            in_specs=[
                whole(rows.shape),
                pl.BlockSpec((depth, width), lambda k, ids: (0, k)),
            ],
            out_specs=pl.BlockSpec(
                (groups, 1, count, width), lambda k, ids: (0, lax.rem(ids[1] + k, blocks), 0, 0)
            ),
        ),
        out_shape=jax.ShapeDtypeStruct((groups, blocks, count, width), bf16),
        compiler_params=params(40),
        name="project",
    )(ids, rows, weight)


def fetches(refs, blocks, weight_ref, sems):
    copies, n, left = [], 0, 0
    for column in blocks:
        top = 0
        for w in column:
            at = weight_ref.at[pl.ds(top, w.shape[0]), pl.ds(left, w.shape[1])]
            copies.append(pltpu.make_async_copy(refs[n], at, sems.at[n]))
            n, top = n + 1, top + w.shape[0]
        left += column[0].shape[1]
    return copies


def join(blocks):
    flat = [w for column in blocks for w in column]
    depth = sum(w.shape[0] for w in blocks[0])
    width = sum(column[0].shape[1] for column in blocks)

    def body(*refs):
        out_ref, sems = refs[len(flat) :]
        copies = fetches(refs, blocks, out_ref, sems)
        for copy in copies:
            copy.start()
        for copy in copies:
            copy.wait()

    return pl.pallas_call(
        body,
        in_specs=[pl.BlockSpec(memory_space=pl.ANY) for _ in flat],
        out_specs=pl.BlockSpec(memory_space=pl.ANY),
        scratch_shapes=[pltpu.SemaphoreType.DMA((len(flat),))],
        out_shape=jax.ShapeDtypeStruct((depth, width), bf16),
        compiler_params=params(8),
        name="join",
    )(*flat)


def combine(ids, rows, blocks):
    groups, count, depth = rows.shape
    width = blocks[0][0].shape[1]
    flat = [w for column in blocks for w in column]

    def body(ids_ref, rows_ref, *refs):
        out_ref, weight_ref, sems = refs[len(flat) :]
        copies = fetches(refs, blocks, weight_ref, sems)
        for copy in copies:
            copy.start()
        lhs = rows_ref[...].reshape(groups * count, depth)
        n = 0
        for k in range(2):
            total, top = 0.0, 0
            for w in blocks[k]:
                end = top + w.shape[0]
                copies[n].wait()
                total += jnp.dot(
                    lhs[:, top:end],
                    weight_ref[top:end, k * width : (k + 1) * width],
                    preferred_element_type=f32,
                )
                n, top = n + 1, end
            at = lax.rem(ids_ref[1] + k, 2)
            out_ref[:, at] = total.astype(bf16).reshape(groups, count, width)

    return pl.pallas_call(
        body,
        grid_spec=pltpu.PrefetchScalarGridSpec(
            num_scalar_prefetch=1,
            grid=(1,),
            in_specs=[whole(rows.shape)] + [pl.BlockSpec(memory_space=pl.ANY) for _ in flat],
            out_specs=whole((groups, 2, count, width)),
            scratch_shapes=[
                pltpu.VMEM((depth, 2 * width), bf16),
                pltpu.SemaphoreType.DMA((len(flat),)),
            ],
        ),
        out_shape=jax.ShapeDtypeStruct((groups, 2, count, width), bf16),
        compiler_params=params(60),
        name="combine",
    )(ids, rows, *flat)


def widen(ids, rows, weight):
    halves, chunks, blocks, count, features = rows.shape
    depth, columns = weight.shape
    every = halves * chunks * count

    def body(ids_ref, rows_ref, weight_ref, out_ref, lhs_ref):
        tile = pl.program_id(0)

        def put(at, value):
            value = value.astype(bf16).reshape(halves, chunks, count, value.shape[1])
            for h in range(halves):
                out_ref[:, h, :, at] = value[h]

        @pl.when(tile == 0)
        def _():
            squares = jnp.zeros((every, 1), f32)
            for k in range(blocks):
                block = rows_ref[:, :, lax.rem(ids_ref[1] + k, blocks)].reshape(every, features)
                lhs_ref[:, k * features : (k + 1) * features] = block
                wide = block.astype(f32)
                squares += jnp.sum(wide * wide, axis=1, keepdims=True)
            high = squares.astype(bf16).astype(f32)
            lane = lax.broadcasted_iota(jnp.int32, (every, 128), 1)
            extra = jnp.where(lane == 0, high, jnp.where(lane == 1, squares - high, 0.0))
            put(slice(columns, columns + 128), extra)

        total = jnp.dot(lhs_ref[...], weight_ref[...], preferred_element_type=f32)
        put(pl.ds(pl.multiple_of(tile * TILE, 128), TILE), total)

    return pl.pallas_call(
        body,
        grid_spec=pltpu.PrefetchScalarGridSpec(
            num_scalar_prefetch=1,
            grid=(columns // TILE,),
            in_specs=[
                whole(rows.shape),
                pl.BlockSpec((depth, TILE), lambda k, ids: (0, k)),
            ],
            out_specs=whole((chunks, halves, count, columns + 128)),
            scratch_shapes=[pltpu.VMEM((every, depth), bf16)],
        ),
        out_shape=jax.ShapeDtypeStruct((chunks, halves, count, columns + 128), bf16),
        compiler_params=params(51),
        name="widen",
    )(ids, rows, weight)


def local(
    cache,
    cache_length,
    move_slot,
    move_peer,
    queries,
    new_latent,
    value_up,
    out_proj,
    residual,
    norm_gain,
    gate_weight,
    up_weight,
    down_weight,
):
    member = lax.axis_index(TP)
    core = lax.axis_index("c")
    pair = lax.axis_index("xl")
    steps = new_latent.shape[0]
    heads, latent_width, value_width = value_up.shape
    rows_out = residual.shape[1] // N_TP
    chunk = rows_out * steps
    count = chunk // 2
    features, units = gate_weight.shape

    def by_pair(mine, other):
        first = pair == 0
        return jnp.stack([jnp.where(first, mine, other), jnp.where(first, other, mine)])

    def at_pair(blocks):
        return lax.dynamic_index_in_dim(blocks, pair, 0, False)

    def at_other(blocks):
        return lax.dynamic_index_in_dim(blocks, 1 - pair, 0, False)

    out_came = swap(out_proj, "xl")
    value_ups = jnp.concatenate([value_up, swap(value_up, "c")], axis=0)
    lanes = jnp.arange(N_TP, dtype=jnp.int32)
    own_slot = jnp.sum(jnp.where(lanes == member, move_slot[0], 0))
    ids = jnp.stack([own_slot, pair]).astype(jnp.int32)
    cache_t = cache.transpose(0, 2, 1)
    pieces = exchange(leave(move_slot[0], cache_t), TP)
    pieces, gate_weight, up_weight = lax.optimization_barrier((pieces, gate_weight, up_weight))

    gain = norm_gain.astype(f32)[:, None]

    def scaled(low, high, first, second):
        weight = jnp.where(pair == 0, first[low:high], second[low:high])
        return (weight.astype(f32) * gain[low:high]).astype(bf16)

    kept = scaled(0, features, gate_weight, up_weight)
    sent = scaled(0, CUT, up_weight, gate_weight)
    arrived = exchange(route(move_peer[0], pieces), TP)
    arrived, kept, sent, value_ups = lax.optimization_barrier((arrived, kept, sent, value_ups))
    fresh_t = new_latent.transpose(1, 2, 0)
    queries_t = queries.transpose(0, 1, 3, 2)
    out = attend(ids, cache_length, cache_t, fresh_t, queries_t, heads, latent_width)
    out = attend(
        ids, cache_length, cache_t, fresh_t, queries_t, heads, latent_width, arrived, out
    )
    out, out_came, out_proj, down_weight = lax.optimization_barrier(
        (out, out_came, out_proj, down_weight)
    )
    came = [swap(sent, "xl")]
    out_near = swap(out_proj, "c")
    out_weights = [[out_proj, out_near], [out_came, swap(out_came, "c")]]
    out = out.reshape((N_TP,) + out.shape[2:])
    by_head = exchange(out, TP).reshape(-1, 2 * heads, latent_width)

    downs = jnp.concatenate([down_weight, swap(down_weight, "c")], axis=0)
    out_weights[0][1], gate_weight, up_weight, residual = lax.optimization_barrier(
        (out_near, gate_weight, up_weight, residual)
    )
    sent = scaled(CUT, features, up_weight, gate_weight)
    residue = lax.dynamic_slice_in_dim(residual, lax.div(member, 2) * 2 * rows_out, 2 * rows_out, 1)
    residue = residue.reshape(steps, 2, 2, rows_out // 8, 2, 2, features)
    residue = lax.dynamic_index_in_dim(residue, core, 4, False)
    residue = residue.transpose(2, 1, 3, 4, 0, 5).reshape(2, count, features)
    residue = [at_pair(residue), at_other(residue)]
    by_head, kept, came, sent, downs, residue, out_weights = lax.optimization_barrier(
        (by_head, kept, came, sent, downs, residue, out_weights)
    )
    value_heads = jnp.einsum(
        "thl,hlv->thv", by_head, value_ups, preferred_element_type=f32
    ).astype(bf16)

    value_heads = value_heads.reshape(2, 2, count // 2, 2 * heads * value_width)
    value_heads = value_heads.transpose(1, 0, 2, 3).reshape(2, count, -1)
    value_heads = jnp.broadcast_to(
        value_heads[None, :, None], (2, 2, 2) + value_heads.shape[1:]
    ).reshape((N_DP,) + value_heads.shape[1:])
    gathered = exchange(value_heads, DP)
    gathered, sent, kept, residue = lax.optimization_barrier((gathered, sent, kept, residue))
    came.append(swap(sent, "xl"))
    residue[1] = swap(residue[1], "xl")
    parts = exchange(combine(ids, gathered, out_weights), ZY)
    parts, came, kept, residue = lax.optimization_barrier((parts, came, kept, residue))
    kept = [kept, swap(kept, "c")]
    in_weight = join([[kept[0]] + came, [kept[1]] + [swap(w, "c") for w in came]])
    hidden = by_pair(*residue).astype(f32) + jnp.sum(parts.astype(f32), axis=0)

    rows = spread(hidden.astype(bf16), PAIR, 2 * N_ZY).reshape((2, N_ZY) + hidden.shape)
    near = swap(at_other(hidden), "xl")
    hidden = by_pair(at_pair(hidden), near).reshape(chunk, -1)
    hidden, in_weight = lax.optimization_barrier((hidden, in_weight))
    rows, hidden = lax.optimization_barrier((rows, hidden))
    sums = exchange(widen(ids, rows, in_weight).reshape(N_DP, chunk, -1), DP)
    sums = jnp.sum(sums.reshape(2, 2, 2, chunk, -1).astype(f32), axis=(0, 2))
    squares = sums[0, :, 2 * units] + sums[0, :, 2 * units + 1]
    inverse = lax.rsqrt(squares / D + norm_eps)[:, None]
    active = sums[:, :, : 2 * units] * inverse
    active = (jax.nn.silu(active[0]) * active[1]).astype(bf16)
    parts = exchange(project(ids, spread(active, DP, N_DP), downs, 1)[:, 0], ZY)
    result = (hidden + jnp.sum(parts.astype(f32), axis=0)).astype(bf16)

    result = result.reshape(2, 2, rows_out // 8, 2, steps, features)
    mine = lax.dynamic_index_in_dim(result, core, 1, False)
    near = swap(lax.dynamic_index_in_dim(result, 1 - core, 1, False), "c")
    first = core == 0
    result = jnp.stack([jnp.where(first, mine, near), jnp.where(first, near, mine)])
    return result.transpose(4, 1, 2, 0, 3, 5).reshape(steps, rows_out, features)


def solution(mesh):
    split = Mesh(
        mesh.devices.reshape(2, 2, 2, 2, 4, 2), ("xh", "xl", "zl", "zh", "y", "c")
    )
    in_specs = (
        P(DP + TP, None, None),
        P(DP + TP),
        P(DP, None),
        P(DP, None),
        P(None, DP + TP, None, None),
        P(None, DP + TP, None),
        P(TP, None, None),
        P(TP, DP),
        P(None, None, DP),
        P(DP),
        P(DP, TP),
        P(DP, TP),
        P(TP, DP),
    )
    out_specs = P(None, TP, DP)
    return jax.shard_map(local, mesh=split, in_specs=in_specs, out_specs=out_specs, check_vma=False)
```

```python
import jax
import jax.numpy as jnp
from jax import lax
from jax.experimental import pallas as pl
from jax.experimental.pallas import tpu as pltpu
from jax.sharding import Mesh, PartitionSpec as P

D = 7168
QKD = 192
norm_eps = 1e-06

DP = ("xh", "xl", "zl")
TP = ("zh", "y", "c")
ZY = ("zh", "y")
PAIR = ("xl",) + ZY
N_DP = 8
N_TP = 16
N_ZY = 8
SWAP = [(0, 1), (1, 0)]
CUT = 384
TILE = 768
bf16 = jnp.bfloat16
f32 = jnp.float32
MIB = 1024 * 1024


def exchange(blocks, axes):
    return lax.all_to_all(blocks, axes, 0, 0, tiled=True)


def spread(block, axes, copies):
    return exchange(jnp.broadcast_to(block[None], (copies,) + block.shape), axes)


def swap(block, axis):
    return lax.ppermute(block, axis, SWAP)


def params(mib):
    return pltpu.CompilerParams(vmem_limit_bytes=mib * MIB)


def whole(shape):
    return pl.BlockSpec(shape, lambda *_: (0,) * len(shape))


def leave(slots, cache_t):
    _, entries, length = cache_t.shape
    tall, wide = 2 * entries // N_TP, length // 2

    def body(slots_ref, cache_ref, out_ref, row_ref, sem):
        slot = slots_ref[lax.axis_index(TP)]
        copy = pltpu.make_async_copy(cache_ref.at[slot], row_ref, sem)
        copy.start()
        copy.wait()
        row = row_ref[...].astype(f32)
        for j in range(N_TP):
            top, left = j // 2 * tall, j % 2 * wide
            out_ref[j] = row[top : top + tall, left : left + wide].astype(bf16)

    return pl.pallas_call(
        body,
        grid_spec=pltpu.PrefetchScalarGridSpec(
            num_scalar_prefetch=1,
            grid=(1,),
            in_specs=[pl.BlockSpec(memory_space=pl.ANY)],
            out_specs=whole((N_TP, tall, wide)),
            scratch_shapes=[pltpu.VMEM((entries, length), bf16), pltpu.SemaphoreType.DMA],
        ),
        out_shape=jax.ShapeDtypeStruct((N_TP, tall, wide), bf16),
        compiler_params=params(60),
        name="leave",
    )(slots, cache_t)


def route(peer, pieces):
    def body(peer_ref, in_ref, out_ref):
        for i in range(N_TP):
            out_ref[peer_ref[i]] = in_ref[i]

    return pl.pallas_call(
        body,
        grid_spec=pltpu.PrefetchScalarGridSpec(
            num_scalar_prefetch=1,
            grid=(1,),
            in_specs=[whole(pieces.shape)],
            out_specs=whole(pieces.shape),
        ),
        out_shape=jax.ShapeDtypeStruct(pieces.shape, bf16),
        compiler_params=params(40),
        name="route",
    )(peer, pieces)


def attend(ids, lengths, cache_t, fresh_t, queries_t, heads, latent_width, arrived=None, done=None):
    rows, entries, length = cache_t.shape
    steps, _, _, all_heads = queries_t.shape
    chips = all_heads // (2 * heads)
    again = arrived is not None

    def slot(r, ids):
        return ids[0] if again else r

    def body(ids_ref, lengths_ref, fresh_ref, q_ref, *refs):
        out_ref = refs[-1]
        row = slot(pl.program_id(0), ids_ref)
        current = lengths_ref[row]
        if again:
            latents = [
                jnp.concatenate([refs[0][j + b].astype(f32) for b in range(2)], axis=1)
                for j in range(0, N_TP, 2)
            ]
            latents = jnp.concatenate(latents, axis=0)
        else:
            latents = refs[0][0].astype(f32)
        position = lax.broadcasted_iota(jnp.int32, (entries, length), 1)
        for s in range(steps):
            token = fresh_ref[0, :, s : s + 1].astype(f32)
            latents = jnp.where(position == current + s, token, latents)
        latents = latents.astype(bf16)
        place = lax.broadcasted_iota(jnp.int32, (all_heads, length), 1)
        outs = []
        for s in range(steps):
            scores = lax.dot_general(
                q_ref[s, 0], latents, (((0,), (0,)), ((), ())), preferred_element_type=f32
            )
            scores = jnp.where(place <= current + s, scores * QKD ** (-0.5), -jnp.inf)
            expo = jnp.exp(scores - jnp.max(scores, axis=-1, keepdims=True))
            probs = (expo / jnp.sum(expo, axis=-1, keepdims=True)).astype(bf16)
            out = lax.dot_general(
                probs, latents[:latent_width], (((1,), (1,)), ((), ())), preferred_element_type=f32
            )
            out = out.reshape(chips, 2, heads, latent_width)
            turned = jnp.concatenate([out[:, 1:], out[:, :1]], axis=1)
            out = jnp.where(row >= rows // 2, turned, out)
            outs.append(out.reshape(chips, 2 * heads, latent_width))
        out_ref[:, 0, 0] = jnp.concatenate(outs, axis=1).astype(bf16)

    if again:
        extra_specs = [whole(arrived.shape), pl.BlockSpec(memory_space=pl.ANY)]
        extra = [arrived, done]
    else:
        extra_specs = [pl.BlockSpec((1, entries, length), lambda r, *_: (r, 0, 0))]
        extra = [cache_t]
    return pl.pallas_call(
        body,
        grid_spec=pltpu.PrefetchScalarGridSpec(
            num_scalar_prefetch=2,
            grid=(1 if again else rows,),
            in_specs=[
                pl.BlockSpec((1, entries, steps), lambda r, ids, _: (slot(r, ids), 0, 0)),
                pl.BlockSpec(
                    (steps, 1, entries, all_heads), lambda r, ids, _: (0, slot(r, ids), 0, 0)
                ),
            ]
            + extra_specs,
            out_specs=pl.BlockSpec(
                (chips, 1, 1, 2 * steps * heads, latent_width),
                lambda r, ids, _: (
                    0,
                    lax.div(slot(r, ids), rows // 2),
                    lax.rem(slot(r, ids), rows // 2),
                    0,
                    0,
                ),
            ),
        ),
        out_shape=jax.ShapeDtypeStruct(
            (chips, 2, rows // 2, 2 * steps * heads, latent_width), bf16
        ),
        input_output_aliases={5: 0} if again else {},
        compiler_params=params(60),
        name="again" if again else "attend",
    )(ids, lengths, fresh_t, queries_t, *extra)


def project(ids, rows, weight, blocks):
    groups, count, depth = rows.shape
    width = weight.shape[1] // blocks

    def body(ids_ref, rows_ref, weight_ref, out_ref):
        lhs = rows_ref[...].reshape(groups * count, depth)
        total = jnp.dot(lhs, weight_ref[...], preferred_element_type=f32)
        out_ref[:, 0] = total.astype(bf16).reshape(groups, count, width)

    return pl.pallas_call(
        body,
        grid_spec=pltpu.PrefetchScalarGridSpec(
            num_scalar_prefetch=1,
            grid=(blocks,),
            in_specs=[
                whole(rows.shape),
                pl.BlockSpec((depth, width), lambda k, ids: (0, k)),
            ],
            out_specs=pl.BlockSpec(
                (groups, 1, count, width), lambda k, ids: (0, lax.rem(ids[1] + k, blocks), 0, 0)
            ),
        ),
        out_shape=jax.ShapeDtypeStruct((groups, blocks, count, width), bf16),
        compiler_params=params(40),
        name="project",
    )(ids, rows, weight)


def fetches(refs, blocks, weight_ref, sems):
    copies, n, left = [], 0, 0
    for column in blocks:
        top = 0
        for w in column:
            at = weight_ref.at[pl.ds(top, w.shape[0]), pl.ds(left, w.shape[1])]
            copies.append(pltpu.make_async_copy(refs[n], at, sems.at[n]))
            n, top = n + 1, top + w.shape[0]
        left += column[0].shape[1]
    return copies


def combine(ids, rows, blocks):
    groups, count, depth = rows.shape
    width = blocks[0][0].shape[1]
    flat = [w for column in blocks for w in column]
    half = len(flat) // 2

    def body(ids_ref, rows_ref, *refs):
        out_ref, weight_ref, sems = refs[len(flat) :]
        copies = fetches(refs, blocks, weight_ref, sems)
        for copy in copies:
            copy.start()
        lhs = rows_ref[...].reshape(groups * count, depth)
        for k in range(2):
            for copy in copies[k * half : (k + 1) * half]:
                copy.wait()
            total = jnp.dot(
                lhs, weight_ref[:, k * width : (k + 1) * width], preferred_element_type=f32
            )
            at = lax.rem(ids_ref[1] + k, 2)
            out_ref[:, at] = total.astype(bf16).reshape(groups, count, width)

    return pl.pallas_call(
        body,
        grid_spec=pltpu.PrefetchScalarGridSpec(
            num_scalar_prefetch=1,
            grid=(1,),
            in_specs=[whole(rows.shape)] + [pl.BlockSpec(memory_space=pl.ANY) for _ in flat],
            out_specs=whole((groups, 2, count, width)),
            scratch_shapes=[
                pltpu.VMEM((depth, 2 * width), bf16),
                pltpu.SemaphoreType.DMA((len(flat),)),
            ],
        ),
        out_shape=jax.ShapeDtypeStruct((groups, 2, count, width), bf16),
        compiler_params=params(60),
        name="combine",
    )(ids, rows, *flat)


def widen(ids, rows, weight):
    halves, chunks, blocks, count, features = rows.shape
    depth, columns = weight.shape
    every = halves * chunks * count

    def body(ids_ref, rows_ref, weight_ref, out_ref, lhs_ref):
        tile = pl.program_id(0)

        def put(at, value):
            value = value.astype(bf16).reshape(halves, chunks, count, value.shape[1])
            for h in range(halves):
                out_ref[:, h, :, at] = value[h]

        @pl.when(tile == 0)
        def _():
            squares = jnp.zeros((every, 1), f32)
            for k in range(blocks):
                block = rows_ref[:, :, lax.rem(ids_ref[1] + k, blocks)].reshape(every, features)
                lhs_ref[:, k * features : (k + 1) * features] = block
                wide = block.astype(f32)
                squares += jnp.sum(wide * wide, axis=1, keepdims=True)
            high = squares.astype(bf16).astype(f32)
            lane = lax.broadcasted_iota(jnp.int32, (every, 128), 1)
            extra = jnp.where(lane == 0, high, jnp.where(lane == 1, squares - high, 0.0))
            put(slice(columns, columns + 128), extra)

        total = jnp.dot(lhs_ref[...], weight_ref[...], preferred_element_type=f32)
        put(pl.ds(pl.multiple_of(tile * TILE, 128), TILE), total)

    return pl.pallas_call(
        body,
        grid_spec=pltpu.PrefetchScalarGridSpec(
            num_scalar_prefetch=1,
            grid=(columns // TILE,),
            in_specs=[
                whole(rows.shape),
                pl.BlockSpec((depth, TILE), lambda k, ids: (0, k)),
            ],
            out_specs=whole((chunks, halves, count, columns + 128)),
            scratch_shapes=[pltpu.VMEM((every, depth), bf16)],
        ),
        out_shape=jax.ShapeDtypeStruct((chunks, halves, count, columns + 128), bf16),
        compiler_params=params(40),
        name="widen",
    )(ids, rows, weight)


def local(
    cache,
    cache_length,
    move_slot,
    move_peer,
    queries,
    new_latent,
    value_up,
    out_proj,
    residual,
    norm_gain,
    gate_weight,
    up_weight,
    down_weight,
):
    member = lax.axis_index(TP)
    core = lax.axis_index("c")
    pair = lax.axis_index("xl")
    steps = new_latent.shape[0]
    heads, latent_width, value_width = value_up.shape
    rows_out = residual.shape[1] // N_TP
    chunk = rows_out * steps
    count = chunk // 2
    features, units = gate_weight.shape

    def by_pair(mine, other):
        first = pair == 0
        return jnp.stack([jnp.where(first, mine, other), jnp.where(first, other, mine)])

    def at_pair(blocks):
        return lax.dynamic_index_in_dim(blocks, pair, 0, False)

    def at_other(blocks):
        return lax.dynamic_index_in_dim(blocks, 1 - pair, 0, False)

    out_came = swap(out_proj, "xl")
    value_near = swap(value_up, "c")
    lanes = jnp.arange(N_TP, dtype=jnp.int32)
    cache_t = cache.transpose(0, 2, 1)
    pieces = exchange(leave(move_slot[0], cache_t), TP)
    fresh_t = new_latent.transpose(1, 2, 0)
    queries_t = queries.transpose(0, 1, 3, 2)
    out = attend(cache_length, cache_length, cache_t, fresh_t, queries_t, heads, latent_width)
    pieces, out, gate_weight, up_weight, slots = lax.optimization_barrier(
        (pieces, out, gate_weight, up_weight, move_slot[0])
    )
    own_slot = jnp.sum(jnp.where(lanes == member, slots, 0))
    ids = jnp.stack([own_slot, pair]).astype(jnp.int32)

    gain = norm_gain.astype(f32)[:, None]

    def scaled(low, high, first, second):
        weight = jnp.where(pair == 0, first[low:high], second[low:high])
        return (weight.astype(f32) * gain[low:high]).astype(bf16)

    kept = scaled(0, features, gate_weight, up_weight)
    sent = scaled(0, CUT, up_weight, gate_weight)
    arrived = exchange(route(move_peer[0], pieces), TP)
    arrived, kept, sent, ids, value_near = lax.optimization_barrier(
        (arrived, kept, sent, ids, value_near)
    )
    out = attend(
        ids, cache_length, cache_t, fresh_t, queries_t, heads, latent_width, arrived, out
    )
    out, out_came, out_proj, down_weight = lax.optimization_barrier(
        (out, out_came, out_proj, down_weight)
    )
    came = [swap(sent, "xl")]
    out_near = swap(out_proj, "c")
    out_weights = [[out_proj, out_near], [out_came, swap(out_came, "c")]]
    out = out.reshape((N_TP,) + out.shape[2:])
    by_head = exchange(out, TP).reshape(-1, 2 * heads, latent_width)

    downs = jnp.concatenate([down_weight, swap(down_weight, "c")], axis=0)
    out_weights[0][1], gate_weight, up_weight, residual, value_near = lax.optimization_barrier(
        (out_near, gate_weight, up_weight, residual, value_near)
    )
    value_ups = jnp.concatenate([value_up, value_near], axis=0)
    sent = scaled(CUT, features, up_weight, gate_weight)
    residue = lax.dynamic_slice_in_dim(residual, lax.div(member, 2) * 2 * rows_out, 2 * rows_out, 1)
    residue = residue.reshape(steps, 2, 2, rows_out // 8, 2, 2, features)
    residue = lax.dynamic_index_in_dim(residue, core, 4, False)
    residue = residue.transpose(2, 1, 3, 4, 0, 5).reshape(2, count, features)
    residue = [at_pair(residue), at_other(residue)]
    by_head, kept, came, sent, downs, residue, out_weights, value_ups = lax.optimization_barrier(
        (by_head, kept, came, sent, downs, residue, out_weights, value_ups)
    )
    value_heads = jnp.einsum(
        "thl,hlv->thv", by_head, value_ups, preferred_element_type=f32
    ).astype(bf16)

    value_heads = value_heads.reshape(2, 2, count // 2, 2 * heads * value_width)
    value_heads = value_heads.transpose(1, 0, 2, 3).reshape(2, count, -1)
    value_heads = jnp.broadcast_to(
        value_heads[None, :, None], (2, 2, 2) + value_heads.shape[1:]
    ).reshape((N_DP,) + value_heads.shape[1:])
    gathered = exchange(value_heads, DP)
    gathered, sent, kept, residue = lax.optimization_barrier((gathered, sent, kept, residue))
    came.append(swap(sent, "xl"))
    residue[1] = swap(residue[1], "xl")
    parts = exchange(combine(ids, gathered, out_weights), ZY)
    parts, came, kept, residue = lax.optimization_barrier((parts, came, kept, residue))
    kept = [kept, swap(kept, "c")]
    in_weight = jnp.concatenate(
        [
            jnp.concatenate([own, swap(own, "c") if k else kept[1]], axis=1)
            for k, own in enumerate([kept[0]] + came)
        ],
        axis=0,
    )
    hidden = by_pair(*residue).astype(f32) + jnp.sum(parts.astype(f32), axis=0)

    rows = spread(hidden.astype(bf16), PAIR, 2 * N_ZY).reshape((2, N_ZY) + hidden.shape)
    near = swap(at_other(hidden), "xl")
    near, in_weight = lax.optimization_barrier((near, in_weight))
    rows, near = lax.optimization_barrier((rows, near))
    sums = exchange(widen(ids, rows, in_weight).reshape(N_DP, chunk, -1), DP)
    sums = jnp.sum(sums.reshape(2, 2, 2, chunk, -1).astype(f32), axis=(0, 2))
    squares = sums[0, :, 2 * units] + sums[0, :, 2 * units + 1]
    inverse = lax.rsqrt(squares / D + norm_eps)[:, None]
    active = sums[:, :, : 2 * units] * inverse
    active = (jax.nn.silu(active[0]) * active[1]).astype(bf16)
    parts = exchange(project(ids, spread(active, DP, N_DP), downs, 1)[:, 0], ZY)
    hidden = by_pair(at_pair(hidden), near).reshape(chunk, -1)
    result = (hidden + jnp.sum(parts.astype(f32), axis=0)).astype(bf16)

    result = result.reshape(2, 2, rows_out // 8, 2, steps, features)
    mine = lax.dynamic_index_in_dim(result, core, 1, False)
    near = swap(lax.dynamic_index_in_dim(result, 1 - core, 1, False), "c")
    first = core == 0
    result = jnp.stack([jnp.where(first, mine, near), jnp.where(first, near, mine)])
    return result.transpose(4, 1, 2, 0, 3, 5).reshape(steps, rows_out, features)


def solution(mesh):
    split = Mesh(
        mesh.devices.reshape(2, 2, 2, 2, 4, 2), ("xh", "xl", "zl", "zh", "y", "c")
    )
    in_specs = (
        P(DP + TP, None, None),
        P(DP + TP),
        P(DP, None),
        P(DP, None),
        P(None, DP + TP, None, None),
        P(None, DP + TP, None),
        P(TP, None, None),
        P(TP, DP),
        P(None, None, DP),
        P(DP),
        P(DP, TP),
        P(DP, TP),
        P(TP, DP),
    )
    out_specs = P(None, TP, DP)
    return jax.shard_map(local, mesh=split, in_specs=in_specs, out_specs=out_specs, check_vma=False)
```

```python
import jax
import jax.numpy as jnp
from jax import lax
from jax.experimental import pallas as pl
from jax.experimental.pallas import tpu as pltpu
from jax.sharding import Mesh, PartitionSpec as P

D = 7168
QKD = 192
norm_eps = 1e-06

DP = ("xh", "xl", "zl")
TP = ("zh", "y", "c")
ZY = ("zh", "y")
PAIR = ("xl",) + ZY
N_DP = 8
N_TP = 16
N_ZY = 8
SWAP = [(0, 1), (1, 0)]
CUT = 448
TILE = 768
bf16 = jnp.bfloat16
f32 = jnp.float32
MIB = 1024 * 1024


def exchange(blocks, axes):
    return lax.all_to_all(blocks, axes, 0, 0, tiled=True)


def spread(block, axes, copies):
    return exchange(jnp.broadcast_to(block[None], (copies,) + block.shape), axes)


def swap(block, axis):
    return lax.ppermute(block, axis, SWAP)


def params(mib):
    return pltpu.CompilerParams(vmem_limit_bytes=mib * MIB)


def whole(shape):
    return pl.BlockSpec(shape, lambda *_: (0,) * len(shape))


def leave(slots, cache_t):
    _, entries, length = cache_t.shape
    tall, wide = 2 * entries // N_TP, length // 2

    def body(slots_ref, cache_ref, out_ref, row_ref, sem):
        slot = slots_ref[lax.axis_index(TP)]
        copy = pltpu.make_async_copy(cache_ref.at[slot], row_ref, sem)
        copy.start()
        copy.wait()
        row = row_ref[...].astype(f32)
        for j in range(N_TP):
            top, left = j // 2 * tall, j % 2 * wide
            out_ref[j] = row[top : top + tall, left : left + wide].astype(bf16)

    return pl.pallas_call(
        body,
        grid_spec=pltpu.PrefetchScalarGridSpec(
            num_scalar_prefetch=1,
            grid=(1,),
            in_specs=[pl.BlockSpec(memory_space=pl.ANY)],
            out_specs=whole((N_TP, tall, wide)),
            scratch_shapes=[pltpu.VMEM((entries, length), bf16), pltpu.SemaphoreType.DMA],
        ),
        out_shape=jax.ShapeDtypeStruct((N_TP, tall, wide), bf16),
        compiler_params=params(60),
        name="leave",
    )(slots, cache_t)


def route(peer, pieces):
    def body(peer_ref, in_ref, out_ref):
        for i in range(N_TP):
            out_ref[peer_ref[i]] = in_ref[i]

    return pl.pallas_call(
        body,
        grid_spec=pltpu.PrefetchScalarGridSpec(
            num_scalar_prefetch=1,
            grid=(1,),
            in_specs=[whole(pieces.shape)],
            out_specs=whole(pieces.shape),
        ),
        out_shape=jax.ShapeDtypeStruct(pieces.shape, bf16),
        compiler_params=params(40),
        name="route",
    )(peer, pieces)


def attend(ids, lengths, cache_t, fresh_t, queries_t, heads, latent_width, arrived=None, done=None):
    rows, entries, length = cache_t.shape
    steps, _, _, all_heads = queries_t.shape
    chips = all_heads // (2 * heads)
    again = arrived is not None

    def slot(r, ids):
        return ids[0] if again else r

    def body(ids_ref, lengths_ref, fresh_ref, q_ref, *refs):
        out_ref = refs[-1]
        row = slot(pl.program_id(0), ids_ref)
        current = lengths_ref[row]
        if again:
            latents = [
                jnp.concatenate([refs[0][j + b].astype(f32) for b in range(2)], axis=1)
                for j in range(0, N_TP, 2)
            ]
            latents = jnp.concatenate(latents, axis=0)
        else:
            latents = refs[0][0].astype(f32)
        position = lax.broadcasted_iota(jnp.int32, (entries, length), 1)
        for s in range(steps):
            token = fresh_ref[0, :, s : s + 1].astype(f32)
            latents = jnp.where(position == current + s, token, latents)
        latents = latents.astype(bf16)
        place = lax.broadcasted_iota(jnp.int32, (all_heads, length), 1)
        outs = []
        for s in range(steps):
            scores = lax.dot_general(
                q_ref[s, 0], latents, (((0,), (0,)), ((), ())), preferred_element_type=f32
            )
            scores = jnp.where(place <= current + s, scores * QKD ** (-0.5), -jnp.inf)
            expo = jnp.exp(scores - jnp.max(scores, axis=-1, keepdims=True))
            probs = (expo / jnp.sum(expo, axis=-1, keepdims=True)).astype(bf16)
            out = lax.dot_general(
                probs, latents[:latent_width], (((1,), (1,)), ((), ())), preferred_element_type=f32
            )
            out = out.reshape(chips, 2, heads, latent_width)
            turned = jnp.concatenate([out[:, 1:], out[:, :1]], axis=1)
            out = jnp.where(row >= rows // 2, turned, out)
            outs.append(out.reshape(chips, 2 * heads, latent_width))
        out_ref[:, 0, 0] = jnp.concatenate(outs, axis=1).astype(bf16)

    if again:
        extra_specs = [whole(arrived.shape), pl.BlockSpec(memory_space=pl.ANY)]
        extra = [arrived, done]
    else:
        extra_specs = [pl.BlockSpec((1, entries, length), lambda r, *_: (r, 0, 0))]
        extra = [cache_t]
    return pl.pallas_call(
        body,
        grid_spec=pltpu.PrefetchScalarGridSpec(
            num_scalar_prefetch=2,
            grid=(1 if again else rows,),
            in_specs=[
                pl.BlockSpec((1, entries, steps), lambda r, ids, _: (slot(r, ids), 0, 0)),
                pl.BlockSpec(
                    (steps, 1, entries, all_heads), lambda r, ids, _: (0, slot(r, ids), 0, 0)
                ),
            ]
            + extra_specs,
            out_specs=pl.BlockSpec(
                (chips, 1, 1, 2 * steps * heads, latent_width),
                lambda r, ids, _: (
                    0,
                    lax.div(slot(r, ids), rows // 2),
                    lax.rem(slot(r, ids), rows // 2),
                    0,
                    0,
                ),
            ),
        ),
        out_shape=jax.ShapeDtypeStruct(
            (chips, 2, rows // 2, 2 * steps * heads, latent_width), bf16
        ),
        input_output_aliases={5: 0} if again else {},
        compiler_params=params(60),
        name="again" if again else "attend",
    )(ids, lengths, fresh_t, queries_t, *extra)


def project(ids, rows, weight, blocks):
    groups, count, depth = rows.shape
    width = weight.shape[1] // blocks

    def body(ids_ref, rows_ref, weight_ref, out_ref):
        lhs = rows_ref[...].reshape(groups * count, depth)
        total = jnp.dot(lhs, weight_ref[...], preferred_element_type=f32)
        out_ref[:, 0] = total.astype(bf16).reshape(groups, count, width)

    return pl.pallas_call(
        body,
        grid_spec=pltpu.PrefetchScalarGridSpec(
            num_scalar_prefetch=1,
            grid=(blocks,),
            in_specs=[
                whole(rows.shape),
                pl.BlockSpec((depth, width), lambda k, ids: (0, k)),
            ],
            out_specs=pl.BlockSpec(
                (groups, 1, count, width), lambda k, ids: (0, lax.rem(ids[1] + k, blocks), 0, 0)
            ),
        ),
        out_shape=jax.ShapeDtypeStruct((groups, blocks, count, width), bf16),
        compiler_params=params(40),
        name="project",
    )(ids, rows, weight)


def fetches(refs, blocks, weight_ref, sems):
    copies, n, left = [], 0, 0
    for column in blocks:
        top = 0
        for w in column:
            at = weight_ref.at[pl.ds(top, w.shape[0]), pl.ds(left, w.shape[1])]
            copies.append(pltpu.make_async_copy(refs[n], at, sems.at[n]))
            n, top = n + 1, top + w.shape[0]
        left += column[0].shape[1]
    return copies


def combine(ids, rows, blocks):
    groups, count, depth = rows.shape
    width = blocks[0][0].shape[1]
    flat = [w for column in blocks for w in column]
    half = len(flat) // 2

    def body(ids_ref, rows_ref, *refs):
        out_ref, weight_ref, sems = refs[len(flat) :]
        copies = fetches(refs, blocks, weight_ref, sems)
        for copy in copies:
            copy.start()
        lhs = rows_ref[...].reshape(groups * count, depth)
        for k in range(2):
            for copy in copies[k * half : (k + 1) * half]:
                copy.wait()
            total = jnp.dot(
                lhs, weight_ref[:, k * width : (k + 1) * width], preferred_element_type=f32
            )
            at = lax.rem(ids_ref[1] + k, 2)
            out_ref[:, at] = total.astype(bf16).reshape(groups, count, width)

    return pl.pallas_call(
        body,
        grid_spec=pltpu.PrefetchScalarGridSpec(
            num_scalar_prefetch=1,
            grid=(1,),
            in_specs=[whole(rows.shape)] + [pl.BlockSpec(memory_space=pl.ANY) for _ in flat],
            out_specs=whole((groups, 2, count, width)),
            scratch_shapes=[
                pltpu.VMEM((depth, 2 * width), bf16),
                pltpu.SemaphoreType.DMA((len(flat),)),
            ],
        ),
        out_shape=jax.ShapeDtypeStruct((groups, 2, count, width), bf16),
        compiler_params=params(60),
        name="combine",
    )(ids, rows, *flat)


def widen(ids, rows, weight):
    halves, chunks, blocks, count, features = rows.shape
    depth, columns = weight.shape
    every = halves * chunks * count

    def body(ids_ref, rows_ref, weight_ref, out_ref, lhs_ref):
        tile = pl.program_id(0)

        def put(at, value):
            value = value.astype(bf16).reshape(halves, chunks, count, value.shape[1])
            for h in range(halves):
                out_ref[:, h, :, at] = value[h]

        @pl.when(tile == 0)
        def _():
            squares = jnp.zeros((every, 1), f32)
            for k in range(blocks):
                block = rows_ref[:, :, lax.rem(ids_ref[1] + k, blocks)].reshape(every, features)
                lhs_ref[:, k * features : (k + 1) * features] = block
                wide = block.astype(f32)
                squares += jnp.sum(wide * wide, axis=1, keepdims=True)
            high = squares.astype(bf16).astype(f32)
            lane = lax.broadcasted_iota(jnp.int32, (every, 128), 1)
            extra = jnp.where(lane == 0, high, jnp.where(lane == 1, squares - high, 0.0))
            put(slice(columns, columns + 128), extra)

        total = jnp.dot(lhs_ref[...], weight_ref[...], preferred_element_type=f32)
        put(pl.ds(pl.multiple_of(tile * TILE, 128), TILE), total)

    return pl.pallas_call(
        body,
        grid_spec=pltpu.PrefetchScalarGridSpec(
            num_scalar_prefetch=1,
            grid=(columns // TILE,),
            in_specs=[
                whole(rows.shape),
                pl.BlockSpec((depth, TILE), lambda k, ids: (0, k)),
            ],
            out_specs=whole((chunks, halves, count, columns + 128)),
            scratch_shapes=[pltpu.VMEM((every, depth), bf16)],
        ),
        out_shape=jax.ShapeDtypeStruct((chunks, halves, count, columns + 128), bf16),
        compiler_params=params(40),
        name="widen",
    )(ids, rows, weight)


def local(
    cache,
    cache_length,
    move_slot,
    move_peer,
    queries,
    new_latent,
    value_up,
    out_proj,
    residual,
    norm_gain,
    gate_weight,
    up_weight,
    down_weight,
):
    member = lax.axis_index(TP)
    core = lax.axis_index("c")
    pair = lax.axis_index("xl")
    steps = new_latent.shape[0]
    heads, latent_width, value_width = value_up.shape
    rows_out = residual.shape[1] // N_TP
    chunk = rows_out * steps
    count = chunk // 2
    features, units = gate_weight.shape

    def by_pair(mine, other):
        first = pair == 0
        return jnp.stack([jnp.where(first, mine, other), jnp.where(first, other, mine)])

    def at_pair(blocks):
        return lax.dynamic_index_in_dim(blocks, pair, 0, False)

    def at_other(blocks):
        return lax.dynamic_index_in_dim(blocks, 1 - pair, 0, False)

    out_came = swap(out_proj, "xl")
    value_near = swap(value_up, "c")
    lanes = jnp.arange(N_TP, dtype=jnp.int32)
    cache_t = cache.transpose(0, 2, 1)
    pieces = exchange(leave(move_slot[0], cache_t), TP)
    fresh_t = new_latent.transpose(1, 2, 0)
    queries_t = queries.transpose(0, 1, 3, 2)
    out = attend(cache_length, cache_length, cache_t, fresh_t, queries_t, heads, latent_width)
    pieces, out, gate_weight, up_weight, slots = lax.optimization_barrier(
        (pieces, out, gate_weight, up_weight, move_slot[0])
    )
    own_slot = jnp.sum(jnp.where(lanes == member, slots, 0))
    ids = jnp.stack([own_slot, pair]).astype(jnp.int32)

    gain = norm_gain.astype(f32)[:, None]

    def scaled(low, high, first, second):
        weight = jnp.where(pair == 0, first[low:high], second[low:high])
        return (weight.astype(f32) * gain[low:high]).astype(bf16)

    kept = scaled(0, features, gate_weight, up_weight)
    sent = scaled(0, CUT, up_weight, gate_weight)
    arrived = exchange(route(move_peer[0], pieces), TP)
    arrived, kept, sent, ids, value_near = lax.optimization_barrier(
        (arrived, kept, sent, ids, value_near)
    )
    out = attend(
        ids, cache_length, cache_t, fresh_t, queries_t, heads, latent_width, arrived, out
    )
    out, out_came, out_proj, down_weight = lax.optimization_barrier(
        (out, out_came, out_proj, down_weight)
    )
    came = [swap(sent, "xl")]
    out_near = swap(out_proj, "c")
    out_weights = [[out_proj, out_near], [out_came, swap(out_came, "c")]]
    out = out.reshape((N_TP,) + out.shape[2:])
    by_head = exchange(out, TP).reshape(-1, 2 * heads, latent_width)

    downs = jnp.concatenate([down_weight, swap(down_weight, "c")], axis=0)
    out_weights[0][1], gate_weight, up_weight, residual, value_near = lax.optimization_barrier(
        (out_near, gate_weight, up_weight, residual, value_near)
    )
    value_ups = jnp.concatenate([value_up, value_near], axis=0)
    sent = scaled(CUT, features, up_weight, gate_weight)
    residue = lax.dynamic_slice_in_dim(residual, lax.div(member, 2) * 2 * rows_out, 2 * rows_out, 1)
    residue = residue.reshape(steps, 2, 2, rows_out // 8, 2, 2, features)
    residue = lax.dynamic_index_in_dim(residue, core, 4, False)
    residue = residue.transpose(2, 1, 3, 4, 0, 5).reshape(2, count, features)
    residue = [at_pair(residue), at_other(residue)]
    by_head, kept, came, sent, downs, residue, out_weights, value_ups = lax.optimization_barrier(
        (by_head, kept, came, sent, downs, residue, out_weights, value_ups)
    )
    value_heads = jnp.einsum(
        "thl,hlv->thv", by_head, value_ups, preferred_element_type=f32
    ).astype(bf16)

    value_heads = value_heads.reshape(2, 2, count // 2, 2 * heads * value_width)
    value_heads = value_heads.transpose(1, 0, 2, 3).reshape(2, count, -1)
    value_heads = jnp.broadcast_to(
        value_heads[None, :, None], (2, 2, 2) + value_heads.shape[1:]
    ).reshape((N_DP,) + value_heads.shape[1:])
    gathered = exchange(value_heads, DP)
    gathered, sent, kept, residue = lax.optimization_barrier((gathered, sent, kept, residue))
    came.append(swap(sent, "xl"))
    residue[1] = swap(residue[1], "xl")
    parts = exchange(combine(ids, gathered, out_weights), ZY)
    parts, came, kept, residue = lax.optimization_barrier((parts, came, kept, residue))
    kept = [kept, swap(kept, "c")]
    in_weight = jnp.concatenate(
        [
            jnp.concatenate([own, swap(own, "c") if k else kept[1]], axis=1)
            for k, own in enumerate([kept[0]] + came)
        ],
        axis=0,
    )
    hidden = by_pair(*residue).astype(f32) + jnp.sum(parts.astype(f32), axis=0)

    rows = spread(hidden.astype(bf16), PAIR, 2 * N_ZY).reshape((2, N_ZY) + hidden.shape)
    near = swap(at_other(hidden), "xl")
    near, in_weight = lax.optimization_barrier((near, in_weight))
    rows, near = lax.optimization_barrier((rows, near))
    sums = exchange(widen(ids, rows, in_weight).reshape(N_DP, chunk, -1), DP)
    sums = jnp.sum(sums.reshape(2, 2, 2, chunk, -1).astype(f32), axis=(0, 2))
    squares = sums[0, :, 2 * units] + sums[0, :, 2 * units + 1]
    inverse = lax.rsqrt(squares / D + norm_eps)[:, None]
    active = sums[:, :, : 2 * units] * inverse
    active = (jax.nn.silu(active[0]) * active[1]).astype(bf16)
    parts = exchange(project(ids, spread(active, DP, N_DP), downs, 1)[:, 0], ZY)
    hidden = by_pair(at_pair(hidden), near).reshape(chunk, -1)
    result = (hidden + jnp.sum(parts.astype(f32), axis=0)).astype(bf16)

    result = result.reshape(2, 2, rows_out // 8, 2, steps, features)
    mine = lax.dynamic_index_in_dim(result, core, 1, False)
    near = swap(lax.dynamic_index_in_dim(result, 1 - core, 1, False), "c")
    first = core == 0
    result = jnp.stack([jnp.where(first, mine, near), jnp.where(first, near, mine)])
    return result.transpose(4, 1, 2, 0, 3, 5).reshape(steps, rows_out, features)


def solution(mesh):
    split = Mesh(
        mesh.devices.reshape(2, 2, 2, 2, 4, 2), ("xh", "xl", "zl", "zh", "y", "c")
    )
    in_specs = (
        P(DP + TP, None, None),
        P(DP + TP),
        P(DP, None),
        P(DP, None),
        P(None, DP + TP, None, None),
        P(None, DP + TP, None),
        P(TP, None, None),
        P(TP, DP),
        P(None, None, DP),
        P(DP),
        P(DP, TP),
        P(DP, TP),
        P(TP, DP),
    )
    out_specs = P(None, TP, DP)
    return jax.shard_map(local, mesh=split, in_specs=in_specs, out_specs=out_specs, check_vma=False)
```

```python
import jax
import jax.numpy as jnp
from jax import lax
from jax.experimental import pallas as pl
from jax.experimental.pallas import tpu as pltpu
from jax.sharding import Mesh, PartitionSpec as P

D = 7168
QKD = 192
norm_eps = 1e-06

DP = ("xh", "xl", "zl")
TP = ("zh", "y", "c")
ZY = ("zh", "y")
PAIR = ("xl",) + ZY
N_DP = 8
N_TP = 16
N_ZY = 8
SWAP = [(0, 1), (1, 0)]
CUT = 448
TILE = 768
bf16 = jnp.bfloat16
f32 = jnp.float32
MIB = 1024 * 1024


def exchange(blocks, axes):
    return lax.all_to_all(blocks, axes, 0, 0, tiled=True)


def spread(block, axes, copies):
    return exchange(jnp.broadcast_to(block[None], (copies,) + block.shape), axes)


def swap(block, axis):
    return lax.ppermute(block, axis, SWAP)


def cross(block):
    return lax.ppermute(block, ("xh", "xl"), [(i, 3 - i) for i in range(4)])


def params(mib):
    return pltpu.CompilerParams(vmem_limit_bytes=mib * MIB)


def whole(shape):
    return pl.BlockSpec(shape, lambda *_: (0,) * len(shape))


def leave(slots, cache_t):
    _, entries, length = cache_t.shape
    tall, wide = 2 * entries // N_TP, length // 2

    def body(slots_ref, cache_ref, out_ref, row_ref, sem):
        slot = slots_ref[lax.axis_index(TP)]
        copy = pltpu.make_async_copy(cache_ref.at[slot], row_ref, sem)
        copy.start()
        copy.wait()
        row = row_ref[...].astype(f32)
        for j in range(N_TP):
            top, left = j // 2 * tall, j % 2 * wide
            out_ref[j] = row[top : top + tall, left : left + wide].astype(bf16)

    return pl.pallas_call(
        body,
        grid_spec=pltpu.PrefetchScalarGridSpec(
            num_scalar_prefetch=1,
            grid=(1,),
            in_specs=[pl.BlockSpec(memory_space=pl.ANY)],
            out_specs=whole((N_TP, tall, wide)),
            scratch_shapes=[pltpu.VMEM((entries, length), bf16), pltpu.SemaphoreType.DMA],
        ),
        out_shape=jax.ShapeDtypeStruct((N_TP, tall, wide), bf16),
        compiler_params=params(60),
        name="leave",
    )(slots, cache_t)


def route(peer, pieces):
    def body(peer_ref, in_ref, out_ref):
        for i in range(N_TP):
            out_ref[peer_ref[i]] = in_ref[i]

    return pl.pallas_call(
        body,
        grid_spec=pltpu.PrefetchScalarGridSpec(
            num_scalar_prefetch=1,
            grid=(1,),
            in_specs=[whole(pieces.shape)],
            out_specs=whole(pieces.shape),
        ),
        out_shape=jax.ShapeDtypeStruct(pieces.shape, bf16),
        compiler_params=params(40),
        name="route",
    )(peer, pieces)


def attend(ids, lengths, cache_t, fresh_t, queries_t, heads, latent_width, arrived=None, done=None):
    rows, entries, length = cache_t.shape
    steps, _, _, all_heads = queries_t.shape
    chips = all_heads // (2 * heads)
    again = arrived is not None

    def slot(r, ids):
        return ids[0] if again else r

    def body(ids_ref, lengths_ref, fresh_ref, q_ref, *refs):
        out_ref = refs[-1]
        row = slot(pl.program_id(0), ids_ref)
        current = lengths_ref[row]
        if again:
            latents = [
                jnp.concatenate([refs[0][j + b].astype(f32) for b in range(2)], axis=1)
                for j in range(0, N_TP, 2)
            ]
            latents = jnp.concatenate(latents, axis=0)
        else:
            latents = refs[0][0].astype(f32)
        position = lax.broadcasted_iota(jnp.int32, (entries, length), 1)
        for s in range(steps):
            token = fresh_ref[0, :, s : s + 1].astype(f32)
            latents = jnp.where(position == current + s, token, latents)
        latents = latents.astype(bf16)
        place = lax.broadcasted_iota(jnp.int32, (all_heads, length), 1)
        outs = []
        for s in range(steps):
            scores = lax.dot_general(
                q_ref[s, 0], latents, (((0,), (0,)), ((), ())), preferred_element_type=f32
            )
            scores = jnp.where(place <= current + s, scores * QKD ** (-0.5), -jnp.inf)
            expo = jnp.exp(scores - jnp.max(scores, axis=-1, keepdims=True))
            probs = (expo / jnp.sum(expo, axis=-1, keepdims=True)).astype(bf16)
            out = lax.dot_general(
                probs, latents[:latent_width], (((1,), (1,)), ((), ())), preferred_element_type=f32
            )
            out = out.reshape(chips, 2, heads, latent_width)
            turned = jnp.concatenate([out[:, 1:], out[:, :1]], axis=1)
            out = jnp.where(row >= rows // 2, turned, out)
            outs.append(out.reshape(chips, 2 * heads, latent_width))
        out_ref[:, 0, 0] = jnp.concatenate(outs, axis=1).astype(bf16)

    if again:
        extra_specs = [whole(arrived.shape), pl.BlockSpec(memory_space=pl.ANY)]
        extra = [arrived, done]
    else:
        extra_specs = [pl.BlockSpec((1, entries, length), lambda r, *_: (r, 0, 0))]
        extra = [cache_t]
    return pl.pallas_call(
        body,
        grid_spec=pltpu.PrefetchScalarGridSpec(
            num_scalar_prefetch=2,
            grid=(1 if again else rows,),
            in_specs=[
                pl.BlockSpec((1, entries, steps), lambda r, ids, _: (slot(r, ids), 0, 0)),
                pl.BlockSpec(
                    (steps, 1, entries, all_heads), lambda r, ids, _: (0, slot(r, ids), 0, 0)
                ),
            ]
            + extra_specs,
            out_specs=pl.BlockSpec(
                (chips, 1, 1, 2 * steps * heads, latent_width),
                lambda r, ids, _: (
                    0,
                    lax.div(slot(r, ids), rows // 2),
                    lax.rem(slot(r, ids), rows // 2),
                    0,
                    0,
                ),
            ),
        ),
        out_shape=jax.ShapeDtypeStruct(
            (chips, 2, rows // 2, 2 * steps * heads, latent_width), bf16
        ),
        input_output_aliases={5: 0} if again else {},
        compiler_params=params(60),
        name="again" if again else "attend",
    )(ids, lengths, fresh_t, queries_t, *extra)


def project(ids, rows, weight, blocks):
    groups, count, depth = rows.shape
    width = weight.shape[1] // blocks

    def body(ids_ref, rows_ref, weight_ref, out_ref):
        lhs = rows_ref[...].reshape(groups * count, depth)
        total = jnp.dot(lhs, weight_ref[...], preferred_element_type=f32)
        out_ref[:, 0] = total.astype(bf16).reshape(groups, count, width)

    return pl.pallas_call(
        body,
        grid_spec=pltpu.PrefetchScalarGridSpec(
            num_scalar_prefetch=1,
            grid=(blocks,),
            in_specs=[
                whole(rows.shape),
                pl.BlockSpec((depth, width), lambda k, ids: (0, k)),
            ],
            out_specs=pl.BlockSpec(
                (groups, 1, count, width), lambda k, ids: (0, lax.rem(ids[1] + k, blocks), 0, 0)
            ),
        ),
        out_shape=jax.ShapeDtypeStruct((groups, blocks, count, width), bf16),
        compiler_params=params(40),
        name="project",
    )(ids, rows, weight)


def fetches(refs, blocks, weight_ref, sems):
    copies, n, left = [], 0, 0
    for column in blocks:
        top = 0
        for w in column:
            at = weight_ref.at[pl.ds(top, w.shape[0]), pl.ds(left, w.shape[1])]
            copies.append(pltpu.make_async_copy(refs[n], at, sems.at[n]))
            n, top = n + 1, top + w.shape[0]
        left += column[0].shape[1]
    return copies


def combine(ids, rows, blocks):
    groups, count, depth = rows.shape
    width = blocks[0][0].shape[1]
    flat = [w for column in blocks for w in column]
    half = len(flat) // 2

    def body(ids_ref, rows_ref, *refs):
        out_ref, weight_ref, sems = refs[len(flat) :]
        copies = fetches(refs, blocks, weight_ref, sems)
        for copy in copies:
            copy.start()
        lhs = rows_ref[...].reshape(groups * count, depth)
        for k in range(2):
            for copy in copies[k * half : (k + 1) * half]:
                copy.wait()
            total = jnp.dot(
                lhs, weight_ref[:, k * width : (k + 1) * width], preferred_element_type=f32
            )
            out_ref[:, k] = total.astype(bf16).reshape(groups, count, width)

    return pl.pallas_call(
        body,
        grid_spec=pltpu.PrefetchScalarGridSpec(
            num_scalar_prefetch=1,
            grid=(1,),
            in_specs=[whole(rows.shape)] + [pl.BlockSpec(memory_space=pl.ANY) for _ in flat],
            out_specs=whole((groups, 2, count, width)),
            scratch_shapes=[
                pltpu.VMEM((depth, 2 * width), bf16),
                pltpu.SemaphoreType.DMA((len(flat),)),
            ],
        ),
        out_shape=jax.ShapeDtypeStruct((groups, 2, count, width), bf16),
        compiler_params=params(60),
        name="combine",
    )(ids, rows, *flat)


def widen(ids, rows, weight):
    blocks, chunks, count, features = rows.shape
    depth, columns = weight.shape
    every = chunks * count

    def body(ids_ref, rows_ref, weight_ref, out_ref, lhs_ref):
        tile = pl.program_id(0)

        def put(at, value):
            out_ref[:, :, at] = value.astype(bf16).reshape(chunks, count, value.shape[1])

        @pl.when(tile == 0)
        def _():
            squares = jnp.zeros((every, 1), f32)
            for k in range(blocks):
                block = rows_ref[lax.rem(ids_ref[1] + k, blocks)].reshape(every, features)
                lhs_ref[:, k * features : (k + 1) * features] = block
                wide = block.astype(f32)
                squares += jnp.sum(wide * wide, axis=1, keepdims=True)
            high = squares.astype(bf16).astype(f32)
            lane = lax.broadcasted_iota(jnp.int32, (every, 128), 1)
            extra = jnp.where(lane == 0, high, jnp.where(lane == 1, squares - high, 0.0))
            put(slice(columns, columns + 128), extra)

        total = jnp.dot(lhs_ref[...], weight_ref[...], preferred_element_type=f32)
        put(pl.ds(pl.multiple_of(tile * TILE, 128), TILE), total)

    return pl.pallas_call(
        body,
        grid_spec=pltpu.PrefetchScalarGridSpec(
            num_scalar_prefetch=1,
            grid=(columns // TILE,),
            in_specs=[
                whole(rows.shape),
                pl.BlockSpec((depth, TILE), lambda k, ids: (0, k)),
            ],
            out_specs=whole((chunks, count, columns + 128)),
            scratch_shapes=[pltpu.VMEM((every, depth), bf16)],
        ),
        out_shape=jax.ShapeDtypeStruct((chunks, count, columns + 128), bf16),
        compiler_params=params(40),
        name="widen",
    )(ids, rows, weight)


def local(
    cache,
    cache_length,
    move_slot,
    move_peer,
    queries,
    new_latent,
    value_up,
    out_proj,
    residual,
    norm_gain,
    gate_weight,
    up_weight,
    down_weight,
):
    member = lax.axis_index(TP)
    core = lax.axis_index("c")
    pair = lax.axis_index("xl")
    steps = new_latent.shape[0]
    heads, latent_width, value_width = value_up.shape
    rows_out = residual.shape[1] // N_TP
    chunk = rows_out * steps
    count = chunk // 2
    features, units = gate_weight.shape

    out_came = cross(out_proj)
    value_near = swap(value_up, "c")
    lanes = jnp.arange(N_TP, dtype=jnp.int32)
    cache_t = cache.transpose(0, 2, 1)
    pieces = exchange(leave(move_slot[0], cache_t), TP)
    fresh_t = new_latent.transpose(1, 2, 0)
    queries_t = queries.transpose(0, 1, 3, 2)
    out = attend(cache_length, cache_length, cache_t, fresh_t, queries_t, heads, latent_width)
    pieces, out, gate_weight, up_weight, slots = lax.optimization_barrier(
        (pieces, out, gate_weight, up_weight, move_slot[0])
    )
    own_slot = jnp.sum(jnp.where(lanes == member, slots, 0))
    ids = jnp.stack([own_slot, pair]).astype(jnp.int32)

    gain = norm_gain.astype(f32)[:, None]

    def scaled(low, high, first, second):
        weight = jnp.where(pair == 0, first[low:high], second[low:high])
        return (weight.astype(f32) * gain[low:high]).astype(bf16)

    kept = scaled(0, features, gate_weight, up_weight)
    sent = scaled(0, CUT, up_weight, gate_weight)
    arrived = exchange(route(move_peer[0], pieces), TP)
    arrived, kept, sent, ids, value_near = lax.optimization_barrier(
        (arrived, kept, sent, ids, value_near)
    )
    out = attend(
        ids, cache_length, cache_t, fresh_t, queries_t, heads, latent_width, arrived, out
    )
    out, out_came, out_proj, down_weight = lax.optimization_barrier(
        (out, out_came, out_proj, down_weight)
    )
    came = [swap(sent, "xl")]
    out_near = swap(out_proj, "c")
    out = out.reshape((N_TP,) + out.shape[2:])
    by_head = exchange(out, TP).reshape(-1, 2 * heads, latent_width)

    downs = jnp.concatenate([down_weight, swap(down_weight, "c")], axis=0)
    out_near, gate_weight, up_weight, residual, value_near = lax.optimization_barrier(
        (out_near, gate_weight, up_weight, residual, value_near)
    )
    value_ups = jnp.concatenate([value_up, value_near], axis=0)
    sent = scaled(CUT, features, up_weight, gate_weight)
    residue = lax.dynamic_slice_in_dim(residual, lax.div(member, 2) * 2 * rows_out, 2 * rows_out, 1)
    residue = residue.reshape(steps, 2, 2, rows_out // 8, 2, 2, features)
    residue = lax.dynamic_index_in_dim(residue, core, 4, False)
    residue = residue.transpose(2, 1, 3, 4, 0, 5).reshape(2, count, features)
    residue = residue.reshape(chunk, features)
    by_head, kept, came, sent, downs, residue, out_near, out_came, value_ups = (
        lax.optimization_barrier(
            (by_head, kept, came, sent, downs, residue, out_near, out_came, value_ups)
        )
    )
    out_weights = [[out_proj, out_near], [out_came, swap(out_came, "c")]]
    value_heads = jnp.einsum(
        "thl,hlv->thv", by_head, value_ups, preferred_element_type=f32
    ).astype(bf16)

    value_heads = value_heads.reshape(2, 2, count // 2, 2 * heads * value_width)
    value_heads = value_heads.transpose(1, 0, 2, 3).reshape(2, count, -1)
    value_heads = jnp.broadcast_to(
        value_heads[:, None, None], (2, 2, 2) + value_heads.shape[1:]
    ).reshape((N_DP,) + value_heads.shape[1:])
    gathered = exchange(value_heads, DP)
    gathered, sent, kept = lax.optimization_barrier((gathered, sent, kept))
    came.append(swap(sent, "xl"))
    parts = exchange(combine(ids, gathered, out_weights), ZY)
    parts, came, kept = lax.optimization_barrier((parts, came, kept))
    kept = [kept, swap(kept, "c")]
    in_weight = jnp.concatenate(
        [
            jnp.concatenate([own, swap(own, "c") if k else kept[1]], axis=1)
            for k, own in enumerate([kept[0]] + came)
        ],
        axis=0,
    )
    attended = jnp.sum(parts.astype(f32), axis=0)
    mine, near = attended[0], cross(attended[1])
    low = lax.axis_index("xh") == 0
    attended = jnp.concatenate([jnp.where(low, mine, near), jnp.where(low, near, mine)], axis=0)
    hidden = residue.astype(f32) + attended

    rows = spread(hidden.astype(bf16), PAIR, 2 * N_ZY).reshape(2, N_ZY, chunk, features)
    rows, in_weight = lax.optimization_barrier((rows, in_weight))
    sums = exchange(widen(ids, rows, in_weight), DP)
    sums = jnp.sum(sums.reshape(2, 2, 2, chunk, -1).astype(f32), axis=(0, 2))
    squares = sums[0, :, 2 * units] + sums[0, :, 2 * units + 1]
    inverse = lax.rsqrt(squares / D + norm_eps)[:, None]
    active = sums[:, :, : 2 * units] * inverse
    active = (jax.nn.silu(active[0]) * active[1]).astype(bf16)
    parts = exchange(project(ids, spread(active, DP, N_DP), downs, 1)[:, 0], ZY)
    result = (hidden + jnp.sum(parts.astype(f32), axis=0)).astype(bf16)

    result = result.reshape(2, 2, rows_out // 8, 2, steps, features)
    mine = lax.dynamic_index_in_dim(result, core, 1, False)
    near = swap(lax.dynamic_index_in_dim(result, 1 - core, 1, False), "c")
    first = core == 0
    result = jnp.stack([jnp.where(first, mine, near), jnp.where(first, near, mine)])
    return result.transpose(4, 1, 2, 0, 3, 5).reshape(steps, rows_out, features)


def solution(mesh):
    split = Mesh(
        mesh.devices.reshape(2, 2, 2, 2, 4, 2), ("xh", "xl", "zl", "zh", "y", "c")
    )
    in_specs = (
        P(DP + TP, None, None),
        P(DP + TP),
        P(DP, None),
        P(DP, None),
        P(None, DP + TP, None, None),
        P(None, DP + TP, None),
        P(TP, None, None),
        P(TP, DP),
        P(None, None, DP),
        P(DP),
        P(DP, TP),
        P(DP, TP),
        P(TP, DP),
    )
    out_specs = P(None, TP, DP)
    return jax.shard_map(local, mesh=split, in_specs=in_specs, out_specs=out_specs, check_vma=False)
```

```python
import jax
import jax.numpy as jnp
from jax import lax
from jax.experimental import pallas as pl
from jax.experimental.pallas import tpu as pltpu
from jax.sharding import Mesh, PartitionSpec as P

D = 7168
QKD = 192
norm_eps = 1e-06

DP = ("xh", "xl", "zl")
TP = ("zh", "y", "c")
ZY = ("zh", "y")
PAIR = ("xl",) + ZY
N_DP = 8
N_TP = 16
N_ZY = 8
SWAP = [(0, 1), (1, 0)]
CUT = 384
TILE = 768
bf16 = jnp.bfloat16
f32 = jnp.float32
MIB = 1024 * 1024


def exchange(blocks, axes):
    return lax.all_to_all(blocks, axes, 0, 0, tiled=True)


def spread(block, axes, copies):
    return exchange(jnp.broadcast_to(block[None], (copies,) + block.shape), axes)


def swap(block, axis):
    return lax.ppermute(block, axis, SWAP)


def params(mib):
    return pltpu.CompilerParams(vmem_limit_bytes=mib * MIB)


def whole(shape):
    return pl.BlockSpec(shape, lambda *_: (0,) * len(shape))


def leave(slots, cache_t):
    _, entries, length = cache_t.shape
    tall, wide = 2 * entries // N_TP, length // 2

    def body(slots_ref, cache_ref, out_ref, row_ref, sem):
        slot = slots_ref[lax.axis_index(TP)]
        copy = pltpu.make_async_copy(cache_ref.at[slot], row_ref, sem)
        copy.start()
        copy.wait()
        row = row_ref[...].astype(f32)
        for j in range(N_TP):
            top, left = j // 2 * tall, j % 2 * wide
            out_ref[j] = row[top : top + tall, left : left + wide].astype(bf16)

    return pl.pallas_call(
        body,
        grid_spec=pltpu.PrefetchScalarGridSpec(
            num_scalar_prefetch=1,
            grid=(1,),
            in_specs=[pl.BlockSpec(memory_space=pl.ANY)],
            out_specs=whole((N_TP, tall, wide)),
            scratch_shapes=[pltpu.VMEM((entries, length), bf16), pltpu.SemaphoreType.DMA],
        ),
        out_shape=jax.ShapeDtypeStruct((N_TP, tall, wide), bf16),
        compiler_params=params(60),
        name="leave",
    )(slots, cache_t)


def route(peer, pieces):
    def body(peer_ref, in_ref, out_ref):
        for i in range(N_TP):
            out_ref[peer_ref[i]] = in_ref[i]

    return pl.pallas_call(
        body,
        grid_spec=pltpu.PrefetchScalarGridSpec(
            num_scalar_prefetch=1,
            grid=(1,),
            in_specs=[whole(pieces.shape)],
            out_specs=whole(pieces.shape),
        ),
        out_shape=jax.ShapeDtypeStruct(pieces.shape, bf16),
        compiler_params=params(40),
        name="route",
    )(peer, pieces)


def attend(ids, lengths, cache_t, fresh_t, queries_t, heads, latent_width, arrived=None, done=None):
    rows, entries, length = cache_t.shape
    steps, _, _, all_heads = queries_t.shape
    chips = all_heads // (2 * heads)
    again = arrived is not None

    def slot(r, ids):
        return ids[0] if again else r

    def body(ids_ref, lengths_ref, fresh_ref, q_ref, *refs):
        out_ref = refs[-1]
        row = slot(pl.program_id(0), ids_ref)
        current = lengths_ref[row]
        if again:
            latents = [
                jnp.concatenate([refs[0][j + b].astype(f32) for b in range(2)], axis=1)
                for j in range(0, N_TP, 2)
            ]
            latents = jnp.concatenate(latents, axis=0)
        else:
            latents = refs[0][0].astype(f32)
        position = lax.broadcasted_iota(jnp.int32, (entries, length), 1)
        for s in range(steps):
            token = fresh_ref[0, :, s : s + 1].astype(f32)
            latents = jnp.where(position == current + s, token, latents)
        latents = latents.astype(bf16)
        place = lax.broadcasted_iota(jnp.int32, (all_heads, length), 1)
        outs = []
        for s in range(steps):
            scores = lax.dot_general(
                q_ref[s, 0], latents, (((0,), (0,)), ((), ())), preferred_element_type=f32
            )
            scores = jnp.where(place <= current + s, scores * QKD ** (-0.5), -jnp.inf)
            expo = jnp.exp(scores - jnp.max(scores, axis=-1, keepdims=True))
            probs = (expo / jnp.sum(expo, axis=-1, keepdims=True)).astype(bf16)
            out = lax.dot_general(
                probs, latents[:latent_width], (((1,), (1,)), ((), ())), preferred_element_type=f32
            )
            out = out.reshape(chips, 2, heads, latent_width)
            turned = jnp.concatenate([out[:, 1:], out[:, :1]], axis=1)
            out = jnp.where(row >= rows // 2, turned, out)
            outs.append(out.reshape(chips, 2 * heads, latent_width))
        out_ref[:, 0, 0] = jnp.concatenate(outs, axis=1).astype(bf16)

    if again:
        extra_specs = [whole(arrived.shape), pl.BlockSpec(memory_space=pl.ANY)]
        extra = [arrived, done]
    else:
        extra_specs = [pl.BlockSpec((1, entries, length), lambda r, *_: (r, 0, 0))]
        extra = [cache_t]
    return pl.pallas_call(
        body,
        grid_spec=pltpu.PrefetchScalarGridSpec(
            num_scalar_prefetch=2,
            grid=(1 if again else rows,),
            in_specs=[
                pl.BlockSpec((1, entries, steps), lambda r, ids, _: (slot(r, ids), 0, 0)),
                pl.BlockSpec(
                    (steps, 1, entries, all_heads), lambda r, ids, _: (0, slot(r, ids), 0, 0)
                ),
            ]
            + extra_specs,
            out_specs=pl.BlockSpec(
                (chips, 1, 1, 2 * steps * heads, latent_width),
                lambda r, ids, _: (
                    0,
                    lax.div(slot(r, ids), rows // 2),
                    lax.rem(slot(r, ids), rows // 2),
                    0,
                    0,
                ),
            ),
        ),
        out_shape=jax.ShapeDtypeStruct(
            (chips, 2, rows // 2, 2 * steps * heads, latent_width), bf16
        ),
        input_output_aliases={5: 0} if again else {},
        compiler_params=params(60),
        name="again" if again else "attend",
    )(ids, lengths, fresh_t, queries_t, *extra)


def project(rows, weight):
    groups, count, depth = rows.shape
    width = weight.shape[1]
    part = count // 4

    def body(rows_ref, weight_ref, out_ref):
        lhs = rows_ref[...].reshape(groups * count, depth)
        total = jnp.dot(lhs, weight_ref[...], preferred_element_type=f32)
        total = total.astype(bf16).reshape(groups, count, width)
        for k in range(4):
            out_ref[:, k % 2, k // 2] = total[:, k * part : (k + 1) * part]

    return pl.pallas_call(
        body,
        grid=(1,),
        in_specs=[whole(rows.shape), whole(weight.shape)],
        out_specs=whole((groups, 2, 2, part, width)),
        out_shape=jax.ShapeDtypeStruct((groups, 2, 2, part, width), bf16),
        compiler_params=params(40),
        name="project",
    )(rows, weight)


def fetches(refs, blocks, weight_ref, sems):
    copies, n, left = [], 0, 0
    for column in blocks:
        top = 0
        for w in column:
            at = weight_ref.at[pl.ds(top, w.shape[0]), pl.ds(left, w.shape[1])]
            copies.append(pltpu.make_async_copy(refs[n], at, sems.at[n]))
            n, top = n + 1, top + w.shape[0]
        left += column[0].shape[1]
    return copies


def combine(ids, rows, blocks):
    groups, count, depth = rows.shape
    width = blocks[0][0].shape[1]
    flat = [w for column in blocks for w in column]
    half = len(flat) // 2

    def body(ids_ref, rows_ref, *refs):
        out_ref, weight_ref, sems = refs[len(flat) :]
        copies = fetches(refs, blocks, weight_ref, sems)
        for copy in copies:
            copy.start()
        lhs = rows_ref[...].reshape(groups * count, depth)
        for k in range(2):
            for copy in copies[k * half : (k + 1) * half]:
                copy.wait()
            total = jnp.dot(
                lhs, weight_ref[:, k * width : (k + 1) * width], preferred_element_type=f32
            )
            at = lax.rem(ids_ref[1] + k, 2)
            out_ref[:, at] = total.astype(bf16).reshape(groups, count, width)

    return pl.pallas_call(
        body,
        grid_spec=pltpu.PrefetchScalarGridSpec(
            num_scalar_prefetch=1,
            grid=(1,),
            in_specs=[whole(rows.shape)] + [pl.BlockSpec(memory_space=pl.ANY) for _ in flat],
            out_specs=whole((groups, 2, count, width)),
            scratch_shapes=[
                pltpu.VMEM((depth, 2 * width), bf16),
                pltpu.SemaphoreType.DMA((len(flat),)),
            ],
        ),
        out_shape=jax.ShapeDtypeStruct((groups, 2, count, width), bf16),
        compiler_params=params(60),
        name="combine",
    )(ids, rows, *flat)


def widen(ids, rows, weight):
    halves, chunks, blocks, count, features = rows.shape
    depth, columns = weight.shape
    every = halves * chunks * count

    def body(ids_ref, rows_ref, weight_ref, out_ref, lhs_ref):
        tile = pl.program_id(0)

        def put(at, value):
            value = value.astype(bf16).reshape(halves, chunks, count, value.shape[1])
            for h in range(halves):
                out_ref[:, h, :, at] = value[h]

        @pl.when(tile == 0)
        def _():
            squares = jnp.zeros((every, 1), f32)
            for k in range(blocks):
                block = rows_ref[:, :, lax.rem(ids_ref[1] + k, blocks)].reshape(every, features)
                lhs_ref[:, k * features : (k + 1) * features] = block
                wide = block.astype(f32)
                squares += jnp.sum(wide * wide, axis=1, keepdims=True)
            high = squares.astype(bf16).astype(f32)
            lane = lax.broadcasted_iota(jnp.int32, (every, 128), 1)
            extra = jnp.where(lane == 0, high, jnp.where(lane == 1, squares - high, 0.0))
            put(slice(columns, columns + 128), extra)

        total = jnp.dot(lhs_ref[...], weight_ref[...], preferred_element_type=f32)
        put(pl.ds(pl.multiple_of(tile * TILE, 128), TILE), total)

    return pl.pallas_call(
        body,
        grid_spec=pltpu.PrefetchScalarGridSpec(
            num_scalar_prefetch=1,
            grid=(columns // TILE,),
            in_specs=[
                whole(rows.shape),
                pl.BlockSpec((depth, TILE), lambda k, ids: (0, k)),
            ],
            out_specs=whole((chunks, halves, count, columns + 128)),
            scratch_shapes=[pltpu.VMEM((every, depth), bf16)],
        ),
        out_shape=jax.ShapeDtypeStruct((chunks, halves, count, columns + 128), bf16),
        compiler_params=params(40),
        name="widen",
    )(ids, rows, weight)


def local(
    cache,
    cache_length,
    move_slot,
    move_peer,
    queries,
    new_latent,
    value_up,
    out_proj,
    residual,
    norm_gain,
    gate_weight,
    up_weight,
    down_weight,
):
    member = lax.axis_index(TP)
    core = lax.axis_index("c")
    pair = lax.axis_index("xl")
    steps = new_latent.shape[0]
    heads, latent_width, value_width = value_up.shape
    rows_out = residual.shape[1] // N_TP
    chunk = rows_out * steps
    count = chunk // 2
    features, units = gate_weight.shape

    def by_pair(mine, other):
        first = pair == 0
        return jnp.stack([jnp.where(first, mine, other), jnp.where(first, other, mine)])

    def at_pair(blocks):
        return lax.dynamic_index_in_dim(blocks, pair, 0, False)

    def at_other(blocks):
        return lax.dynamic_index_in_dim(blocks, 1 - pair, 0, False)

    out_came = swap(out_proj, "xl")
    value_near = swap(value_up, "c")
    lanes = jnp.arange(N_TP, dtype=jnp.int32)
    cache_t = cache.transpose(0, 2, 1)
    pieces = exchange(leave(move_slot[0], cache_t), TP)
    fresh_t = new_latent.transpose(1, 2, 0)
    queries_t = queries.transpose(0, 1, 3, 2)
    out = attend(cache_length, cache_length, cache_t, fresh_t, queries_t, heads, latent_width)
    pieces, out, gate_weight, up_weight, slots = lax.optimization_barrier(
        (pieces, out, gate_weight, up_weight, move_slot[0])
    )
    own_slot = jnp.sum(jnp.where(lanes == member, slots, 0))
    ids = jnp.stack([own_slot, pair]).astype(jnp.int32)

    gain = norm_gain.astype(f32)[:, None]

    def scaled(low, high, first, second):
        weight = jnp.where(pair == 0, first[low:high], second[low:high])
        return (weight.astype(f32) * gain[low:high]).astype(bf16)

    kept = scaled(0, features, gate_weight, up_weight)
    sent = scaled(0, CUT, up_weight, gate_weight)
    arrived = exchange(route(move_peer[0], pieces), TP)
    arrived, kept, sent, ids, value_near = lax.optimization_barrier(
        (arrived, kept, sent, ids, value_near)
    )
    out = attend(
        ids, cache_length, cache_t, fresh_t, queries_t, heads, latent_width, arrived, out
    )
    out, out_came, out_proj, down_weight = lax.optimization_barrier(
        (out, out_came, out_proj, down_weight)
    )
    came = [swap(sent, "xl")]
    out_near = swap(out_proj, "c")
    out_weights = [[out_proj, out_near], [out_came, swap(out_came, "c")]]
    out = out.reshape((N_TP,) + out.shape[2:])
    by_head = exchange(out, TP).reshape(-1, 2 * heads, latent_width)

    downs = jnp.concatenate([down_weight, swap(down_weight, "c")], axis=0)
    out_weights[0][1], gate_weight, up_weight, residual, value_near = lax.optimization_barrier(
        (out_near, gate_weight, up_weight, residual, value_near)
    )
    value_ups = jnp.concatenate([value_up, value_near], axis=0)
    sent = scaled(CUT, features, up_weight, gate_weight)
    residue = lax.dynamic_slice_in_dim(residual, lax.div(member, 2) * 2 * rows_out, 2 * rows_out, 1)
    residue = residue.reshape(steps, 2, 2, rows_out // 8, 2, 2, features)
    residue = lax.dynamic_index_in_dim(residue, core, 4, False)
    residue = residue.transpose(2, 1, 3, 4, 0, 5).reshape(2, count, features)
    residue = [at_pair(residue), at_other(residue)]
    by_head, kept, came, sent, downs, residue, out_weights, value_ups = lax.optimization_barrier(
        (by_head, kept, came, sent, downs, residue, out_weights, value_ups)
    )
    value_heads = jnp.einsum(
        "thl,hlv->thv", by_head, value_ups, preferred_element_type=f32
    ).astype(bf16)

    value_heads = value_heads.reshape(2, 2, count // 2, 2 * heads * value_width)
    value_heads = value_heads.transpose(1, 0, 2, 3).reshape(2, count, -1)
    value_heads = jnp.broadcast_to(
        value_heads[None, :, None], (2, 2, 2) + value_heads.shape[1:]
    ).reshape((N_DP,) + value_heads.shape[1:])
    gathered = exchange(value_heads, DP)
    gathered, sent, kept, residue = lax.optimization_barrier((gathered, sent, kept, residue))
    came.append(swap(sent, "xl"))
    residue[1] = swap(residue[1], "xl")
    parts = exchange(combine(ids, gathered, out_weights), ZY)
    parts, came, kept, residue = lax.optimization_barrier((parts, came, kept, residue))
    kept = [kept, swap(kept, "c")]
    in_weight = jnp.concatenate(
        [
            jnp.concatenate([own, swap(own, "c") if k else kept[1]], axis=1)
            for k, own in enumerate([kept[0]] + came)
        ],
        axis=0,
    )
    hidden = by_pair(*residue).astype(f32) + jnp.sum(parts.astype(f32), axis=0)

    rows = spread(hidden.astype(bf16), PAIR, 2 * N_ZY).reshape((2, N_ZY) + hidden.shape)
    near = swap(at_other(hidden), "xl")
    near, in_weight = lax.optimization_barrier((near, in_weight))
    hidden = by_pair(at_pair(hidden), near).reshape(2, 2, count // 2, features)
    mine = lax.dynamic_index_in_dim(hidden, core, 1, False)
    near = swap(lax.dynamic_index_in_dim(hidden, 1 - core, 1, False), "c")
    first = core == 0
    hidden = jnp.stack([jnp.where(first, mine, near), jnp.where(first, near, mine)])
    sums = exchange(widen(ids, rows, in_weight).reshape(N_DP, chunk, -1), DP)
    sums = jnp.sum(sums.reshape(2, 2, 2, chunk, -1).astype(f32), axis=(0, 2))
    squares = sums[0, :, 2 * units] + sums[0, :, 2 * units + 1]
    inverse = lax.rsqrt(squares / D + norm_eps)[:, None]
    active = sums[:, :, : 2 * units] * inverse
    active = (jax.nn.silu(active[0]) * active[1]).astype(bf16)
    parts = project(spread(active, DP, N_DP), downs).reshape(N_TP, count, features)
    parts = exchange(parts, TP).reshape((N_ZY,) + hidden.shape)
    result = (hidden + jnp.sum(parts.astype(f32), axis=0)).astype(bf16)
    result = result.reshape(2, 2, rows_out // 8, 2, steps, features)
    return result.transpose(4, 1, 2, 0, 3, 5).reshape(steps, rows_out, features)


def solution(mesh):
    split = Mesh(
        mesh.devices.reshape(2, 2, 2, 2, 4, 2), ("xh", "xl", "zl", "zh", "y", "c")
    )
    in_specs = (
        P(DP + TP, None, None),
        P(DP + TP),
        P(DP, None),
        P(DP, None),
        P(None, DP + TP, None, None),
        P(None, DP + TP, None),
        P(TP, None, None),
        P(TP, DP),
        P(None, None, DP),
        P(DP),
        P(DP, TP),
        P(DP, TP),
        P(TP, DP),
    )
    out_specs = P(None, TP, DP)
    return jax.shard_map(local, mesh=split, in_specs=in_specs, out_specs=out_specs, check_vma=False)
```

```python
import jax
import jax.numpy as jnp
from jax import lax
from jax.experimental import pallas as pl
from jax.experimental.pallas import tpu as pltpu
from jax.sharding import Mesh, PartitionSpec as P

D = 7168
QKD = 192
norm_eps = 1e-06

DP = ("xh", "xl", "zl")
TP = ("zh", "y", "c")
ZY = ("zh", "y")
PAIR = ("xl",) + ZY
N_DP = 8
N_TP = 16
N_ZY = 8
SWAP = [(0, 1), (1, 0)]
CUT = 384
TILE = 768
bf16 = jnp.bfloat16
f32 = jnp.float32
MIB = 1024 * 1024


def exchange(blocks, axes):
    return lax.all_to_all(blocks, axes, 0, 0, tiled=True)


def spread(block, axes, copies):
    return exchange(jnp.broadcast_to(block[None], (copies,) + block.shape), axes)


def swap(block, axis):
    return lax.ppermute(block, axis, SWAP)


def params(mib):
    return pltpu.CompilerParams(vmem_limit_bytes=mib * MIB)


def whole(shape):
    return pl.BlockSpec(shape, lambda *_: (0,) * len(shape))


def leave(slots, cache_t):
    _, entries, length = cache_t.shape
    tall, wide = 2 * entries // N_TP, length // 2

    def body(slots_ref, cache_ref, out_ref, row_ref, sem):
        slot = slots_ref[lax.axis_index(TP)]
        copy = pltpu.make_async_copy(cache_ref.at[slot], row_ref, sem)
        copy.start()
        copy.wait()
        row = row_ref[...].astype(f32)
        for j in range(N_TP):
            top, left = j // 2 * tall, j % 2 * wide
            out_ref[j] = row[top : top + tall, left : left + wide].astype(bf16)

    return pl.pallas_call(
        body,
        grid_spec=pltpu.PrefetchScalarGridSpec(
            num_scalar_prefetch=1,
            grid=(1,),
            in_specs=[pl.BlockSpec(memory_space=pl.ANY)],
            out_specs=whole((N_TP, tall, wide)),
            scratch_shapes=[pltpu.VMEM((entries, length), bf16), pltpu.SemaphoreType.DMA],
        ),
        out_shape=jax.ShapeDtypeStruct((N_TP, tall, wide), bf16),
        compiler_params=params(60),
        name="leave",
    )(slots, cache_t)


def route(peer, pieces):
    def body(peer_ref, in_ref, out_ref):
        for i in range(N_TP):
            out_ref[peer_ref[i]] = in_ref[i]

    return pl.pallas_call(
        body,
        grid_spec=pltpu.PrefetchScalarGridSpec(
            num_scalar_prefetch=1,
            grid=(1,),
            in_specs=[whole(pieces.shape)],
            out_specs=whole(pieces.shape),
        ),
        out_shape=jax.ShapeDtypeStruct(pieces.shape, bf16),
        compiler_params=params(40),
        name="route",
    )(peer, pieces)


def attend(ids, lengths, cache_t, fresh_t, queries_t, heads, latent_width, arrived=None, done=None):
    rows, entries, length = cache_t.shape
    steps, _, _, all_heads = queries_t.shape
    chips = all_heads // (2 * heads)
    again = arrived is not None

    def slot(r, ids):
        return ids[0] if again else r

    def body(ids_ref, lengths_ref, fresh_ref, q_ref, *refs):
        out_ref = refs[-1]
        row = slot(pl.program_id(0), ids_ref)
        current = lengths_ref[row]
        if again:
            latents = [
                jnp.concatenate([refs[0][j + b].astype(f32) for b in range(2)], axis=1)
                for j in range(0, N_TP, 2)
            ]
            latents = jnp.concatenate(latents, axis=0)
        else:
            latents = refs[0][0].astype(f32)
        position = lax.broadcasted_iota(jnp.int32, (entries, length), 1)
        for s in range(steps):
            token = fresh_ref[0, :, s : s + 1].astype(f32)
            latents = jnp.where(position == current + s, token, latents)
        latents = latents.astype(bf16)
        place = lax.broadcasted_iota(jnp.int32, (all_heads, length), 1)
        outs = []
        for s in range(steps):
            scores = lax.dot_general(
                q_ref[s, 0], latents, (((0,), (0,)), ((), ())), preferred_element_type=f32
            )
            scores = jnp.where(place <= current + s, scores * QKD ** (-0.5), -jnp.inf)
            expo = jnp.exp(scores - jnp.max(scores, axis=-1, keepdims=True))
            probs = (expo / jnp.sum(expo, axis=-1, keepdims=True)).astype(bf16)
            out = lax.dot_general(
                probs, latents[:latent_width], (((1,), (1,)), ((), ())), preferred_element_type=f32
            )
            out = out.reshape(chips, 2, heads, latent_width)
            turned = jnp.concatenate([out[:, 1:], out[:, :1]], axis=1)
            out = jnp.where(row >= rows // 2, turned, out)
            outs.append(out.reshape(chips, 2 * heads, latent_width))
        out_ref[:, 0, 0] = jnp.concatenate(outs, axis=1).astype(bf16)

    if again:
        extra_specs = [whole(arrived.shape), pl.BlockSpec(memory_space=pl.ANY)]
        extra = [arrived, done]
    else:
        extra_specs = [pl.BlockSpec((1, entries, length), lambda r, *_: (r, 0, 0))]
        extra = [cache_t]
    return pl.pallas_call(
        body,
        grid_spec=pltpu.PrefetchScalarGridSpec(
            num_scalar_prefetch=2,
            grid=(1 if again else rows,),
            in_specs=[
                pl.BlockSpec((1, entries, steps), lambda r, ids, _: (slot(r, ids), 0, 0)),
                pl.BlockSpec(
                    (steps, 1, entries, all_heads), lambda r, ids, _: (0, slot(r, ids), 0, 0)
                ),
            ]
            + extra_specs,
            out_specs=pl.BlockSpec(
                (chips, 1, 1, 2 * steps * heads, latent_width),
                lambda r, ids, _: (
                    0,
                    lax.div(slot(r, ids), rows // 2),
                    lax.rem(slot(r, ids), rows // 2),
                    0,
                    0,
                ),
            ),
        ),
        out_shape=jax.ShapeDtypeStruct(
            (chips, 2, rows // 2, 2 * steps * heads, latent_width), bf16
        ),
        input_output_aliases={5: 0} if again else {},
        compiler_params=params(60),
        name="again" if again else "attend",
    )(ids, lengths, fresh_t, queries_t, *extra)


def project(ids, rows, weight, blocks):
    groups, count, depth = rows.shape
    width = weight.shape[1] // blocks

    def body(ids_ref, rows_ref, weight_ref, out_ref):
        lhs = rows_ref[...].reshape(groups * count, depth)
        total = jnp.dot(lhs, weight_ref[...], preferred_element_type=f32)
        out_ref[:, 0] = total.astype(bf16).reshape(groups, count, width)

    return pl.pallas_call(
        body,
        grid_spec=pltpu.PrefetchScalarGridSpec(
            num_scalar_prefetch=1,
            grid=(blocks,),
            in_specs=[
                whole(rows.shape),
                pl.BlockSpec((depth, width), lambda k, ids: (0, k)),
            ],
            out_specs=pl.BlockSpec(
                (groups, 1, count, width), lambda k, ids: (0, lax.rem(ids[1] + k, blocks), 0, 0)
            ),
        ),
        out_shape=jax.ShapeDtypeStruct((groups, blocks, count, width), bf16),
        compiler_params=params(40),
        name="project",
    )(ids, rows, weight)


def fetches(refs, blocks, weight_ref, sems):
    copies, n, left = [], 0, 0
    for column in blocks:
        top = 0
        for w in column:
            at = weight_ref.at[pl.ds(top, w.shape[0]), pl.ds(left, w.shape[1])]
            copies.append(pltpu.make_async_copy(refs[n], at, sems.at[n]))
            n, top = n + 1, top + w.shape[0]
        left += column[0].shape[1]
    return copies


def combine(ids, rows, blocks):
    groups, count, depth = rows.shape
    width = blocks[0][0].shape[1]
    flat = [w for column in blocks for w in column]
    half = len(flat) // 2

    def body(ids_ref, rows_ref, *refs):
        out_ref, weight_ref, sems = refs[len(flat) :]
        copies = fetches(refs, blocks, weight_ref, sems)
        for copy in copies:
            copy.start()
        lhs = rows_ref[...].reshape(groups * count, depth)
        for k in range(2):
            for copy in copies[k * half : (k + 1) * half]:
                copy.wait()
            total = jnp.dot(
                lhs, weight_ref[:, k * width : (k + 1) * width], preferred_element_type=f32
            )
            at = lax.rem(ids_ref[1] + k, 2)
            out_ref[:, at] = total.astype(bf16).reshape(groups, count, width)

    return pl.pallas_call(
        body,
        grid_spec=pltpu.PrefetchScalarGridSpec(
            num_scalar_prefetch=1,
            grid=(1,),
            in_specs=[whole(rows.shape)] + [pl.BlockSpec(memory_space=pl.ANY) for _ in flat],
            out_specs=whole((groups, 2, count, width)),
            scratch_shapes=[
                pltpu.VMEM((depth, 2 * width), bf16),
                pltpu.SemaphoreType.DMA((len(flat),)),
            ],
        ),
        out_shape=jax.ShapeDtypeStruct((groups, 2, count, width), bf16),
        compiler_params=params(60),
        name="combine",
    )(ids, rows, *flat)


def widen(ids, rows, weight):
    halves, chunks, blocks, count, features = rows.shape
    depth, columns = weight.shape
    every = halves * chunks * count

    def body(ids_ref, rows_ref, weight_ref, out_ref, lhs_ref):
        tile = pl.program_id(0)

        def put(at, value):
            value = value.astype(bf16).reshape(halves, chunks, count, value.shape[1])
            for h in range(halves):
                out_ref[:, h, :, at] = value[h]

        @pl.when(tile == 0)
        def _():
            squares = jnp.zeros((every, 1), f32)
            for k in range(blocks):
                block = rows_ref[:, :, lax.rem(ids_ref[1] + k, blocks)].reshape(every, features)
                lhs_ref[:, k * features : (k + 1) * features] = block
                wide = block.astype(f32)
                squares += jnp.sum(wide * wide, axis=1, keepdims=True)
            high = squares.astype(bf16).astype(f32)
            lane = lax.broadcasted_iota(jnp.int32, (every, 128), 1)
            extra = jnp.where(lane == 0, high, jnp.where(lane == 1, squares - high, 0.0))
            put(slice(columns, columns + 128), extra)

        total = jnp.dot(lhs_ref[...], weight_ref[...], preferred_element_type=f32)
        put(pl.ds(pl.multiple_of(tile * TILE, 128), TILE), total)

    return pl.pallas_call(
        body,
        grid_spec=pltpu.PrefetchScalarGridSpec(
            num_scalar_prefetch=1,
            grid=(columns // TILE,),
            in_specs=[
                whole(rows.shape),
                pl.BlockSpec((depth, TILE), lambda k, ids: (0, k)),
            ],
            out_specs=whole((chunks, halves, count, columns + 128)),
            scratch_shapes=[pltpu.VMEM((every, depth), bf16)],
        ),
        out_shape=jax.ShapeDtypeStruct((chunks, halves, count, columns + 128), bf16),
        compiler_params=params(40),
        name="widen",
    )(ids, rows, weight)


def local(
    cache,
    cache_length,
    move_slot,
    move_peer,
    queries,
    new_latent,
    value_up,
    out_proj,
    residual,
    norm_gain,
    gate_weight,
    up_weight,
    down_weight,
):
    member = lax.axis_index(TP)
    core = lax.axis_index("c")
    pair = lax.axis_index("xl")
    steps = new_latent.shape[0]
    heads, latent_width, value_width = value_up.shape
    rows_out = residual.shape[1] // N_TP
    chunk = rows_out * steps
    count = chunk // 2
    features, units = gate_weight.shape

    def by_pair(mine, other):
        first = pair == 0
        return jnp.stack([jnp.where(first, mine, other), jnp.where(first, other, mine)])

    def at_pair(blocks):
        return lax.dynamic_index_in_dim(blocks, pair, 0, False)

    def at_other(blocks):
        return lax.dynamic_index_in_dim(blocks, 1 - pair, 0, False)

    out_came = swap(out_proj, "xl")
    value_near = swap(value_up, "c")
    lanes = jnp.arange(N_TP, dtype=jnp.int32)
    cache_t = cache.transpose(0, 2, 1)
    pieces = exchange(leave(move_slot[0], cache_t), TP)
    fresh_t = new_latent.transpose(1, 2, 0)
    queries_t = queries.transpose(0, 1, 3, 2)
    out = attend(cache_length, cache_length, cache_t, fresh_t, queries_t, heads, latent_width)
    pieces, out, gate_weight, up_weight, slots = lax.optimization_barrier(
        (pieces, out, gate_weight, up_weight, move_slot[0])
    )
    own_slot = jnp.sum(jnp.where(lanes == member, slots, 0))
    ids = jnp.stack([own_slot, pair]).astype(jnp.int32)

    gain = norm_gain.astype(f32)[:, None]

    def scaled(low, high, first, second):
        weight = jnp.where(pair == 0, first[low:high], second[low:high])
        return (weight.astype(f32) * gain[low:high]).astype(bf16)

    kept = scaled(0, features, gate_weight, up_weight)
    sent = scaled(0, CUT, up_weight, gate_weight)
    arrived = exchange(route(move_peer[0], pieces), TP)
    arrived, kept, sent, ids, value_near = lax.optimization_barrier(
        (arrived, kept, sent, ids, value_near)
    )
    out = attend(
        ids, cache_length, cache_t, fresh_t, queries_t, heads, latent_width, arrived, out
    )
    out, out_came, out_proj, down_weight = lax.optimization_barrier(
        (out, out_came, out_proj, down_weight)
    )
    came = [swap(sent, "xl")]
    out_near = swap(out_proj, "c")
    out_weights = [[out_proj, out_near], [out_came, swap(out_came, "c")]]
    out = out.reshape((N_TP,) + out.shape[2:])
    by_head = exchange(out, TP).reshape(-1, 2 * heads, latent_width)

    downs = jnp.concatenate([down_weight, swap(down_weight, "c")], axis=0)
    out_weights[0][1], gate_weight, up_weight, residual, value_near = lax.optimization_barrier(
        (out_near, gate_weight, up_weight, residual, value_near)
    )
    value_ups = jnp.concatenate([value_up, value_near], axis=0)
    sent = scaled(CUT, features, up_weight, gate_weight)
    residue = lax.dynamic_slice_in_dim(residual, lax.div(member, 2) * 2 * rows_out, 2 * rows_out, 1)
    residue = residue.reshape(steps, 2, 2, rows_out // 8, 2, 2, features)
    residue = lax.dynamic_index_in_dim(residue, core, 4, False)
    residue = residue.transpose(2, 1, 3, 4, 0, 5).reshape(2, count, features)
    residue = [at_pair(residue), at_other(residue)]
    by_head, kept, came, sent, downs, residue, out_weights, value_ups = lax.optimization_barrier(
        (by_head, kept, came, sent, downs, residue, out_weights, value_ups)
    )
    residue[1] = swap(residue[1], "xl")
    value_heads = jnp.einsum(
        "thl,hlv->thv", by_head, value_ups, preferred_element_type=f32
    ).astype(bf16)

    value_heads = value_heads.reshape(2, 2, count // 2, 2 * heads * value_width)
    value_heads = value_heads.transpose(1, 0, 2, 3).reshape(2, count, -1)
    value_heads = jnp.broadcast_to(
        value_heads[None, :, None], (2, 2, 2) + value_heads.shape[1:]
    ).reshape((N_DP,) + value_heads.shape[1:])
    gathered = exchange(value_heads, DP)
    gathered, sent, kept, residue = lax.optimization_barrier((gathered, sent, kept, residue))
    came.append(swap(sent, "xl"))
    parts = exchange(combine(ids, gathered, out_weights), ZY)
    parts, came, kept, residue = lax.optimization_barrier((parts, came, kept, residue))
    kept = [kept, swap(kept, "c")]
    in_weight = jnp.concatenate(
        [
            jnp.concatenate([own, swap(own, "c") if k else kept[1]], axis=1)
            for k, own in enumerate([kept[0]] + came)
        ],
        axis=0,
    )
    hidden = by_pair(*residue).astype(f32) + jnp.sum(parts.astype(f32), axis=0)

    rows = spread(hidden.astype(bf16), PAIR, 2 * N_ZY).reshape((2, N_ZY) + hidden.shape)
    near = swap(at_other(hidden), "xl")
    near, in_weight = lax.optimization_barrier((near, in_weight))
    rows, near = lax.optimization_barrier((rows, near))
    sums = exchange(widen(ids, rows, in_weight).reshape(N_DP, chunk, -1), DP)
    sums = jnp.sum(sums.reshape(2, 2, 2, chunk, -1).astype(f32), axis=(0, 2))
    squares = sums[0, :, 2 * units] + sums[0, :, 2 * units + 1]
    inverse = lax.rsqrt(squares / D + norm_eps)[:, None]
    active = sums[:, :, : 2 * units] * inverse
    active = (jax.nn.silu(active[0]) * active[1]).astype(bf16)
    parts = exchange(project(ids, spread(active, DP, N_DP), downs, 1)[:, 0], ZY)
    hidden = by_pair(at_pair(hidden), near).reshape(chunk, -1)
    result = (hidden + jnp.sum(parts.astype(f32), axis=0)).astype(bf16)

    result = result.reshape(2, 2, rows_out // 8, 2, steps, features)
    mine = lax.dynamic_index_in_dim(result, core, 1, False)
    near = swap(lax.dynamic_index_in_dim(result, 1 - core, 1, False), "c")
    first = core == 0
    result = jnp.stack([jnp.where(first, mine, near), jnp.where(first, near, mine)])
    return result.transpose(4, 1, 2, 0, 3, 5).reshape(steps, rows_out, features)


def solution(mesh):
    split = Mesh(
        mesh.devices.reshape(2, 2, 2, 2, 4, 2), ("xh", "xl", "zl", "zh", "y", "c")
    )
    in_specs = (
        P(DP + TP, None, None),
        P(DP + TP),
        P(DP, None),
        P(DP, None),
        P(None, DP + TP, None, None),
        P(None, DP + TP, None),
        P(TP, None, None),
        P(TP, DP),
        P(None, None, DP),
        P(DP),
        P(DP, TP),
        P(DP, TP),
        P(TP, DP),
    )
    out_specs = P(None, TP, DP)
    return jax.shard_map(local, mesh=split, in_specs=in_specs, out_specs=out_specs, check_vma=False)
```
